512 devices in a mesh: dp: 64 (over x, z), fsdp: 8 (over y, core).
Axes of the slice: x: 4, y: 4, z: 16, core: 2. Of those that a mesh axis runs over, the one named last changes fastest.
Arguments:
- actions: bfloat16 [8, 8192, 1024], P('fsdp', 'dp'), may hold values from -6 to 6
- lengths: int32 [8, 64, 7], P('fsdp', 'dp'), may hold values from 1 to 74, as said below
- partner_mask: int32 [8, 64], P('fsdp', 'dp'), may hold values from 1 to 7, as said below
- norm_gain: float32 [1024], replicated, may hold values from 0.1 to 1.9
- w_in: bfloat16 [1024, 4096], P('fsdp'), may hold values from -0.1875 to 0.1875
- w_out: bfloat16 [1024, 1024], P('fsdp'), may hold values from -0.1875 to 0.1875
- cotangent: bfloat16 [8, 8192, 1024], P('fsdp', 'dp'), may hold values from -16 to 16
Outputs:
- output: bfloat16 [8, 8192, 1024], P('fsdp', 'dp')
- grad_input: bfloat16 [8, 8192, 1024], P('fsdp', 'dp')
- grad_weights: float32 [1024, 1024], P('dp')
The draws below stay inside these ranges and needn't reach their ends.
Inputs may be any that keep to these rules, and one draw needn't show every extreme that they name: The 7 lengths of each block sum to 80. partner_mask is equal over aligned groups of 8 indices of dp within a stream, so block b and block b XOR partner_mask[., b] name each other.
All inputs are finite; a program needn't handle non-finite values.
Results may differ from the reference program's by a relative error of at most 0.015.
Values may be sent and summed in bfloat16 or wider, within the bound.
A program may use at most 128 MiB of HBM per device.

```python
import jax
import jax.numpy as jnp
from jax import lax

D = 1024
HEADS = 8
HEAD_DIM = 128
TOK_DEV = 128
USERS = 7
SPILL = 16
MOST = 32
ATT_WIDTH = 1024
STREAM = 8192
ROWS_ALL = 65536
N_DP = 64
N_FSDP = 8


def draw_lengths(key, part):
    key = jax.random.fold_in(key, 11)
    count = N_FSDP * N_DP
    total = TOK_DEV - SPILL - MOST
    scores = jax.random.randint(key, (count, total - 1), 0, 1 << 20) * (total - 1) + jnp.arange(total - 1, dtype=jnp.int32)[None, :]
    chosen = lax.top_k(scores, USERS - 1)[1].astype(jnp.int32) + 1
    cuts = jnp.sort(chosen, axis=1)
    edges = jnp.concatenate([jnp.zeros((count, 1), jnp.int32), cuts, jnp.full((count, 1), total, jnp.int32)], axis=1)
    pieces = edges[:, 1:] - edges[:, :-1]
    extreme = jnp.concatenate([jnp.ones((USERS - 1,), jnp.int32), jnp.array([total - USERS + 1], jnp.int32)])
    chosen_row = jax.random.randint(jax.random.fold_in(key, 1), (), 0, count)
    pieces = jnp.where(jnp.arange(count, dtype=jnp.int32)[:, None] == chosen_row, extreme[None, :], pieces)
    return pieces.reshape(N_FSDP, N_DP, USERS).astype(jnp.int32)


def draw_partner_mask(key, part):
    key = jax.random.fold_in(key, 23)
    groups = N_FSDP * N_DP // 8
    picks = jax.random.randint(key, (groups,), 1, 8)
    spots = jax.random.permutation(jax.random.fold_in(key, 1), groups)
    picks = picks.at[spots[0]].set(7).at[spots[1]].set(1)
    return jnp.repeat(picks, 8).reshape(N_FSDP, N_DP).astype(jnp.int32)


def strengthened(values, key, source, target, blocks, factor):
    owner, partner = [(jnp.arange(values.shape[dim]) // (values.shape[dim] // blocks)).reshape([-1 if axis == dim else 1 for axis in range(values.ndim)]) for dim in (source, target)]
    chosen = jax.random.permutation(key, blocks)[partner]
    strong = (owner == chosen) | (owner == (partner + blocks // 2) % blocks)
    return jnp.where(strong, factor * values, values)


def block_scale(own_key, dims, split, low, largest):
    def one(axis_at, blocks):
        heights = jax.random.uniform(jax.random.fold_in(jax.random.fold_in(own_key, 6), axis_at), (blocks,), jnp.float32, low / len(split), largest / len(split))
        return jnp.repeat(jnp.exp(heights), dims[axis_at] // blocks).reshape((-1,) + (1,) * (len(dims) - axis_at - 1))

    factor_of = one(*split[0])
    for cut in split[1:]:
        factor_of = factor_of * one(*cut)
    return factor_of


def bell_draw(key, dims, spread, limit, shards=(), kind=jnp.bfloat16):
    entries = jax.random.normal(key, dims, jnp.float32) * spread
    if len(shards) > 0:
        entries = block_scale(key, dims, shards, -0.22, 0.18) * entries
    return jnp.clip(entries, min=-limit, max=limit).astype(kind)


def bell_draw_with(stream_key, extent, scale, reach, cuts, heavy, kind=jnp.bfloat16):
    drawn = scale * jax.random.normal(stream_key, extent, jnp.float32)
    if cuts:
        drawn = drawn * block_scale(stream_key, extent, cuts, -0.22, 0.18)
    return jnp.clip(strengthened(drawn, jax.random.fold_in(stream_key, 3), *heavy), -reach, reach).astype(kind)


def setup_inputs(seed: int = 0) -> dict:
    key_of = jax.random.split(jax.random.key(seed), 8)
    actions = bell_draw(key_of[0], (N_FSDP, STREAM, D), 1.0, 6.0, ((0, 8), (1, 64)))
    lengths = draw_lengths(jax.random.fold_in(key_of[7], 71), 0)
    partner_mask = draw_partner_mask(jax.random.fold_in(key_of[7], 71), 0)
    norm_gain = jnp.clip(1.0 + 0.18 * jax.random.normal(key_of[3], (D,), jnp.float32), 0.1, 1.9)
    w_in = bell_draw(key_of[4], (D, 4 * ATT_WIDTH), D ** -0.5, 0.1875, ((0, 8),))
    w_out = bell_draw(key_of[5], (ATT_WIDTH, D), ATT_WIDTH ** -0.5, 0.1875, ((0, 8),))
    cotangent = bell_draw_with(key_of[6], (N_FSDP, STREAM, D), 1.0, 16.0, ((0, 8), (1, 64)), (1, 2, 64, 4.0))
    return dict(actions=actions, lengths=lengths, partner_mask=partner_mask, norm_gain=norm_gain, w_in=w_in, w_out=w_out, cotangent=cotangent)


EPSILON = 1e-05

def silu_slope(values):
    sigma = jax.nn.sigmoid(values)
    return sigma * (1.0 + values * (1.0 - sigma))

def normalize(values):
    centred = values - lax.optimization_barrier(jnp.mean(values, axis=-1, keepdims=True))
    inverse = lax.rsqrt(lax.optimization_barrier(jnp.mean(centred * centred, axis=-1, keepdims=True)) + EPSILON)
    return (centred * inverse, inverse)

def norm_backward(grad, normed, inverse):
    return inverse * (grad - lax.optimization_barrier(jnp.mean(grad, axis=-1, keepdims=True)) - normed * lax.optimization_barrier(jnp.mean(grad * normed, axis=-1, keepdims=True)))

def user_starts(user_lengths, positions):
    ends = jnp.cumsum(user_lengths, dtype=jnp.int32)
    before = jnp.where(ends[None, :] <= positions[:, None], user_lengths[None, :], jnp.zeros((), jnp.int32))
    return lax.optimization_barrier(jnp.sum(before, axis=1, dtype=jnp.int32))

def project(row_actions, norm_gain, w_in):
    inputs = row_actions.astype(jnp.float32)
    normed_in, inverse_in = normalize(inputs)
    normed = (normed_in * norm_gain).astype(jnp.bfloat16)
    hidden = jnp.dot(normed, w_in, preferred_element_type=jnp.float32)
    active = jax.nn.silu(hidden).astype(jnp.bfloat16)
    return (inputs, normed_in, inverse_in, normed, hidden, active)

def heads_of(active, index):
    width = HEADS * HEAD_DIM
    return active[:, index * width:(index + 1) * width].reshape(-1, HEADS, HEAD_DIM).astype(jnp.float32)

def attend(query_heads, key_heads, value_heads, visible):
    scores = jnp.einsum('qhd,khd->hqk', query_heads, key_heads) * HEAD_DIM ** (-0.5)
    weights = (jnp.where(visible[None], jax.nn.silu(scores), 0.0) / MOST).astype(jnp.bfloat16)
    attended = jnp.einsum('hqk,khd->qhd', weights.astype(jnp.float32), value_heads)
    return (scores, weights, attended)

def attend_back(query_heads, key_heads, value_heads, visible, scores, weights, grad_heads):
    grad_w = jnp.einsum('qhd,khd->hqk', grad_heads, value_heads)
    grad_scores = (jnp.where(visible[None], grad_w * silu_slope(scores), 0.0) * (HEAD_DIM ** (-0.5) / MOST)).astype(jnp.bfloat16).astype(jnp.float32)
    grad_queries = jnp.einsum('hqk,khd->qhd', grad_scores, key_heads)
    grad_keys = jnp.einsum('hqk,qhd->khd', grad_scores, query_heads)
    grad_values = jnp.einsum('hqk,qhd->khd', weights.astype(jnp.float32), grad_heads)
    return (grad_queries, grad_keys, grad_values)

def gate_forward(attended, gates):
    normed_out, inverse_out = normalize(attended)
    mixed = (normed_out * gates.astype(jnp.float32)).astype(jnp.bfloat16)
    return (normed_out, inverse_out, mixed)

def gate_backward(cotangent, w_out, gates, normed_out, inverse_out):
    grad_mixed = lax.dot_general(cotangent, w_out, (((1,), (1,)), ((), ())), preferred_element_type=jnp.float32)
    grad_gates = grad_mixed * normed_out
    grad_attended = norm_backward(grad_mixed * gates.astype(jnp.float32), normed_out, inverse_out).astype(jnp.bfloat16)
    return (grad_gates, grad_attended)

def one_block(actions, user_lengths, cotangent, partner_actions, partner_cotangent, norm_gain, w_in, w_out):
    width = HEADS * HEAD_DIM
    rows = TOK_DEV
    first = rows - SPILL - MOST
    inputs, normed_in, inverse_in, normed, hidden, active = project(actions, norm_gain, w_in)
    gates = active[:, :width]
    value_heads = heads_of(active, 1)
    query_heads = heads_of(active, 2)
    key_heads = heads_of(active, 3)
    partner_active = project(partner_actions[first:], norm_gain, w_in)[5]
    partner_values = heads_of(partner_active, 1)
    partner_queries = heads_of(partner_active, 2)
    partner_keys = heads_of(partner_active, 3)
    partner_gates = partner_active[MOST:, :width]
    positions = jnp.arange(rows, dtype=jnp.int32)
    all_lengths = jnp.concatenate([user_lengths, jnp.array([MOST, SPILL], dtype=jnp.int32)])
    starts = user_starts(all_lengths, positions)
    local_mask = (positions[None, :] >= starts[:, None]) & (positions[None, :] <= positions[:, None])
    far_mask = jnp.broadcast_to((positions >= rows - SPILL)[:, None], (rows, MOST))
    visible = jnp.concatenate([local_mask, far_mask], axis=1)
    key_all = jnp.concatenate([key_heads, partner_keys[:MOST]], axis=0)
    value_all = jnp.concatenate([value_heads, partner_values[:MOST]], axis=0)
    scores, weights, attended = attend(query_heads, key_all, value_all, visible)
    normed_out, inverse_out, mixed = gate_forward(attended.reshape(rows, width), gates)
    output = (jnp.dot(mixed, w_out, preferred_element_type=jnp.float32) + inputs).astype(jnp.bfloat16)
    grad_gates, grad_attended = gate_backward(cotangent, w_out, gates, normed_out, inverse_out)
    grad_heads = grad_attended.reshape(rows, HEADS, HEAD_DIM).astype(jnp.float32)
    grad_queries, grad_keys, grad_values = attend_back(query_heads, key_all, value_all, visible, scores, weights, grad_heads)
    spare_positions = jnp.arange(SPILL, dtype=jnp.int32)
    spare_mask = jnp.concatenate([spare_positions[None, :] <= spare_positions[:, None], jnp.ones((SPILL, MOST), dtype=bool)], axis=1)
    spare_keys = jnp.concatenate([partner_keys[MOST:], key_heads[first:first + MOST]], axis=0)
    spare_values = jnp.concatenate([partner_values[MOST:], value_heads[first:first + MOST]], axis=0)
    spare_queries = partner_queries[MOST:]
    spare_scores, spare_weights, spare_attended = attend(spare_queries, spare_keys, spare_values, spare_mask)
    spare_normed, spare_inverse, spare_mixed = gate_forward(spare_attended.reshape(SPILL, width), partner_gates)
    spare_gate_grads, spare_grad = gate_backward(partner_cotangent[rows - SPILL:], w_out, partner_gates, spare_normed, spare_inverse)
    spare_heads = spare_grad.reshape(SPILL, HEADS, HEAD_DIM).astype(jnp.float32)
    spare_query_grads, spare_key_grads, spare_value_grads = attend_back(spare_queries, spare_keys, spare_values, spare_mask, spare_scores, spare_weights, spare_heads)
    grad_keys = grad_keys[:rows].at[first:first + MOST].add(spare_key_grads[SPILL:])
    grad_values = grad_values[:rows].at[first:first + MOST].add(spare_value_grads[SPILL:])
    grad_active = jnp.concatenate([grad_gates, grad_values.reshape(rows, width), grad_queries.reshape(rows, width), grad_keys.reshape(rows, width)], axis=1)
    grad_hidden = (grad_active * silu_slope(hidden)).astype(jnp.bfloat16)
    grad_normed = lax.dot_general(grad_hidden, w_in, (((1,), (1,)), ((), ())), preferred_element_type=jnp.float32)
    grad_input = cotangent.astype(jnp.float32) + norm_backward(grad_normed * norm_gain, normed_in, inverse_in)
    term = lax.dot_general(cotangent, mixed, (((0,), (0,)), ((), ())), preferred_element_type=jnp.float32)
    return (output, grad_input.astype(jnp.bfloat16), term)

def reference(actions, lengths, partner_mask, norm_gain, w_in, w_out, cotangent):
    width = HEADS * HEAD_DIM
    count = N_FSDP * N_DP
    action_blocks = actions.reshape(count, TOK_DEV, D)
    cotangent_blocks = cotangent.reshape(count, TOK_DEV, D)
    length_blocks = lengths.reshape(count, USERS)
    stream_base = jnp.arange(N_FSDP, dtype=jnp.int32)[:, None] * N_DP
    partners = (stream_base + jnp.bitwise_xor(jnp.arange(N_DP, dtype=jnp.int32)[None, :], partner_mask)).reshape(count).astype(jnp.int32)

    def step(total, items):
        block_actions, block_lengths, block_cotangent, partner = items
        partner_actions = lax.dynamic_index_in_dim(action_blocks, partner, 0, keepdims=False)
        partner_cotangent = lax.dynamic_index_in_dim(cotangent_blocks, partner, 0, keepdims=False)
        output, grad_input, term = one_block(block_actions, block_lengths, block_cotangent, partner_actions, partner_cotangent, norm_gain, w_in, w_out)
        return (total + term, (output, grad_input))
    start_total = jnp.zeros((D, width), jnp.float32)
    total, outs = lax.scan(step, start_total, (action_blocks, length_blocks, cotangent_blocks, partners))
    output = outs[0].reshape(actions.shape)
    grad_input = outs[1].reshape(actions.shape)
    grad_weights = total * ROWS_ALL ** (-0.5)
    return (output, grad_input, grad_weights)
```

```python
import jax
import jax.numpy as jnp
from jax import lax
from jax.experimental import pallas as pl
from jax.experimental.pallas import tpu as pltpu
from jax.sharding import PartitionSpec as P

HEADS = 8
HEAD_DIM = 128
SPILL = 16
MOST = 32
ROWS = 128
WIDTH = 1024
KEPT = SPILL + MOST
FIRST = ROWS - KEPT
LAST = ROWS - SPILL
QROWS = ROWS + SPILL
KROWS = ROWS + KEPT
NX, NY, NZ = 4, 4, 16
EPSILON = 1e-05
MESH = pl.DeviceIdType.MESH
F32 = jnp.float32
BF16 = jnp.bfloat16


def place():
    dp = lax.axis_index("dp")
    fsdp = lax.axis_index("fsdp")
    return dp // NZ, fsdp // 2, dp % NZ, fsdp % 2


def device(x, y, z, c):
    return (x * NZ + z, y * 2 + c)


def remote(src, dst, send, recv, target):
    return pltpu.make_async_remote_copy(
        src_ref=src, dst_ref=dst, send_sem=send, recv_sem=recv, device_id=target, device_id_type=MESH
    )


def greet(targets):
    barrier = pltpu.get_barrier_semaphore()
    for target in targets:
        pl.semaphore_signal(barrier, inc=1, device_id=target, device_id_type=MESH)
    pl.semaphore_wait(barrier, len(targets))


class Ring:
    def __init__(self, own, view, half, me, towards, other, send, recv):
        ahead, behind, across = (me + 1) % 4, (me + 3) % 4, (me + 2) % 4
        self.first = [
            remote(own, view(me), send.at[0], recv.at[0], towards(ahead)),
            remote(own, view(me), send.at[1], recv.at[1], towards(behind)),
            remote(own, view(me), send.at[4], recv.at[4], other),
        ]
        self.behind = [
            remote(half(behind, 0), half(behind, 0), send.at[2], recv.at[2], towards(ahead)),
            remote(view(behind), view(behind), send.at[5], recv.at[5], other),
        ]
        self.ahead = [
            remote(half(ahead, 1), half(ahead, 1), send.at[3], recv.at[3], towards(behind)),
            remote(view(ahead), view(ahead), send.at[6], recv.at[6], other),
        ]
        self.across = [
            remote(half(across, 0), half(across, 0), send.at[7], recv.at[7], other),
            remote(half(across, 1), half(across, 1), send.at[8], recv.at[8], other),
        ]

    def start(self):
        for copy in self.first:
            copy.start()

    def forward(self):
        self.first[0].wait_recv()
        for copy in self.behind:
            copy.start()
        self.first[1].wait_recv()
        for copy in self.ahead:
            copy.start()

    def finish(self):
        self.behind[0].wait_recv()
        self.across[0].start()
        self.ahead[0].wait_recv()
        self.across[1].start()

    def arrived(self):
        self.first[2].wait_recv()
        self.behind[1].wait_recv()
        self.ahead[1].wait_recv()
        self.across[0].wait_recv()
        self.across[1].wait_recv()

    def sent(self):
        for copy in self.first + self.behind + self.ahead + self.across:
            copy.wait_send()


def gather_kernel(
    mask_ref, actions_ref, cot_ref, w_in_ref, w_out_ref,
    wall_ref, cots_ref, far_ref,
    cot_t, mine, landed,
    wsend, wrecv, csend, crecv, zsend, zrecv, local,
):
    x, y, z, c = place()
    other = device(x, y, z, 1 - c)
    along_y = lambda i: device(x, i, z, c)
    along_x = lambda i: device(i, y, z, c)
    swaps = [device(x, y, z + (1 << k) - 2 * (1 << k) * (z // (1 << k) % 2), c) for k in range(3)]
    greet([along_y((y + 1) % 4), along_y((y + 3) % 4), along_x((x + 1) % 4), along_x((x + 3) % 4), other] + swaps)

    def view(section):
        return lambda i: wall_ref.at[section, pl.ds(pl.multiple_of((2 * i + c) * ROWS, ROWS), ROWS)]

    def half(section):
        return lambda i, h: wall_ref.at[section, pl.ds(pl.multiple_of((2 * i + c) * ROWS + h * 64, 64), 64)]

    rings = []
    own = []
    for t in range(5):
        src = w_in_ref.at[:, t * WIDTH : (t + 1) * WIDTH] if t < 4 else w_out_ref
        rings.append(Ring(src, view(t), half(t), y, along_y, other, wsend.at[t], wrecv.at[t]))
        own.append(pltpu.make_async_copy(src, view(t)(y), local.at[t]))

    cview = lambda i: cots_ref.at[:, pl.ds(pl.multiple_of((2 * i + c) * ROWS, ROWS), ROWS)]
    chalf = lambda i, h: cots_ref.at[h * 512 : h * 512 + 512, pl.ds(pl.multiple_of((2 * i + c) * ROWS, ROWS), ROWS)]
    cring = Ring(cot_t, cview, chalf, x, along_x, other, csend, crecv)
    cown = pltpu.make_async_copy(cot_t, cview(x), local.at[5])
    swap = [
        remote(mine.at[k], landed.at[k], zsend.at[k], zrecv.at[k], swaps[k]) for k in range(3)
    ]

    def turn(k):
        swap[k].wait_recv()
        bit = jnp.full((KEPT + SPILL, WIDTH), lax.shift_right_logical(mask_ref[0, 0], k) & 1, jnp.int32)
        chosen = jnp.where(bit == 1, landed[k].astype(F32), mine[k].astype(F32)).astype(BF16)
        if k < 2:
            mine[k + 1] = chosen
            swap[k + 1].start()
        else:
            far_ref[...] = chosen

    rings[0].start()
    rings[1].start()
    mine[0, :KEPT] = actions_ref[0, FIRST:]
    mine[0, KEPT:] = cot_ref[0, LAST:]
    swap[0].start()
    for copy in own:
        copy.start()
    cot_t[...] = cot_ref[0].astype(F32).T.astype(BF16)
    cring.start()
    cown.start()
    for t in range(5):
        rings[t].forward()
        if t + 2 < 5:
            rings[t + 2].start()
        if t >= 1:
            rings[t - 1].finish()
        if t < 3:
            turn(t)
        if t == 1:
            cring.forward()
        if t == 2:
            cring.finish()
    rings[4].finish()
    for copy in own + [cown]:
        copy.wait()
    for ring in rings + [cring]:
        ring.arrived()
    for ring in rings + [cring]:
        ring.sent()
    for copy in swap:
        copy.wait_send()


def gather(partner_mask, actions, cotangent, w_in, w_out):
    any_space = pl.BlockSpec(memory_space=pl.ANY)
    vmem = pl.BlockSpec(memory_space=pltpu.VMEM)
    return pl.pallas_call(
        gather_kernel,
        out_shape=(
            jax.ShapeDtypeStruct((5, WIDTH, WIDTH), BF16),
            jax.ShapeDtypeStruct((WIDTH, WIDTH), BF16),
            jax.ShapeDtypeStruct((KEPT + SPILL, WIDTH), BF16),
        ),
        in_specs=[pl.BlockSpec(memory_space=pltpu.SMEM), vmem, vmem, any_space, any_space],
        out_specs=(any_space, any_space, vmem),
        scratch_shapes=[
            pltpu.VMEM((WIDTH, ROWS), BF16),
            pltpu.VMEM((3, KEPT + SPILL, WIDTH), BF16),
            pltpu.VMEM((3, KEPT + SPILL, WIDTH), BF16),
            pltpu.SemaphoreType.DMA((5, 9)),
            pltpu.SemaphoreType.DMA((5, 9)),
            pltpu.SemaphoreType.DMA((9,)),
            pltpu.SemaphoreType.DMA((9,)),
            pltpu.SemaphoreType.DMA((3,)),
            pltpu.SemaphoreType.DMA((3,)),
            pltpu.SemaphoreType.DMA((6,)),
        ],
        compiler_params=pltpu.CompilerParams(
            collective_id=0, has_side_effects=True, vmem_limit_bytes=32 * 1024 * 1024
        ),
        name="gather_inputs",
    )(partner_mask, actions, cotangent, w_in, w_out)


def weight_kernel(
    mixed_ref, cots_ref, out_ref,
    all_mixed, total, sums, ybuf, part, zbuf, final, wide,
    msend, mrecv, ysend, yrecv, zsend, zrecv, asend, arecv,
):
    x, y, z, c = place()
    g = 2 * x + c
    group = [((g + d) % 8) for d in range(1, 8)]
    in_group = [device(i // 2, y, z, i % 2) for i in group]
    in_y = [device(x, (y + d) % 4, z, c) for d in range(1, 4)]
    in_z = [device(x, y, (z + d) % 16, c) for d in range(1, 16)]
    ends = [device(y, i // 2, z, i % 2) for i in range(8)]
    begins = [device(i // 2, x, z, i % 2) for i in range(8)]
    barrier = pltpu.get_barrier_semaphore()
    for target in in_group + in_y + in_z:
        pl.semaphore_signal(barrier, inc=1, device_id=target, device_id_type=MESH)
    to_self = [(x == y) & (y == i // 2) & (c == i % 2) for i in range(8)]
    from_self = [(x == y) & (x == i // 2) & (c == i % 2) for i in range(8)]
    for i in range(8):
        @pl.when(jnp.logical_not(to_self[i]))
        def _():
            pl.semaphore_signal(barrier, inc=1, device_id=ends[i], device_id_type=MESH)

        @pl.when(jnp.logical_not(from_self[i]))
        def _():
            pl.semaphore_signal(barrier, inc=1, device_id=begins[i], device_id_type=MESH)
    pl.semaphore_wait(barrier, 7 + 3 + 15 + 16 - 2 * (x == y).astype(jnp.int32))

    spread = []
    for d in range(7):
        copy = remote(
            mixed_ref.at[group[d]], all_mixed.at[pl.ds(pl.multiple_of(g * ROWS, ROWS), ROWS)],
            msend.at[d], mrecv.at[d], in_group[d],
        )
        copy.start()
        spread.append(copy)
    all_mixed[pl.ds(pl.multiple_of(g * ROWS, ROWS), ROWS)] = mixed_ref[g]
    for copy in spread:
        copy.wait()
    total[...] = jnp.dot(cots_ref[...], all_mixed[...], preferred_element_type=F32)
    sums[...] = total[...].astype(BF16)
    copies = []
    for d in range(3):
        to = (y + d + 1) % 4
        copy = remote(sums.at[pl.ds(pl.multiple_of(to * 256, 256), 256)], ybuf.at[d], ysend.at[d], yrecv.at[d], in_y[d])
        copy.start()
        copies.append(copy)
    for copy in copies:
        copy.wait()
    own = total[pl.ds(pl.multiple_of(y * 256, 256), 256)]
    own = own + ybuf[0].astype(F32) + ybuf[1].astype(F32) + ybuf[2].astype(F32)
    part[...] = own.astype(BF16)
    copies = []
    for d in range(15):
        to = (z + d + 1) % 16
        copy = remote(part.at[pl.ds(pl.multiple_of(to * 16, 16), 16)], zbuf.at[d], zsend.at[d], zrecv.at[d], in_z[d])
        copy.start()
        copies.append(copy)
    for copy in copies:
        copy.wait()
    summed = part[pl.ds(pl.multiple_of(z * 16, 16), 16)].astype(F32)
    for d in range(15):
        summed = summed + zbuf[d].astype(F32)
    final[...] = summed * (1.0 / 256.0)
    for i in range(8):
        copy = remote(final, wide.at[g], asend.at[i], arecv.at[g], ends[i])

        @pl.when(jnp.logical_not(to_self[i]))
        def _():
            copy.start()

        @pl.when(to_self[i])
        def _():
            wide[g] = final[...]
    for i in range(8):
        @pl.when(jnp.logical_not(from_self[i]))
        def _():
            remote(final, wide.at[i], asend.at[i], arecv.at[i], begins[i]).wait_recv()

        @pl.when(jnp.logical_not(to_self[i]))
        def _():
            remote(final, wide.at[g], asend.at[i], arecv.at[g], ends[i]).wait_send()
    for i in range(8):
        out_ref[:, i * 128 : (i + 1) * 128] = wide[i]


def weight_sum(mixed_heads, cots):
    vmem = pl.BlockSpec(memory_space=pltpu.VMEM)
    dma = pltpu.SemaphoreType.DMA
    return pl.pallas_call(
        weight_kernel,
        out_shape=jax.ShapeDtypeStruct((16, WIDTH), F32),
        in_specs=[vmem, vmem],
        out_specs=vmem,
        scratch_shapes=[
            pltpu.VMEM((WIDTH, 128), BF16),
            pltpu.VMEM((WIDTH, 128), F32),
            pltpu.VMEM((WIDTH, 128), BF16),
            pltpu.VMEM((3, 256, 128), BF16),
            pltpu.VMEM((256, 128), BF16),
            pltpu.VMEM((15, 16, 128), BF16),
            pltpu.VMEM((16, 128), F32),
            pltpu.VMEM((8, 16, 128), F32),
            dma((7,)), dma((7,)), dma((3,)), dma((3,)), dma((15,)), dma((15,)), dma((8,)), dma((8,)),
        ],
        compiler_params=pltpu.CompilerParams(
            collective_id=1, has_side_effects=True, vmem_limit_bytes=32 * 1024 * 1024
        ),
        name="weight_sum",
    )(mixed_heads, cots)


def normalize(values):
    centred = values - jnp.mean(values, axis=-1, keepdims=True)
    inverse = lax.rsqrt(jnp.mean(centred * centred, axis=-1, keepdims=True) + EPSILON)
    return (centred * inverse, inverse)


def norm_backward(grad, normed, inverse):
    return inverse * (
        grad
        - jnp.mean(grad, axis=-1, keepdims=True)
        - normed * jnp.mean(grad * normed, axis=-1, keepdims=True)
    )


def slope_of(values):
    sigma = jax.nn.sigmoid(values)
    return sigma * (1.0 + values * (1.0 - sigma))


def seen(lengths):
    row = lax.broadcasted_iota(jnp.int32, (QROWS, KROWS), 0)
    column = lax.broadcasted_iota(jnp.int32, (QROWS, KROWS), 1)
    start = jnp.zeros((QROWS, KROWS), jnp.int32)
    end = jnp.zeros((), jnp.int32)
    for k in range(7):
        end = end + lengths[k]
        start = start + jnp.where(row >= end, lengths[k], 0)
    start = jnp.where(row >= FIRST, FIRST, start)
    start = jnp.where(row >= LAST, LAST, start)
    start = jnp.where(row >= ROWS, ROWS, start)
    local = (column >= start) & (column <= row)
    far = (row >= LAST) & (row < ROWS) & (column >= QROWS)
    near = (row >= ROWS) & (column >= FIRST) & (column < LAST)
    return local | far | near


def per_device(actions, lengths, partner_mask, norm_gain, w_in, w_out, cotangent):
    wall, cots, far = gather(partner_mask, actions, cotangent, w_in, w_out)
    inputs = actions[0].astype(F32)
    normed_in, inverse_in = normalize(inputs)
    far_inputs = jnp.concatenate([far[MOST:KEPT], far[:MOST]], axis=0).astype(F32)
    far_normed = normalize(far_inputs)[0]
    normed = (jnp.concatenate([normed_in, far_normed], axis=0) * norm_gain).astype(BF16)
    hidden = jnp.einsum("rk,skn->srn", normed, wall[:4], preferred_element_type=F32)
    active = jax.nn.silu(hidden).astype(BF16)
    gates = active[0, :QROWS].astype(F32)
    heads = lambda a: a.reshape(a.shape[0], HEADS, HEAD_DIM)
    value_heads, query_heads, key_heads = heads(active[1]), heads(active[2, :QROWS]), heads(active[3])
    visible = seen(lengths[0, 0])
    scores = jnp.einsum("qhd,khd->hqk", query_heads, key_heads, preferred_element_type=F32) * HEAD_DIM ** (-0.5)
    weights = (jnp.where(visible[None], jax.nn.silu(scores), 0.0) / MOST).astype(BF16)
    attended = jnp.einsum("hqk,khd->qhd", weights, value_heads, preferred_element_type=F32).reshape(QROWS, WIDTH)
    normed_out, inverse_out = normalize(attended)
    mixed = (normed_out[:ROWS] * gates[:ROWS]).astype(BF16)
    weight_grads = weight_sum(mixed.reshape(ROWS, HEADS, HEAD_DIM).transpose(1, 0, 2), cots)
    output = (jnp.dot(mixed, wall[4], preferred_element_type=F32) + inputs).astype(BF16)
    incoming = jnp.concatenate([cotangent[0], far[KEPT:]], axis=0)
    grad_mixed = lax.dot_general(incoming, wall[4], (((1,), (1,)), ((), ())), preferred_element_type=F32)
    grad_gates = grad_mixed[:ROWS] * normed_out[:ROWS]
    grad_attended = norm_backward(grad_mixed * gates, normed_out, inverse_out).astype(BF16)
    grad_heads = heads(grad_attended)
    grad_w = jnp.einsum("qhd,khd->hqk", grad_heads, value_heads, preferred_element_type=F32)
    grad_scores = (jnp.where(visible[None], grad_w * slope_of(scores), 0.0) * (HEAD_DIM ** (-0.5) / MOST)).astype(BF16)
    grad_queries = jnp.einsum("hqk,khd->qhd", grad_scores[:, :ROWS], key_heads, preferred_element_type=F32)
    grad_keys = jnp.einsum("hqk,qhd->khd", grad_scores[:, :, :ROWS], query_heads, preferred_element_type=F32)
    grad_values = jnp.einsum("hqk,qhd->khd", weights[:, :, :ROWS], grad_heads, preferred_element_type=F32)
    grad_active = jnp.stack(
        [grad_gates] + [g.reshape(ROWS, WIDTH) for g in (grad_values, grad_queries, grad_keys)], axis=0
    )
    grad_hidden = (grad_active * slope_of(hidden[:, :ROWS])).astype(BF16)
    grad_normed = jnp.einsum("srn,skn->rk", grad_hidden, wall[:4], preferred_element_type=F32)
    grad_input = cotangent[0].astype(F32) + norm_backward(grad_normed * norm_gain, normed_in, inverse_in)
    return (output[None], grad_input.astype(BF16)[None], weight_grads)


def solution(mesh):
    placed = (
        P("fsdp", "dp", None),
        P("fsdp", "dp", None),
        P("fsdp", "dp"),
        P(),
        P("fsdp", None),
        P("fsdp", None),
        P("fsdp", "dp", None),
    )
    return jax.shard_map(
        per_device,
        mesh=mesh,
        in_specs=placed,
        out_specs=(P("fsdp", "dp", None), P("fsdp", "dp", None), P("dp", None)),
        check_vma=False,
    )
```

```python
import jax
import jax.numpy as jnp
from jax import lax
from jax.experimental import pallas as pl
from jax.experimental.pallas import tpu as pltpu
from jax.sharding import PartitionSpec as P

HEADS = 8
HEAD_DIM = 128
SPILL = 16
MOST = 32
ROWS = 128
WIDTH = 1024
LAST = ROWS - SPILL
FIRST = LAST - MOST
NZ = 16
EPSILON = 1e-05
SCALE = HEAD_DIM ** (-0.5)
BACK = SCALE / MOST
MESH = pl.DeviceIdType.MESH
F32 = jnp.float32
BF16 = jnp.bfloat16
GATES, VALUES, QUERIES, KEYS, OUT = range(5)
QUARTER = {QUERIES: 16, KEYS: 16, VALUES: 16, GATES: 32, OUT: 32}
CHUNK = 32
LANES = 256


def device(x, y, z, c):
    return (x * NZ + z, y * 2 + c)


def remote(src, dst, send, recv, target):
    return pltpu.make_async_remote_copy(
        src_ref=src, dst_ref=dst, send_sem=send, recv_sem=recv, device_id=target, device_id_type=MESH
    )


def start_all(copies):
    for copy in copies:
        copy.start()


def dot(a, b):
    return jnp.dot(a, b, preferred_element_type=F32)


def dot_nt(a, b):
    return lax.dot_general(a, b, (((1,), (1,)), ((), ())), preferred_element_type=F32)


def dot_tn(a, b):
    return lax.dot_general(a, b, (((0,), (0,)), ((), ())), preferred_element_type=F32)


def normalize(values):
    centred = values - jnp.mean(values, axis=-1, keepdims=True)
    inverse = lax.rsqrt(jnp.mean(centred * centred, axis=-1, keepdims=True) + EPSILON)
    return (centred * inverse, inverse)


def norm_backward(grad, normed, inverse):
    return inverse * (
        grad
        - jnp.mean(grad, axis=-1, keepdims=True)
        - normed * jnp.mean(grad * normed, axis=-1, keepdims=True)
    )


def silu_parts(values):
    sigma = jax.nn.sigmoid(values)
    return values * sigma, sigma * (1.0 + values * (1.0 - sigma))


class Section:
    def __init__(self, src, wall, t, at, send, recv, local):
        x, y, z, c = at
        quarter = QUARTER[t]
        direct = ROWS - 4 * quarter
        other = device(x, y, z, 1 - c)

        def rows(owner, start, count):
            base = (2 * owner + c) * ROWS + start
            return wall.at[t, pl.ds(pl.multiple_of(base, 16), count)]

        ahead, behind, across = (y + 1) % 4, (y + 3) % 4, (y + 2) % 4
        self.own = pltpu.make_async_copy(src, rows(y, 0, ROWS), local)
        self.first = []
        self.forwards = []
        self.halves = []
        if direct:
            half = direct // 2
            piece = src.at[:direct]
            lane = lambda d, i: device(x, d, z, c)
            self.first += [
                remote(piece, rows(y, 0, direct), send.at[0], recv.at[0], lane(ahead, 0)),
                remote(piece, rows(y, 0, direct), send.at[1], recv.at[1], lane(behind, 0)),
            ]
            self.forwards = [
                remote(rows(behind, 0, half), rows(behind, 0, half), send.at[2], recv.at[2], lane(ahead, 0)),
                remote(rows(ahead, half, half), rows(ahead, half, half), send.at[3], recv.at[3], lane(behind, 0)),
            ]
            self.cores = [
                remote(rows(behind, 0, direct), rows(behind, 0, direct), send.at[5], recv.at[5], other),
                remote(rows(ahead, 0, direct), rows(ahead, 0, direct), send.at[6], recv.at[6], other),
            ]
            self.halves = [
                remote(rows(across, h * half, half), rows(across, h * half, half), send.at[7 + h], recv.at[7 + h], other)
                for h in range(2)
            ]
        self.quarters = []
        self.spread = []
        self.cores_late = []
        place = direct + x * quarter
        for d in range(1, 4):
            to = (y + d) % 4
            source = (y + 4 - d) % 4
            self.quarters.append(
                remote(
                    src.at[pl.ds(pl.multiple_of(place, 16), quarter)], rows(y, place, quarter),
                    send.at[8 + d], recv.at[8 + d], device(x, to, z, c),
                )
            )
            mine = rows(source, place, quarter)
            self.spread.append(
                [
                    remote(
                        mine, mine, send.at[11 + 3 * (d - 1) + e], recv.at[11 + 3 * (d - 1) + e],
                        device((x + e) % 4, y, z, c),
                    )
                    for e in range(1, 4)
                ]
            )
            whole = rows(source, direct, 4 * quarter)
            self.cores_late.append(remote(whole, whole, send.at[20 + d], recv.at[20 + d], other))
        self.to_core = remote(src, rows(y, 0, ROWS), send.at[4], recv.at[4], other)

    def start(self):
        start_all(self.quarters)
        start_all(self.first)
        self.to_core.start()
        self.own.start()

    def forward(self):
        for quarter, spread in zip(self.quarters, self.spread):
            quarter.wait_recv()
            start_all(spread)
        for i, copy in enumerate(self.first):
            copy.wait_recv()
            self.forwards[i].start()
            self.cores[i].start()

    def finish(self):
        for forward, half in zip(self.forwards, self.halves):
            forward.wait_recv()
            half.start()
        for spread, late in zip(self.spread, self.cores_late):
            for copy in spread:
                copy.wait_recv()
            late.start()

    def arrived(self):
        self.own.wait()
        self.to_core.wait_recv()
        if self.first:
            for copy in self.cores + self.halves:
                copy.wait_recv()
        for copy in self.cores_late:
            copy.wait_recv()

    def sent(self):
        copies = self.quarters + sum(self.spread, []) + self.cores_late + [self.to_core]
        if self.first:
            copies += self.first + self.forwards + self.cores + self.halves
        for copy in copies:
            copy.wait_send()


class Ring:
    def __init__(self, own, view, half, me, towards, other, send, recv):
        ahead, behind, across = (me + 1) % 4, (me + 3) % 4, (me + 2) % 4
        self.first = [
            remote(own, view(me), send.at[0], recv.at[0], towards(ahead)),
            remote(own, view(me), send.at[1], recv.at[1], towards(behind)),
            remote(own, view(me), send.at[4], recv.at[4], other),
        ]
        self.behind = [
            remote(half(behind, 0), half(behind, 0), send.at[2], recv.at[2], towards(ahead)),
            remote(view(behind), view(behind), send.at[5], recv.at[5], other),
        ]
        self.ahead = [
            remote(half(ahead, 1), half(ahead, 1), send.at[3], recv.at[3], towards(behind)),
            remote(view(ahead), view(ahead), send.at[6], recv.at[6], other),
        ]
        self.across = [
            remote(half(across, 0), half(across, 0), send.at[7], recv.at[7], other),
            remote(half(across, 1), half(across, 1), send.at[8], recv.at[8], other),
        ]

    def start(self):
        start_all(self.first)

    def forward(self):
        self.first[0].wait_recv()
        start_all(self.behind)
        self.first[1].wait_recv()
        start_all(self.ahead)

    def finish(self):
        self.behind[0].wait_recv()
        self.across[0].start()
        self.ahead[0].wait_recv()
        self.across[1].start()

    def arrived(self):
        for copy in [self.first[2], self.behind[1], self.ahead[1]] + self.across:
            copy.wait_recv()

    def sent(self):
        for copy in self.first + self.behind + self.ahead + self.across:
            copy.wait_send()


class Swap:
    def __init__(self, held, landed, at, order, mask, send, recv):
        x, y, z, c = at
        self.held, self.landed, self.order, self.mask = held, landed, order, mask
        self.copies = []
        for step, bit in enumerate(order):
            size = 1 << bit
            to = z + size - 2 * size * (z // size % 2)
            self.copies.append(
                remote(held.at[step], landed.at[step], send.at[step], recv.at[step], device(x, y, to, c))
            )

    def start(self):
        self.copies[0].start()

    def turn(self, step):
        self.copies[step].wait_recv()
        bit = jnp.full((SPILL, WIDTH), lax.shift_right_logical(self.mask, self.order[step]) & 1, jnp.int32)
        chosen = jnp.where(bit == 1, self.landed[step].astype(F32), self.held[step].astype(F32))
        self.held[step + 1] = chosen.astype(BF16)
        if step < 2:
            self.copies[step + 1].start()

    def sent(self):
        for copy in self.copies:
            copy.wait_send()


def layer_kernel(
    mask_ref, lengths_ref, actions_hbm, gain_hbm, w_in_ref, w_out_ref, cot_hbm,
    output_ref, grad_ref, weight_ref,
    actions, gain, cot, wall, cots, cot_t, normed, normed_in, inverse_in,
    active, slopes, weights, score_slopes, attended, normed_out, inverse_out, mixed,
    far_normed, far_active, grad_att, grad_mix, grad_hidden,
    held, landed, all_mixed, total, sums, xbuf, part, zbuf, final, wide,
    load_sem, wsend, wrecv, wlocal, csend, crecv, clocal, ssend, srecv,
    msend, mrecv, xsend, xrecv, zsend, zrecv, asend, arecv,
):
    dp = lax.axis_index("dp")
    me = lax.axis_index("fsdp")
    x, y, z, c = dp // NZ, me // 2, dp % NZ, me % 2
    at = (x, y, z, c)
    other = device(x, y, z, 1 - c)
    group = [(me + d) % 8 for d in range(1, 8)]
    in_group = [(dp, i) for i in group]
    in_x = [device((x + d) % 4, y, z, c) for d in range(1, 4)]
    in_z = [device(x, y, (z + d) % NZ, c) for d in range(1, NZ)]
    peers = in_group + in_x + in_z

    loads = [
        pltpu.make_async_copy(actions_hbm.at[0], actions, load_sem.at[0]),
        pltpu.make_async_copy(cot_hbm.at[0], cot, load_sem.at[1]),
        pltpu.make_async_copy(gain_hbm, gain, load_sem.at[2]),
    ]
    start_all(loads)
    barrier = pltpu.get_barrier_semaphore()
    for target in peers:
        pl.semaphore_signal(barrier, inc=1, device_id=target, device_id_type=MESH)

    sections = {
        t: Section(
            w_out_ref if t == OUT else w_in_ref.at[:, t * WIDTH : (t + 1) * WIDTH],
            wall, t, at, wsend.at[t], wrecv.at[t], wlocal.at[t],
        )
        for t in range(5)
    }
    column = lambda i: pl.ds(pl.multiple_of((2 * i + c) * ROWS, ROWS), ROWS)
    cring = Ring(
        cot_t,
        lambda i: cots.at[:, column(i)],
        lambda i, h: cots.at[h * 512 : h * 512 + 512, column(i)],
        y, lambda i: device(x, i, z, c), other, csend, crecv,
    )
    cown = pltpu.make_async_copy(cot_t, cots.at[:, column(y)], clocal)
    mask = mask_ref[0, 0]
    orders = [(2, 1, 0), (0, 1, 2), (2, 1, 0), (0, 1, 2)]
    swaps = [Swap(held.at[i], landed.at[i], at, orders[i], mask, ssend.at[i], srecv.at[i]) for i in range(4)]

    for copy in loads:
        copy.wait()
    held[0, 0] = actions[FIRST : FIRST + 16]
    held[1, 0] = actions[FIRST + 16 : LAST]
    held[2, 0] = actions[LAST:]
    held[3, 0] = cot[LAST:]
    pl.semaphore_wait(barrier, len(peers))

    sections[QUERIES].start()
    swaps[0].start()
    swaps[1].start()
    sections[KEYS].start()

    for r in range(0, ROWS, CHUNK):
        n, inverse = normalize(actions[r : r + CHUNK].astype(F32))
        normed_in[r : r + CHUNK] = n
        inverse_in[r : r + CHUNK] = inverse
        normed[r : r + CHUNK] = (n * gain[...]).astype(BF16)
    cot_t[...] = cot[...].astype(F32).T.astype(BF16)
    cown.start()

    row = lax.broadcasted_iota(jnp.int32, (ROWS, ROWS), 0)
    col = lax.broadcasted_iota(jnp.int32, (ROWS, ROWS), 1)
    begin = jnp.zeros((ROWS, ROWS), jnp.int32)
    end = jnp.zeros((), jnp.int32)
    for k in range(7):
        end = end + lengths_ref[0, 0, k]
        begin = begin + jnp.where(row >= end, lengths_ref[0, 0, k], 0)
    begin = jnp.where(row >= FIRST, FIRST, begin)
    begin = jnp.where(row >= LAST, LAST, begin)
    visible = (col >= begin) & (col <= row)

    def project(t):
        for l in range(0, WIDTH, LANES):
            hidden = dot(normed[...], wall[t, :, l : l + LANES])
            value, slope = silu_parts(hidden)
            active[t, :, l : l + LANES] = value.astype(BF16)
            slopes[t, :, l : l + LANES] = slope

    def small(t, rows, first, count):
        for l in range(0, WIDTH, LANES):
            hidden = dot(rows, wall[t, :, l : l + LANES])
            far_active[t, first : first + count, l : l + LANES] = silu_parts(hidden)[0].astype(BF16)

    def head(h):
        return slice(h * HEAD_DIM, (h + 1) * HEAD_DIM)

    swaps[1].turn(0)
    sections[QUERIES].forward()
    sections[VALUES].start()
    swaps[0].turn(0)
    swaps[1].turn(1)
    sections[KEYS].forward()
    sections[GATES].start()
    sections[QUERIES].finish()
    swaps[0].turn(1)
    sections[VALUES].forward()
    sections[KEYS].finish()
    cring.start()
    sections[QUERIES].arrived()
    project(QUERIES)
    swaps[0].turn(2)
    swaps[1].turn(2)
    swaps[2].start()
    swaps[3].start()
    sections[GATES].forward()
    sections[VALUES].finish()
    sections[KEYS].arrived()
    project(KEYS)
    far_inputs = jnp.concatenate([held[0, 3], held[1, 3]], axis=0).astype(F32)
    far_normed[:MOST] = (normalize(far_inputs)[0] * gain[...]).astype(BF16)
    small(KEYS, far_normed[:MOST], 0, MOST)
    sections[GATES].finish()
    sections[OUT].start()
    sections[VALUES].arrived()
    project(VALUES)
    small(VALUES, far_normed[:MOST], 0, MOST)
    cring.forward()
    swaps[3].turn(0)

    far_slopes = []
    for h in range(HEADS):
        q, k, v = active[QUERIES, :, head(h)], active[KEYS, :, head(h)], active[VALUES, :, head(h)]
        value, slope = silu_parts(dot_nt(q, k) * SCALE)
        weight = (jnp.where(visible, value, 0.0) / MOST).astype(BF16)
        weights[h] = weight
        score_slopes[h] = jnp.where(visible, slope, 0.0) * BACK
        value, slope = silu_parts(dot_nt(q[LAST:], far_active[KEYS, :MOST, head(h)]) * SCALE)
        far_slopes.append(slope * BACK)
        far_part = dot((value / MOST).astype(BF16), far_active[VALUES, :MOST, head(h)])
        local_part = dot(weight, v)
        attended[:LAST, head(h)] = local_part[:LAST]
        attended[LAST:, head(h)] = local_part[LAST:] + far_part

    sections[GATES].arrived()
    project(GATES)
    for r in range(0, ROWS, CHUNK):
        n, inverse = normalize(attended[r : r + CHUNK])
        normed_out[r : r + CHUNK] = n
        inverse_out[r : r + CHUNK] = inverse
        mix = (n * active[GATES, r : r + CHUNK].astype(F32)).astype(BF16)
        for h in range(HEADS):
            mixed[h, r : r + CHUNK] = mix[:, head(h)]
    own_rows = pl.ds(pl.multiple_of(me * ROWS, ROWS), ROWS)
    spread = [
        remote(mixed.at[group[d]], all_mixed.at[own_rows], msend.at[d], mrecv.at[d], in_group[d]) for d in range(7)
    ]
    start_all(spread)
    all_mixed[own_rows] = mixed[me]

    cring.finish()
    swaps[2].turn(0)
    swaps[3].turn(1)
    sections[OUT].forward()

    for copy in spread:
        copy.wait_recv()
    cown.wait()
    cring.arrived()
    total[...] = dot(cots[...], all_mixed[...])
    sums[...] = total[...].astype(BF16)
    xcopies = [
        remote(sums.at[pl.ds(pl.multiple_of((x + d + 1) % 4 * 256, 256), 256)], xbuf.at[d], xsend.at[d], xrecv.at[d], in_x[d])
        for d in range(3)
    ]
    start_all(xcopies)

    swaps[2].turn(1)
    sections[OUT].finish()
    sections[OUT].arrived()
    for l in range(0, WIDTH, LANES):
        grad_mix[:, l : l + LANES] = dot_nt(cot[...], wall[OUT, l : l + LANES])

    for copy in xcopies:
        copy.wait_recv()
    part[...] = (
        total[pl.ds(pl.multiple_of(x * 256, 256), 256)]
        + xbuf[0].astype(F32) + xbuf[1].astype(F32) + xbuf[2].astype(F32)
    ).astype(BF16)
    zcopies = [
        remote(part.at[pl.ds(pl.multiple_of((z + d + 1) % NZ * 16, 16), 16)], zbuf.at[d], zsend.at[d], zrecv.at[d], in_z[d])
        for d in range(NZ - 1)
    ]
    start_all(zcopies)

    for r in range(0, ROWS, CHUNK):
        span = slice(r, r + CHUNK)
        grad = grad_mix[span]
        n = normed_out[span]
        grad_hidden[GATES, span] = (grad * n * slopes[GATES, span]).astype(BF16)
        grad_att[span] = norm_backward(
            grad * active[GATES, span].astype(F32), n, inverse_out[span]
        ).astype(BF16)

    swaps[2].turn(2)
    swaps[3].turn(2)
    spill_inputs = held[2, 3].astype(F32)
    far_normed[MOST:] = (normalize(spill_inputs)[0] * gain[...]).astype(BF16)
    for t in (GATES, VALUES, QUERIES, KEYS):
        small(t, far_normed[MOST:], MOST, SPILL)
    near_grad = dot_nt(held[3, 3], wall[OUT])
    rows16 = lax.broadcasted_iota(jnp.int32, (SPILL, SPILL), 0)
    cols16 = lax.broadcasted_iota(jnp.int32, (SPILL, SPILL), 1)
    causal = cols16 <= rows16
    near_weights, near_slopes, near_attended = [], [], []
    for h in range(HEADS):
        q = far_active[QUERIES, MOST:, head(h)]
        value, slope = silu_parts(dot_nt(q, active[KEYS, FIRST:LAST, head(h)]) * SCALE)
        weight = (value / MOST).astype(BF16)
        near_weights.append(weight)
        near_slopes.append(slope * BACK)
        value, _ = silu_parts(dot_nt(q, far_active[KEYS, MOST:, head(h)]) * SCALE)
        weight2 = (jnp.where(causal, value, 0.0) / MOST).astype(BF16)
        near_attended.append(
            dot(weight, active[VALUES, FIRST:LAST, head(h)]) + dot(weight2, far_active[VALUES, MOST:, head(h)])
        )
    near_normed, near_inverse = normalize(jnp.concatenate(near_attended, axis=1))
    near_att = norm_backward(
        near_grad * far_active[GATES, MOST:].astype(F32), near_normed, near_inverse
    ).astype(BF16)

    for h in range(HEADS):
        q, k, v = active[QUERIES, :, head(h)], active[KEYS, :, head(h)], active[VALUES, :, head(h)]
        g = grad_att[:, head(h)]
        grad_s = (dot_nt(g, v) * score_slopes[h]).astype(BF16)
        far_s = (dot_nt(g[LAST:], far_active[VALUES, :MOST, head(h)]) * far_slopes[h]).astype(BF16)
        near_g = near_att[:, head(h)]
        near_s = (dot_nt(near_g, v[FIRST:LAST]) * near_slopes[h]).astype(BF16)
        grad_q = dot(grad_s, k)
        far_q = dot(far_s, far_active[KEYS, :MOST, head(h)])
        grad_k = dot_tn(grad_s, q)
        near_k = dot_tn(near_s, far_active[QUERIES, MOST:, head(h)])
        grad_v = dot_tn(weights[h], g)
        near_v = dot_tn(near_weights[h], near_g)
        slope = slopes[QUERIES, :, head(h)]
        grad_hidden[QUERIES, :LAST, head(h)] = (grad_q[:LAST] * slope[:LAST]).astype(BF16)
        grad_hidden[QUERIES, LAST:, head(h)] = ((grad_q[LAST:] + far_q) * slope[LAST:]).astype(BF16)
        for t, grad, extra in ((KEYS, grad_k, near_k), (VALUES, grad_v, near_v)):
            slope = slopes[t, :, head(h)]
            grad_hidden[t, :FIRST, head(h)] = (grad[:FIRST] * slope[:FIRST]).astype(BF16)
            grad_hidden[t, FIRST:LAST, head(h)] = ((grad[FIRST:LAST] + extra) * slope[FIRST:LAST]).astype(BF16)
            grad_hidden[t, LAST:, head(h)] = (grad[LAST:] * slope[LAST:]).astype(BF16)

    for copy in zcopies:
        copy.wait_recv()
    summed = part[pl.ds(pl.multiple_of(z * 16, 16), 16)].astype(F32)
    for d in range(NZ - 1):
        summed = summed + zbuf[d].astype(F32)
    final[...] = summed * (1.0 / 256.0)
    acopies = [remote(final, wide.at[me], asend.at[d], arecv.at[d], in_group[d]) for d in range(7)]
    start_all(acopies)
    wide[me] = final[...]

    mixed_rows = jnp.concatenate([mixed[h] for h in range(HEADS)], axis=1)
    for l in range(0, WIDTH, LANES):
        output_ref[0, :, l : l + LANES] = (
            dot(mixed_rows, wall[OUT, :, l : l + LANES]) + actions[:, l : l + LANES].astype(F32)
        ).astype(BF16)
    for l in range(0, WIDTH, LANES):
        grad_mix[:, l : l + LANES] = (
            dot_nt(grad_hidden[0], wall[0, l : l + LANES])
            + dot_nt(grad_hidden[1], wall[1, l : l + LANES])
            + dot_nt(grad_hidden[2], wall[2, l : l + LANES])
            + dot_nt(grad_hidden[3], wall[3, l : l + LANES])
        ) * gain[:, l : l + LANES]
    for r in range(0, ROWS, CHUNK):
        span = slice(r, r + CHUNK)
        grad_ref[0, span] = (
            cot[span].astype(F32) + norm_backward(grad_mix[span], normed_in[span], inverse_in[span])
        ).astype(BF16)

    for copy in acopies:
        copy.wait_recv()
    for i in range(8):
        weight_ref[:, i * 128 : (i + 1) * 128] = wide[i]
    for t in range(5):
        sections[t].sent()
    cring.sent()
    for swap in swaps:
        swap.sent()
    for copy in spread + xcopies + zcopies + acopies:
        copy.wait_send()


def per_device(actions, lengths, partner_mask, norm_gain, w_in, w_out, cotangent):
    hbm = pl.BlockSpec(memory_space=pl.ANY)
    vmem = pl.BlockSpec(memory_space=pltpu.VMEM)
    smem = pl.BlockSpec(memory_space=pltpu.SMEM)
    dma = pltpu.SemaphoreType.DMA
    block = (ROWS, WIDTH)
    return pl.pallas_call(
        layer_kernel,
        out_shape=(
            jax.ShapeDtypeStruct((1, ROWS, WIDTH), BF16),
            jax.ShapeDtypeStruct((1, ROWS, WIDTH), BF16),
            jax.ShapeDtypeStruct((16, WIDTH), F32),
        ),
        in_specs=[smem, smem, hbm, hbm, hbm, hbm, hbm],
        out_specs=(vmem, vmem, vmem),
        scratch_shapes=[
            pltpu.VMEM(block, BF16),
            pltpu.VMEM((1, WIDTH), F32),
            pltpu.VMEM(block, BF16),
            pltpu.VMEM((5, WIDTH, WIDTH), BF16),
            pltpu.VMEM((WIDTH, WIDTH), BF16),
            pltpu.VMEM((WIDTH, ROWS), BF16),
            pltpu.VMEM(block, BF16),
            pltpu.VMEM(block, F32),
            pltpu.VMEM((ROWS, 1), F32),
            pltpu.VMEM((4, ROWS, WIDTH), BF16),
            pltpu.VMEM((4, ROWS, WIDTH), F32),
            pltpu.VMEM((HEADS, ROWS, ROWS), BF16),
            pltpu.VMEM((HEADS, ROWS, ROWS), F32),
            pltpu.VMEM(block, F32),
            pltpu.VMEM(block, F32),
            pltpu.VMEM((ROWS, 1), F32),
            pltpu.VMEM((HEADS, ROWS, HEAD_DIM), BF16),
            pltpu.VMEM((MOST + SPILL, WIDTH), BF16),
            pltpu.VMEM((4, MOST + SPILL, WIDTH), BF16),
            pltpu.VMEM(block, BF16),
            pltpu.VMEM(block, F32),
            pltpu.VMEM((4, ROWS, WIDTH), BF16),
            pltpu.VMEM((4, 4, SPILL, WIDTH), BF16),
            pltpu.VMEM((4, 3, SPILL, WIDTH), BF16),
            pltpu.VMEM((WIDTH, 128), BF16),
            pltpu.VMEM((WIDTH, 128), F32),
            pltpu.VMEM((WIDTH, 128), BF16),
            pltpu.VMEM((3, 256, 128), BF16),
            pltpu.VMEM((256, 128), BF16),
            pltpu.VMEM((NZ - 1, 16, 128), BF16),
            pltpu.VMEM((16, 128), F32),
            pltpu.VMEM((8, 16, 128), F32),
            dma((3,)), dma((5, 24)), dma((5, 24)), dma((5,)), dma((9,)), dma((9,)), dma,
            dma((4, 3)), dma((4, 3)), dma((7,)), dma((7,)), dma((3,)), dma((3,)),
            dma((NZ - 1,)), dma((NZ - 1,)), dma((7,)), dma((7,)),
        ],
        compiler_params=pltpu.CompilerParams(
            collective_id=0, has_side_effects=True, vmem_limit_bytes=56 * 1024 * 1024
        ),
        name="layer",
    )(partner_mask, lengths, actions, norm_gain.reshape(1, WIDTH), w_in, w_out, cotangent)


def solution(mesh):
    placed = (
        P("fsdp", "dp", None),
        P("fsdp", "dp", None),
        P("fsdp", "dp"),
        P(),
        P("fsdp", None),
        P("fsdp", None),
        P("fsdp", "dp", None),
    )
    return jax.shard_map(
        per_device,
        mesh=mesh,
        in_specs=placed,
        out_specs=(P("fsdp", "dp", None), P("fsdp", "dp", None), P("dp", None)),
        check_vma=False,
    )
```

```python
import jax
import jax.numpy as jnp
from jax import lax
from jax.experimental import pallas as pl
from jax.experimental.pallas import tpu as pltpu
from jax.sharding import PartitionSpec as P

HEADS = 8
HEAD_DIM = 128
SPILL = 16
MOST = 32
ROWS = 128
WIDTH = 1024
LAST = ROWS - SPILL
FIRST = LAST - MOST
NZ = 16
EPSILON = 1e-05
SCALE = HEAD_DIM ** (-0.5)
BACK = SCALE / MOST
MESH = pl.DeviceIdType.MESH
F32 = jnp.float32
BF16 = jnp.bfloat16
GATES, VALUES, QUERIES, KEYS, OUT = range(5)
HALF = WIDTH // 2
PLAN = {
    QUERIES: (64, [("x", 64, 16, 0, WIDTH)]),
    KEYS: (0, [("x", 0, 16, 0, WIDTH), ("z", 64, 16, 0, WIDTH)]),
    VALUES: (0, [("x", 0, 16, 0, WIDTH), ("z", 64, 16, 0, WIDTH)]),
    GATES: (64, [("x", 64, 16, 0, HALF), ("z", 64, 16, HALF, HALF)]),
    OUT: (0, [("x", 0, 16, 0, WIDTH), ("z", 64, 16, 0, WIDTH)]),
}
CHUNK = 32
LANES = 256


def device(x, y, z, c):
    return (x * NZ + z, y * 2 + c)


def remote(src, dst, send, recv, target):
    return pltpu.make_async_remote_copy(
        src_ref=src, dst_ref=dst, send_sem=send, recv_sem=recv, device_id=target, device_id_type=MESH
    )


def start_all(copies):
    for copy in copies:
        copy.start()


def dot(a, b):
    return jnp.dot(a, b, preferred_element_type=F32)


def dot_nt(a, b):
    return lax.dot_general(a, b, (((1,), (1,)), ((), ())), preferred_element_type=F32)


def dot_tn(a, b):
    return lax.dot_general(a, b, (((0,), (0,)), ((), ())), preferred_element_type=F32)


def normalize(values):
    centred = values - jnp.mean(values, axis=-1, keepdims=True)
    inverse = lax.rsqrt(jnp.mean(centred * centred, axis=-1, keepdims=True) + EPSILON)
    return (centred * inverse, inverse)


def norm_backward(grad, normed, inverse):
    return inverse * (
        grad
        - jnp.mean(grad, axis=-1, keepdims=True)
        - normed * jnp.mean(grad * normed, axis=-1, keepdims=True)
    )


def silu_parts(values):
    sigma = jax.nn.sigmoid(values)
    return values * sigma, sigma * (1.0 + values * (1.0 - sigma))


class Section:
    def __init__(self, src, wall, t, at, send, recv, local):
        x, y, z, c = at
        direct, blocks = PLAN[t]
        other = device(x, y, z, 1 - c)
        used = [0]

        def move(piece, target, source=None):
            slot = used[0]
            used[0] += 1
            return remote(piece if source is None else source, piece, send.at[slot], recv.at[slot], target)

        def block(owner, first, count, column=0, columns=WIDTH):
            base = pl.multiple_of((2 * owner + c) * ROWS + first, 16)
            return wall.at[t, pl.ds(base, count), column : column + columns]

        ahead, behind, across = (y + 1) % 4, (y + 3) % 4, (y + 2) % 4
        to_ahead, to_behind = device(x, ahead, z, c), device(x, behind, z, c)
        self.own = pltpu.make_async_copy(src, block(y, 0, ROWS), local)
        self.to_core = move(block(y, 0, ROWS), other, src)
        self.first, self.forwards, self.cores, self.halves = [], [], [], []
        if direct:
            half = direct // 2
            piece = src.at[:direct]
            self.first = [move(block(y, 0, direct), to_ahead, piece), move(block(y, 0, direct), to_behind, piece)]
            self.forwards = [move(block(behind, 0, half), to_ahead), move(block(ahead, half, half), to_behind)]
            self.cores = [move(block(behind, 0, direct), other), move(block(ahead, 0, direct), other)]
            self.halves = [move(block(across, h * half, half), other) for h in range(2)]
        self.near, self.far, self.spreads = [], [], {}
        for d, source, to, onward in ((1, behind, to_ahead, to_ahead), (3, ahead, to_behind, to_behind)):
            for axis, first, count, column, columns in blocks:
                first = first + (x if axis == "x" else z % 4) * count
                fetched = move(
                    block(y, first, count, column, columns), to,
                    src.at[pl.ds(pl.multiple_of(first, 16), count), column : column + columns],
                )
                part = columns // 2
                passed = move(block(source, first, count, column + (part if d == 3 else 0), part), onward)
                self.near.append((fetched, passed))
        for d, source in ((1, behind), (3, ahead), (2, across)):
            self.spreads[d] = []
            for axis, first, count, column, columns in blocks:
                first = first + (x if axis == "x" else z % 4) * count
                whole = block(source, first, count, column, columns)
                if axis == "x":
                    spread = [move(whole, device((x + e) % 4, y, z, c)) for e in (2, 1, 3)]
                else:
                    part = columns // 2
                    spread = [
                        move(block(source, first, count, column, part), device(x, y, (z + 2) % NZ, c)),
                        move(block(source, first, count, column + part, part), device(x, y, (z + NZ - 2) % NZ, c)),
                        move(whole, device(x, y, (z + 1) % NZ, c)),
                        move(whole, device(x, y, (z + NZ - 1) % NZ, c)),
                    ]
                self.spreads[d].append(spread)
        self.late = {d: move(block((y + 4 - d) % 4, direct, ROWS - direct), other) for d in (1, 3, 2)}

    def fetch(self):
        for fetched, _ in self.near:
            fetched.start()

    def start(self):
        start_all(self.first)
        self.to_core.start()
        self.own.start()

    def spread(self):
        for (fetched, passed), spread in zip(self.near, self.spreads[1] + self.spreads[3]):
            fetched.wait_recv()
            passed.start()
            start_all(spread)

    def across(self):
        kinds = len(self.spreads[2])
        for i, spread in enumerate(self.spreads[2]):
            self.near[i][1].wait_recv()
            self.near[kinds + i][1].wait_recv()
            start_all(spread)

    def collect(self):
        for d, late in self.late.items():
            for copy in sum(self.spreads[d], []):
                copy.wait_recv()
            late.start()

    def forward(self):
        for i, copy in enumerate(self.first):
            copy.wait_recv()
            self.forwards[i].start()
            self.cores[i].start()

    def finish(self):
        for forward, half in zip(self.forwards, self.halves):
            forward.wait_recv()
            half.start()

    def arrived(self):
        self.own.wait()
        for copy in [self.to_core] + self.cores + self.halves + list(self.late.values()):
            copy.wait_recv()

    def sent(self):
        copies = [self.to_core] + self.first + self.forwards + self.cores + self.halves
        copies += list(self.late.values()) + sum(sum(self.spreads.values(), []), [])
        for fetched, passed in self.near:
            copies += [fetched, passed]
        for copy in copies:
            copy.wait_send()


class Ring:
    def __init__(self, own, view, half, me, towards, other, send, recv):
        ahead, behind, across = (me + 1) % 4, (me + 3) % 4, (me + 2) % 4
        self.first = [
            remote(own, view(me), send.at[0], recv.at[0], towards(ahead)),
            remote(own, view(me), send.at[1], recv.at[1], towards(behind)),
            remote(own, view(me), send.at[4], recv.at[4], other),
        ]
        self.behind = [
            remote(half(behind, 0), half(behind, 0), send.at[2], recv.at[2], towards(ahead)),
            remote(view(behind), view(behind), send.at[5], recv.at[5], other),
        ]
        self.ahead = [
            remote(half(ahead, 1), half(ahead, 1), send.at[3], recv.at[3], towards(behind)),
            remote(view(ahead), view(ahead), send.at[6], recv.at[6], other),
        ]
        self.across = [
            remote(half(across, 0), half(across, 0), send.at[7], recv.at[7], other),
            remote(half(across, 1), half(across, 1), send.at[8], recv.at[8], other),
        ]

    def start(self):
        start_all(self.first)

    def forward(self):
        self.first[0].wait_recv()
        start_all(self.behind)
        self.first[1].wait_recv()
        start_all(self.ahead)

    def finish(self):
        self.behind[0].wait_recv()
        self.across[0].start()
        self.ahead[0].wait_recv()
        self.across[1].start()

    def arrived(self):
        for copy in [self.first[2], self.behind[1], self.ahead[1]] + self.across:
            copy.wait_recv()

    def sent(self):
        for copy in self.first + self.behind + self.ahead + self.across:
            copy.wait_send()


class Swap:
    def __init__(self, held, landed, at, order, mask, send, recv):
        x, y, z, c = at
        self.held, self.landed, self.order, self.mask = held, landed, order, mask
        self.copies = []
        for step, bit in enumerate(order):
            size = 1 << bit
            to = z + size - 2 * size * (z // size % 2)
            self.copies.append(
                remote(held.at[step], landed.at[step], send.at[step], recv.at[step], device(x, y, to, c))
            )

    def start(self):
        self.copies[0].start()

    def turn(self, step):
        self.copies[step].wait_recv()
        bit = jnp.full((SPILL, WIDTH), lax.shift_right_logical(self.mask[0, 0], self.order[step]) & 1, jnp.int32)
        chosen = jnp.where(bit == 1, self.landed[step].astype(F32), self.held[step].astype(F32))
        self.held[step + 1] = chosen.astype(BF16)
        if step < 2:
            self.copies[step + 1].start()

    def sent(self):
        for copy in self.copies:
            copy.wait_send()


def layer_kernel(
    mask_hbm, lengths_hbm, actions_hbm, gain_hbm, w_in_ref, w_out_ref, cot_hbm,
    output_hbm, grad_hbm, weight_hbm,
    mask_ref, lengths_ref, output, grad_input, weight_grad, store_sem,
    actions, gain, cot, wall, cots, cot_t, normed, normed_in, inverse_in,
    active, slopes, weights, score_slopes, attended, normed_out, inverse_out, mixed,
    far_normed, far_active, grad_att, grad_mix, grad_hidden,
    held, landed, all_mixed, total, sums, xbuf, part, zbuf, final, wide,
    load_sem, wsend, wrecv, wlocal, csend, crecv, clocal, ssend, srecv,
    msend, mrecv, xsend, xrecv, zsend, zrecv, asend, arecv,
):
    dp = lax.axis_index("dp")
    me = lax.axis_index("fsdp")
    x, y, z, c = dp // NZ, me // 2, dp % NZ, me % 2
    at = (x, y, z, c)
    other = device(x, y, z, 1 - c)
    group = [(me + d) % 8 for d in range(1, 8)]
    in_group = [(dp, i) for i in group]
    in_x = [device((x + d) % 4, y, z, c) for d in range(1, 4)]
    in_z = [device(x, y, (z + d) % NZ, c) for d in range(1, NZ)]
    peers = in_group + in_x + in_z

    loads = [
        pltpu.make_async_copy(actions_hbm.at[0], actions, load_sem.at[0]),
        pltpu.make_async_copy(cot_hbm.at[0], cot, load_sem.at[1]),
        pltpu.make_async_copy(gain_hbm, gain, load_sem.at[2]),
        pltpu.make_async_copy(mask_hbm, mask_ref, load_sem.at[3]),
        pltpu.make_async_copy(lengths_hbm, lengths_ref, load_sem.at[4]),
    ]
    start_all(loads)
    barrier = pltpu.get_barrier_semaphore()
    for target in peers:
        pl.semaphore_signal(barrier, inc=1, device_id=target, device_id_type=MESH)

    sections = {
        t: Section(
            w_out_ref if t == OUT else w_in_ref.at[:, t * WIDTH : (t + 1) * WIDTH],
            wall, t, at, wsend.at[t], wrecv.at[t], wlocal.at[t],
        )
        for t in range(5)
    }
    column = lambda i: pl.ds(pl.multiple_of((2 * i + c) * ROWS, ROWS), ROWS)
    cring = Ring(
        cot_t,
        lambda i: cots.at[:, column(i)],
        lambda i, h: cots.at[h * 512 : h * 512 + 512, column(i)],
        y, lambda i: device(x, i, z, c), other, csend, crecv,
    )
    cown = pltpu.make_async_copy(cot_t, cots.at[:, column(y)], clocal)
    orders = [(2, 1, 0), (0, 1, 2), (2, 1, 0), (0, 1, 2)]
    swaps = [Swap(held.at[i], landed.at[i], at, orders[i], mask_ref, ssend.at[i], srecv.at[i]) for i in range(4)]

    pl.semaphore_wait(barrier, len(peers))
    sections[QUERIES].fetch()
    for copy in loads:
        copy.wait()
    held[0, 0] = actions[FIRST : FIRST + 16]
    held[1, 0] = actions[FIRST + 16 : LAST]
    held[2, 0] = actions[LAST:]
    held[3, 0] = cot[LAST:]
    swaps[0].start()
    swaps[1].start()
    sections[KEYS].fetch()
    sections[VALUES].fetch()
    sections[GATES].fetch()

    for r in range(0, ROWS, CHUNK):
        n, inverse = normalize(actions[r : r + CHUNK].astype(F32))
        normed_in[r : r + CHUNK] = n
        inverse_in[r : r + CHUNK] = inverse
        normed[r : r + CHUNK] = (n * gain[...]).astype(BF16)
    cot_t[...] = cot[...].astype(F32).T.astype(BF16)
    cown.start()

    row = lax.broadcasted_iota(jnp.int32, (ROWS, ROWS), 0)
    col = lax.broadcasted_iota(jnp.int32, (ROWS, ROWS), 1)
    begin = jnp.zeros((ROWS, ROWS), jnp.int32)
    end = jnp.zeros((), jnp.int32)
    for k in range(7):
        end = end + lengths_ref[0, 0, k]
        begin = begin + jnp.where(row >= end, lengths_ref[0, 0, k], 0)
    begin = jnp.where(row >= FIRST, FIRST, begin)
    begin = jnp.where(row >= LAST, LAST, begin)
    visible = (col >= begin) & (col <= row)

    def project(t):
        for l in range(0, WIDTH, LANES):
            hidden = dot(normed[...], wall[t, :, l : l + LANES])
            value, slope = silu_parts(hidden)
            active[t, :, l : l + LANES] = value.astype(BF16)
            slopes[t, :, l : l + LANES] = slope

    def small(t, rows, first, count):
        for l in range(0, WIDTH, LANES):
            hidden = dot(rows, wall[t, :, l : l + LANES])
            far_active[t, first : first + count, l : l + LANES] = silu_parts(hidden)[0].astype(BF16)

    def head(h):
        return slice(h * HEAD_DIM, (h + 1) * HEAD_DIM)

    sections[QUERIES].spread()
    sections[KEYS].spread()
    sections[KEYS].start()
    sections[VALUES].start()
    swaps[1].turn(0)
    sections[VALUES].spread()
    sections[QUERIES].start()
    sections[QUERIES].across()
    swaps[0].turn(0)
    sections[KEYS].across()
    sections[GATES].spread()
    sections[GATES].start()
    sections[VALUES].across()
    sections[GATES].across()
    swaps[1].turn(1)
    sections[QUERIES].forward()
    swaps[0].turn(1)
    sections[GATES].forward()
    cring.start()
    sections[OUT].fetch()
    sections[QUERIES].collect()
    sections[KEYS].collect()
    sections[QUERIES].finish()
    sections[VALUES].collect()
    sections[KEYS].arrived()
    project(KEYS)
    sections[QUERIES].arrived()
    project(QUERIES)
    swaps[0].turn(2)
    swaps[1].turn(2)
    swaps[2].start()
    swaps[3].start()
    far_inputs = jnp.concatenate([held[0, 3], held[1, 3]], axis=0).astype(F32)
    far_normed[:MOST] = (normalize(far_inputs)[0] * gain[...]).astype(BF16)
    small(KEYS, far_normed[:MOST], 0, MOST)
    sections[GATES].finish()
    sections[VALUES].arrived()
    project(VALUES)
    small(VALUES, far_normed[:MOST], 0, MOST)
    sections[GATES].collect()
    cring.forward()

    far_slopes = []
    for h in range(HEADS):
        q, k, v = active[QUERIES, :, head(h)], active[KEYS, :, head(h)], active[VALUES, :, head(h)]
        value, slope = silu_parts(dot_nt(q, k) * SCALE)
        weight = (jnp.where(visible, value, 0.0) / MOST).astype(BF16)
        weights[h] = weight
        score_slopes[h] = jnp.where(visible, slope, 0.0) * BACK
        value, slope = silu_parts(dot_nt(q[LAST:], far_active[KEYS, :MOST, head(h)]) * SCALE)
        far_slopes.append(slope * BACK)
        far_part = dot((value / MOST).astype(BF16), far_active[VALUES, :MOST, head(h)])
        local_part = dot(weight, v)
        attended[:LAST, head(h)] = local_part[:LAST]
        attended[LAST:, head(h)] = local_part[LAST:] + far_part

    sections[GATES].arrived()
    project(GATES)
    for r in range(0, ROWS, CHUNK):
        n, inverse = normalize(attended[r : r + CHUNK])
        normed_out[r : r + CHUNK] = n
        inverse_out[r : r + CHUNK] = inverse
        mix = (n * active[GATES, r : r + CHUNK].astype(F32)).astype(BF16)
        for h in range(HEADS):
            mixed[h, r : r + CHUNK] = mix[:, head(h)]
    own_rows = pl.ds(pl.multiple_of(me * ROWS, ROWS), ROWS)
    spread = [
        remote(mixed.at[group[d]], all_mixed.at[own_rows], msend.at[d], mrecv.at[d], in_group[d]) for d in range(7)
    ]
    start_all(spread)
    all_mixed[own_rows] = mixed[me]
    swaps[3].turn(0)
    swaps[2].turn(0)
    sections[OUT].spread()
    sections[OUT].start()
    cring.finish()
    swaps[3].turn(1)
    swaps[2].turn(1)

    for copy in spread:
        copy.wait_recv()
    cown.wait()
    cring.arrived()
    xcopies = []
    for d in (2, 1, 3, 0):
        quarter = pl.ds(pl.multiple_of((x + d) % 4 * 256, 256), 256)
        product = dot(cots[quarter], all_mixed[...])
        if d:
            sums[quarter] = product.astype(BF16)
            copy = remote(sums.at[quarter], xbuf.at[d - 1], xsend.at[d - 1], xrecv.at[d - 1], in_x[d - 1])
            copy.start()
            xcopies.append(copy)
        else:
            total[...] = product

    sections[OUT].across()
    swaps[2].turn(2)
    swaps[3].turn(2)
    spill_inputs = held[2, 3].astype(F32)
    far_normed[MOST:] = (normalize(spill_inputs)[0] * gain[...]).astype(BF16)
    for t in (GATES, VALUES, QUERIES, KEYS):
        small(t, far_normed[MOST:], MOST, SPILL)
    rows16 = lax.broadcasted_iota(jnp.int32, (SPILL, SPILL), 0)
    cols16 = lax.broadcasted_iota(jnp.int32, (SPILL, SPILL), 1)
    causal = cols16 <= rows16
    near_weights, near_slopes, near_attended = [], [], []
    for h in range(HEADS):
        q = far_active[QUERIES, MOST:, head(h)]
        value, slope = silu_parts(dot_nt(q, active[KEYS, FIRST:LAST, head(h)]) * SCALE)
        weight = (value / MOST).astype(BF16)
        near_weights.append(weight)
        near_slopes.append(slope * BACK)
        value, _ = silu_parts(dot_nt(q, far_active[KEYS, MOST:, head(h)]) * SCALE)
        weight2 = (jnp.where(causal, value, 0.0) / MOST).astype(BF16)
        near_attended.append(
            dot(weight, active[VALUES, FIRST:LAST, head(h)]) + dot(weight2, far_active[VALUES, MOST:, head(h)])
        )
    for copy in xcopies:
        copy.wait_recv()
    part[...] = (
        total[...] + xbuf[0].astype(F32) + xbuf[1].astype(F32) + xbuf[2].astype(F32)
    ).astype(BF16)
    zcopies = [
        remote(part.at[pl.ds(pl.multiple_of((z + d + 1) % NZ * 16, 16), 16)], zbuf.at[d], zsend.at[d], zrecv.at[d], in_z[d])
        for d in range(NZ - 1)
    ]
    for d in (7, 6, 8, 5, 9, 4, 10, 3, 11, 2, 12, 1, 13, 0, 14):
        zcopies[d].start()

    sections[OUT].collect()
    sections[OUT].arrived()
    for l in range(0, WIDTH, LANES):
        grad_mix[:, l : l + LANES] = dot_nt(cot[...], wall[OUT, l : l + LANES])

    for r in range(0, ROWS, CHUNK):
        span = slice(r, r + CHUNK)
        grad = grad_mix[span]
        n = normed_out[span]
        grad_hidden[GATES, span] = (grad * n * slopes[GATES, span]).astype(BF16)
        grad_att[span] = norm_backward(
            grad * active[GATES, span].astype(F32), n, inverse_out[span]
        ).astype(BF16)

    mixed_rows = jnp.concatenate([mixed[h] for h in range(HEADS)], axis=1)
    for l in range(0, WIDTH, LANES):
        output[:, l : l + LANES] = (
            dot(mixed_rows, wall[OUT, :, l : l + LANES]) + actions[:, l : l + LANES].astype(F32)
        ).astype(BF16)
    stores = [
        pltpu.make_async_copy(output, output_hbm.at[0], store_sem.at[0]),
        pltpu.make_async_copy(grad_input, grad_hbm.at[0], store_sem.at[1]),
        pltpu.make_async_copy(weight_grad, weight_hbm, store_sem.at[2]),
    ]
    stores[0].start()
    near_grad = dot_nt(held[3, 3], wall[OUT])
    near_normed, near_inverse = normalize(jnp.concatenate(near_attended, axis=1))
    near_att = norm_backward(
        near_grad * far_active[GATES, MOST:].astype(F32), near_normed, near_inverse
    ).astype(BF16)

    for h in range(HEADS):
        q, k, v = active[QUERIES, :, head(h)], active[KEYS, :, head(h)], active[VALUES, :, head(h)]
        g = grad_att[:, head(h)]
        grad_s = (dot_nt(g, v) * score_slopes[h]).astype(BF16)
        far_s = (dot_nt(g[LAST:], far_active[VALUES, :MOST, head(h)]) * far_slopes[h]).astype(BF16)
        near_g = near_att[:, head(h)]
        near_s = (dot_nt(near_g, v[FIRST:LAST]) * near_slopes[h]).astype(BF16)
        grad_q = dot(grad_s, k)
        far_q = dot(far_s, far_active[KEYS, :MOST, head(h)])
        grad_k = dot_tn(grad_s, q)
        near_k = dot_tn(near_s, far_active[QUERIES, MOST:, head(h)])
        grad_v = dot_tn(weights[h], g)
        near_v = dot_tn(near_weights[h], near_g)
        slope = slopes[QUERIES, :, head(h)]
        grad_hidden[QUERIES, :LAST, head(h)] = (grad_q[:LAST] * slope[:LAST]).astype(BF16)
        grad_hidden[QUERIES, LAST:, head(h)] = ((grad_q[LAST:] + far_q) * slope[LAST:]).astype(BF16)
        for t, grad, extra in ((KEYS, grad_k, near_k), (VALUES, grad_v, near_v)):
            slope = slopes[t, :, head(h)]
            grad_hidden[t, :FIRST, head(h)] = (grad[:FIRST] * slope[:FIRST]).astype(BF16)
            grad_hidden[t, FIRST:LAST, head(h)] = ((grad[FIRST:LAST] + extra) * slope[FIRST:LAST]).astype(BF16)
            grad_hidden[t, LAST:, head(h)] = (grad[LAST:] * slope[LAST:]).astype(BF16)

    for copy in zcopies:
        copy.wait_recv()
    summed = part[pl.ds(pl.multiple_of(z * 16, 16), 16)].astype(F32)
    for d in range(NZ - 1):
        summed = summed + zbuf[d].astype(F32)
    final[...] = summed * (1.0 / 256.0)
    acopies = [remote(final, wide.at[me], asend.at[d], arecv.at[d], in_group[d]) for d in range(7)]
    start_all(acopies)
    wide[me] = final[...]

    for l in range(0, WIDTH, LANES):
        grad_mix[:, l : l + LANES] = (
            dot_nt(grad_hidden[0], wall[0, l : l + LANES])
            + dot_nt(grad_hidden[1], wall[1, l : l + LANES])
            + dot_nt(grad_hidden[2], wall[2, l : l + LANES])
            + dot_nt(grad_hidden[3], wall[3, l : l + LANES])
        ) * gain[:, l : l + LANES]
    for r in range(0, ROWS, CHUNK):
        span = slice(r, r + CHUNK)
        grad_input[span] = (
            cot[span].astype(F32) + norm_backward(grad_mix[span], normed_in[span], inverse_in[span])
        ).astype(BF16)

    stores[1].start()
    for section in sections.values():
        section.sent()
    cring.sent()
    for swap in swaps:
        swap.sent()
    for copy in spread + xcopies + zcopies:
        copy.wait_send()
    for copy in acopies:
        copy.wait_recv()
    for i in range(8):
        weight_grad[:, i * 128 : (i + 1) * 128] = wide[i]
    stores[2].start()
    for copy in acopies:
        copy.wait_send()
    for copy in stores:
        copy.wait()


def publish_kernel(*refs):
    sources, results, staged, load_sem, store_sem = refs[:3], refs[3:6], refs[6:9], refs[9], refs[10]
    loads = [pltpu.make_async_copy(sources[i], staged[i], load_sem.at[i]) for i in range(3)]
    stores = [pltpu.make_async_copy(staged[i], results[i], store_sem.at[i]) for i in range(3)]
    start_all(loads)
    for load, store in zip(loads, stores):
        load.wait()
        store.start()
    for store in stores:
        store.wait()


def per_device(actions, lengths, partner_mask, norm_gain, w_in, w_out, cotangent):
    hbm = pl.BlockSpec(memory_space=pl.ANY)
    dma = pltpu.SemaphoreType.DMA
    block = (ROWS, WIDTH)
    shapes = (
        jax.ShapeDtypeStruct((1, ROWS, WIDTH), BF16),
        jax.ShapeDtypeStruct((1, ROWS, WIDTH), BF16),
        jax.ShapeDtypeStruct((16, WIDTH), F32),
    )
    results = pl.pallas_call(
        layer_kernel,
        out_shape=shapes,
        in_specs=[hbm] * 7,
        out_specs=(hbm, hbm, hbm),
        scratch_shapes=[
            pltpu.SMEM((1, 1), jnp.int32),
            pltpu.SMEM((1, 1, 7), jnp.int32),
            pltpu.VMEM(block, BF16),
            pltpu.VMEM(block, BF16),
            pltpu.VMEM((16, WIDTH), F32),
            dma((3,)),
            pltpu.VMEM(block, BF16),
            pltpu.VMEM((1, WIDTH), F32),
            pltpu.VMEM(block, BF16),
            pltpu.VMEM((5, WIDTH, WIDTH), BF16),
            pltpu.VMEM((WIDTH, WIDTH), BF16),
            pltpu.VMEM((WIDTH, ROWS), BF16),
            pltpu.VMEM(block, BF16),
            pltpu.VMEM(block, F32),
            pltpu.VMEM((ROWS, 1), F32),
            pltpu.VMEM((4, ROWS, WIDTH), BF16),
            pltpu.VMEM((4, ROWS, WIDTH), F32),
            pltpu.VMEM((HEADS, ROWS, ROWS), BF16),
            pltpu.VMEM((HEADS, ROWS, ROWS), F32),
            pltpu.VMEM(block, F32),
            pltpu.VMEM(block, F32),
            pltpu.VMEM((ROWS, 1), F32),
            pltpu.VMEM((HEADS, ROWS, HEAD_DIM), BF16),
            pltpu.VMEM((MOST + SPILL, WIDTH), BF16),
            pltpu.VMEM((4, MOST + SPILL, WIDTH), BF16),
            pltpu.VMEM(block, BF16),
            pltpu.VMEM(block, F32),
            pltpu.VMEM((4, ROWS, WIDTH), BF16),
            pltpu.VMEM((4, 4, SPILL, WIDTH), BF16),
            pltpu.VMEM((4, 3, SPILL, WIDTH), BF16),
            pltpu.VMEM((WIDTH, 128), BF16),
            pltpu.VMEM((256, 128), F32),
            pltpu.VMEM((WIDTH, 128), BF16),
            pltpu.VMEM((3, 256, 128), BF16),
            pltpu.VMEM((256, 128), BF16),
            pltpu.VMEM((NZ - 1, 16, 128), BF16),
            pltpu.VMEM((16, 128), F32),
            pltpu.VMEM((8, 16, 128), F32),
            dma((5,)), dma((5, 42)), dma((5, 42)), dma((5,)), dma((9,)), dma((9,)), dma,
            dma((4, 3)), dma((4, 3)), dma((7,)), dma((7,)), dma((3,)), dma((3,)),
            dma((NZ - 1,)), dma((NZ - 1,)), dma((7,)), dma((7,)),
        ],
        compiler_params=pltpu.CompilerParams(
            collective_id=0, has_side_effects=True, vmem_limit_bytes=56 * 1024 * 1024
        ),
        name="layer",
    )(partner_mask, lengths, actions, norm_gain.reshape(1, WIDTH), w_in, w_out, cotangent)
    return pl.pallas_call(
        publish_kernel,
        out_shape=shapes,
        in_specs=[hbm, hbm, hbm],
        out_specs=(hbm, hbm, hbm),
        scratch_shapes=[pltpu.VMEM(shape.shape, shape.dtype) for shape in shapes] + [dma((3,)), dma((3,))],
        compiler_params=pltpu.CompilerParams(vmem_limit_bytes=60 * 1024 * 1024),
        name="publish",
    )(*results)


def solution(mesh):
    placed = (
        P("fsdp", "dp", None),
        P("fsdp", "dp", None),
        P("fsdp", "dp"),
        P(),
        P("fsdp", None),
        P("fsdp", None),
        P("fsdp", "dp", None),
    )
    return jax.shard_map(
        per_device,
        mesh=mesh,
        in_specs=placed,
        out_specs=(P("fsdp", "dp", None), P("fsdp", "dp", None), P("dp", None)),
        check_vma=False,
    )
```

```python
import jax
import jax.numpy as jnp
from jax import lax
from jax.experimental import pallas as pl
from jax.experimental.pallas import tpu as pltpu
from jax.sharding import PartitionSpec as P

HEADS = 8
HEAD_DIM = 128
SPILL = 16
MOST = 32
ROWS = 128
WIDTH = 1024
LAST = ROWS - SPILL
FIRST = LAST - MOST
NZ = 16
EPSILON = 1e-05
SCALE = HEAD_DIM ** (-0.5)
BACK = SCALE / MOST
MESH = pl.DeviceIdType.MESH
F32 = jnp.float32
BF16 = jnp.bfloat16
GATES, VALUES, QUERIES, KEYS, OUT = range(5)
HALF = WIDTH // 2
PLAN = {
    QUERIES: (64, [("x", 64, 16, 0, WIDTH)]),
    KEYS: (0, [("x", 0, 16, 0, WIDTH), ("z", 64, 16, 0, WIDTH)]),
    VALUES: (0, [("x", 0, 16, 0, WIDTH), ("z", 64, 16, 0, WIDTH)]),
    GATES: (64, [("x", 64, 16, 0, HALF), ("z", 64, 16, HALF, HALF)]),
    OUT: (0, [("x", 0, 16, 0, WIDTH), ("z", 64, 16, 0, WIDTH)]),
}
SEMAPHORES = 86
CHUNK = 32
LANES = 256


def device(x, y, z, c):
    return (x * NZ + z, y * 2 + c)


def remote(src, dst, send, recv, target):
    return pltpu.make_async_remote_copy(
        src_ref=src, dst_ref=dst, send_sem=send, recv_sem=recv, device_id=target, device_id_type=MESH
    )


def start_all(copies):
    for copy in copies:
        copy.start()


def dot(a, b):
    return jnp.dot(a, b, preferred_element_type=F32)


def dot_nt(a, b):
    return lax.dot_general(a, b, (((1,), (1,)), ((), ())), preferred_element_type=F32)


def dot_tn(a, b):
    return lax.dot_general(a, b, (((0,), (0,)), ((), ())), preferred_element_type=F32)


def normalize(values):
    centred = values - jnp.mean(values, axis=-1, keepdims=True)
    inverse = lax.rsqrt(jnp.mean(centred * centred, axis=-1, keepdims=True) + EPSILON)
    return (centred * inverse, inverse)


def norm_backward(grad, normed, inverse):
    return inverse * (
        grad
        - jnp.mean(grad, axis=-1, keepdims=True)
        - normed * jnp.mean(grad * normed, axis=-1, keepdims=True)
    )


def silu_parts(values):
    sigma = jax.nn.sigmoid(values)
    return values * sigma, sigma * (1.0 + values * (1.0 - sigma))


def await_received(ref, sem, target):
    remote(ref, ref, sem, sem, target).wait_recv()


def await_sent(ref, sem, target):
    remote(ref, ref, sem, sem, target).wait_send()


class Section:
    def __init__(self, src, wall, t, at, new):
        x, y, z, c = at
        direct, blocks = PLAN[t]
        other = device(x, y, z, 1 - c)
        sent = new()
        self.send, self.other, self.wall = sent, other, wall.at[t]
        self.rows_sent = 0

        def move(piece, target, recv, source=None):
            self.rows_sent += piece.shape[0] * piece.shape[1] // WIDTH
            return remote(piece if source is None else source, piece, sent, recv, target)

        def block(owner, first, count, column=0, columns=WIDTH):
            base = pl.multiple_of((2 * owner + c) * ROWS + first, 16)
            return wall.at[t, pl.ds(base, count), column : column + columns]

        ahead, behind, across = (y + 1) % 4, (y + 3) % 4, (y + 2) % 4
        to_ahead, to_behind = device(x, ahead, z, c), device(x, behind, z, c)
        self.own = pltpu.make_async_copy(src, block(y, 0, ROWS), new())
        self.core = new()
        self.to_core = move(block(y, 0, ROWS), other, self.core, src)
        self.first, self.forwards, self.cores, self.halves = [], [], [], []
        if direct:
            half = direct // 2
            piece = src.at[:direct]
            self.first = [
                move(block(y, 0, direct), to_ahead, new(), piece), move(block(y, 0, direct), to_behind, new(), piece)
            ]
            self.forwards = [
                move(block(behind, 0, half), to_ahead, new()), move(block(ahead, half, half), to_behind, new())
            ]
            self.cores = [
                move(block(behind, 0, direct), other, self.core), move(block(ahead, 0, direct), other, self.core)
            ]
            self.halves = [move(block(across, h * half, half), other, self.core) for h in range(2)]
        self.fetched, self.passed, self.spreads, self.late = {}, {}, {}, {}
        self.near, self.far, self.spread_sem = {1: new(), 3: new()}, new(), {d: new() for d in (1, 3, 2)}
        self.block_rows = sum(count * columns // WIDTH for _, _, count, _, columns in blocks)
        for d, source, to in ((1, behind, to_ahead), (3, ahead, to_behind)):
            self.fetched[d], self.passed[d] = [], []
            for axis, first, count, column, columns in blocks:
                first = first + (x if axis == "x" else z % 4) * count
                self.fetched[d].append(
                    move(
                        block(y, first, count, column, columns), to, self.near[d],
                        src.at[pl.ds(pl.multiple_of(first, 16), count), column : column + columns],
                    )
                )
                part = columns // 2
                start = column + (part if d == 3 else 0)
                self.passed[d].append(move(block(source, first, count, start, part), to, self.far))
        for d, source in ((1, behind), (3, ahead), (2, across)):
            self.spreads[d] = []
            sem = self.spread_sem[d]
            for axis, first, count, column, columns in blocks:
                first = first + (x if axis == "x" else z % 4) * count
                whole = block(source, first, count, column, columns)
                if axis == "x":
                    self.spreads[d] += [move(whole, device((x + e) % 4, y, z, c), sem) for e in (2, 1, 3)]
                else:
                    part = columns // 2
                    self.spreads[d] += [
                        move(block(source, first, count, column, part), device(x, y, (z + 2) % NZ, c), sem),
                        move(block(source, first, count, column + part, part), device(x, y, (z + NZ - 2) % NZ, c), sem),
                        move(whole, device(x, y, (z + 1) % NZ, c), sem),
                        move(whole, device(x, y, (z + NZ - 1) % NZ, c), sem),
                    ]
            self.late[d] = move(block(source, direct, ROWS - direct), other, self.core)

    def received(self, rows, sem):
        await_received(self.wall.at[:rows], sem, self.other)

    def fetch(self):
        start_all(self.fetched[1] + self.fetched[3])

    def start(self):
        start_all(self.first)
        self.to_core.start()
        self.own.start()

    def spread(self):
        for d in (1, 3):
            self.received(self.block_rows, self.near[d])
            start_all(self.passed[d])
            start_all(self.spreads[d])

    def across(self):
        self.received(self.block_rows, self.far)
        start_all(self.spreads[2])

    def collect(self):
        for d, late in self.late.items():
            self.received(3 * self.block_rows, self.spread_sem[d])
            late.start()

    def forward(self):
        for i, copy in enumerate(self.first):
            copy.wait_recv()
            self.forwards[i].start()
            self.cores[i].start()

    def finish(self):
        for forward, half in zip(self.forwards, self.halves):
            forward.wait_recv()
            half.start()

    def arrived(self):
        self.own.wait()
        self.received(4 * ROWS, self.core)

    def sent(self):
        await_sent(self.wall.at[: self.rows_sent], self.send, self.other)


class Ring:
    def __init__(self, own, cots, view, half, me, towards, other, new):
        ahead, behind, across = (me + 1) % 4, (me + 3) % 4, (me + 2) % 4
        self.cots, self.other = cots, other
        self.send = send = new()
        self.core = core = new()
        self.first = [
            remote(own, view(me), send, new(), towards(ahead)),
            remote(own, view(me), send, new(), towards(behind)),
            remote(own, view(me), send, core, other),
        ]
        self.behind = [
            remote(half(behind, 0), half(behind, 0), send, new(), towards(ahead)),
            remote(view(behind), view(behind), send, core, other),
        ]
        self.ahead = [
            remote(half(ahead, 1), half(ahead, 1), send, new(), towards(behind)),
            remote(view(ahead), view(ahead), send, core, other),
        ]
        self.across = [remote(half(across, h), half(across, h), send, core, other) for h in range(2)]

    def start(self):
        start_all(self.first)

    def forward(self):
        self.first[0].wait_recv()
        start_all(self.behind)
        self.first[1].wait_recv()
        start_all(self.ahead)

    def finish(self):
        self.behind[0].wait_recv()
        self.across[0].start()
        self.ahead[0].wait_recv()
        self.across[1].start()

    def arrived(self):
        await_received(self.cots.at[: 4 * ROWS], self.core, self.other)

    def sent(self):
        await_sent(self.cots.at[: 7 * ROWS], self.send, self.other)


class Swap:
    def __init__(self, held, landed, at, order, mask, send, new):
        x, y, z, c = at
        self.held, self.landed, self.order, self.mask = held, landed, order, mask
        self.copies = []
        for step, bit in enumerate(order):
            size = 1 << bit
            to = z + size - 2 * size * (z // size % 2)
            self.copies.append(
                remote(held.at[step], landed.at[step], send, new(), device(x, y, to, c))
            )

    def start(self):
        self.copies[0].start()

    def turn(self, step):
        self.copies[step].wait_recv()
        bit = jnp.full((SPILL, WIDTH), lax.shift_right_logical(self.mask[0, 0], self.order[step]) & 1, jnp.int32)
        chosen = jnp.where(bit == 1, self.landed[step].astype(F32), self.held[step].astype(F32))
        self.held[step + 1] = chosen.astype(BF16)
        if step < 2:
            self.copies[step + 1].start()


def layer_kernel(
    mask_hbm, lengths_hbm, actions_hbm, gain_hbm, w_in_ref, w_out_ref, cot_hbm,
    output, grad_input, weight_grad,
    mask_ref, lengths_ref,
    actions, gain, cot, wall, cots, cot_t, normed, normed_in, inverse_in,
    active, slopes, weights, score_slopes, attended, normed_out, inverse_out, mixed,
    far_normed, far_active, grad_att, grad_mix, grad_hidden,
    held, landed, all_mixed, total, sums, xbuf, part, zbuf, final, wide,
    sems,
):
    dp = lax.axis_index("dp")
    me = lax.axis_index("fsdp")
    x, y, z, c = dp // NZ, me // 2, dp % NZ, me % 2
    at = (x, y, z, c)
    other = device(x, y, z, 1 - c)
    group = [(me + d) % 8 for d in range(1, 8)]
    in_group = [(dp, i) for i in group]
    in_x = [device((x + d) % 4, y, z, c) for d in range(1, 4)]
    in_z = [device(x, y, (z + d) % NZ, c) for d in range(1, NZ)]
    peers = in_group + in_x + in_z

    used = [0]

    def new():
        used[0] += 1
        return sems.at[used[0] - 1]

    loads = [
        pltpu.make_async_copy(actions_hbm.at[0], actions, new()),
        pltpu.make_async_copy(cot_hbm.at[0], cot, new()),
        pltpu.make_async_copy(gain_hbm, gain, new()),
        pltpu.make_async_copy(mask_hbm, mask_ref, new()),
        pltpu.make_async_copy(lengths_hbm, lengths_ref, new()),
    ]
    start_all(loads)
    barrier = pltpu.get_barrier_semaphore()
    for target in peers:
        pl.semaphore_signal(barrier, inc=1, device_id=target, device_id_type=MESH)

    sections = {
        t: Section(
            w_out_ref if t == OUT else w_in_ref.at[:, t * WIDTH : (t + 1) * WIDTH],
            wall, t, at, new,
        )
        for t in range(5)
    }
    column = lambda i: pl.ds(pl.multiple_of((2 * i + c) * ROWS, ROWS), ROWS)
    cring = Ring(
        cot_t, cots,
        lambda i: cots.at[:, column(i)],
        lambda i, h: cots.at[h * 512 : h * 512 + 512, column(i)],
        y, lambda i: device(x, i, z, c), other, new,
    )
    cown = pltpu.make_async_copy(cot_t, cots.at[:, column(y)], new())
    orders = [(2, 1, 0), (0, 1, 2), (2, 1, 0), (0, 1, 2)]
    swap_send = new()
    swaps = [Swap(held.at[i], landed.at[i], at, orders[i], mask_ref, swap_send, new) for i in range(4)]

    pl.semaphore_wait(barrier, len(peers))
    sections[QUERIES].fetch()
    for copy in loads:
        copy.wait()
    held[0, 0] = actions[FIRST : FIRST + 16]
    held[1, 0] = actions[FIRST + 16 : LAST]
    held[2, 0] = actions[LAST:]
    held[3, 0] = cot[LAST:]
    swaps[0].start()
    swaps[1].start()
    sections[KEYS].fetch()
    sections[VALUES].fetch()
    sections[GATES].fetch()

    for r in range(0, ROWS, CHUNK):
        n, inverse = normalize(actions[r : r + CHUNK].astype(F32))
        normed_in[r : r + CHUNK] = n
        inverse_in[r : r + CHUNK] = inverse
        normed[r : r + CHUNK] = (n * gain[...]).astype(BF16)
    cot_t[...] = cot[...].astype(F32).T.astype(BF16)
    cown.start()

    row = lax.broadcasted_iota(jnp.int32, (ROWS, ROWS), 0)
    col = lax.broadcasted_iota(jnp.int32, (ROWS, ROWS), 1)
    begin = jnp.zeros((ROWS, ROWS), jnp.int32)
    end = jnp.zeros((), jnp.int32)
    for k in range(7):
        end = end + lengths_ref[0, 0, k]
        begin = begin + jnp.where(row >= end, lengths_ref[0, 0, k], 0)
    begin = jnp.where(row >= FIRST, FIRST, begin)
    begin = jnp.where(row >= LAST, LAST, begin)
    visible = (col >= begin) & (col <= row)

    def project(t, count=ROWS):
        for l in range(0, WIDTH, LANES):
            hidden = dot(normed[:count], wall[t, :, l : l + LANES])
            value, slope = silu_parts(hidden)
            active[t, :, l : l + LANES] = value[:ROWS].astype(BF16)
            slopes[t, :, l : l + LANES] = slope[:ROWS]
            if count > ROWS:
                far_active[t, :MOST, l : l + LANES] = value[ROWS:].astype(BF16)

    def small(t, rows, first, count):
        for l in range(0, WIDTH, LANES):
            hidden = dot(rows, wall[t, :, l : l + LANES])
            far_active[t, first : first + count, l : l + LANES] = silu_parts(hidden)[0].astype(BF16)

    def head(h):
        return slice(h * HEAD_DIM, (h + 1) * HEAD_DIM)

    sections[QUERIES].spread()
    sections[KEYS].spread()
    sections[KEYS].start()
    sections[VALUES].start()
    swaps[1].turn(0)
    sections[VALUES].spread()
    sections[QUERIES].start()
    sections[QUERIES].across()
    swaps[0].turn(0)
    sections[KEYS].across()
    sections[GATES].spread()
    sections[GATES].start()
    sections[VALUES].across()
    sections[GATES].across()
    swaps[1].turn(1)
    sections[QUERIES].forward()
    swaps[0].turn(1)
    sections[GATES].forward()
    cring.start()
    sections[OUT].fetch()
    sections[QUERIES].collect()
    sections[KEYS].collect()
    sections[QUERIES].finish()
    sections[VALUES].collect()
    sections[QUERIES].arrived()
    project(QUERIES)
    swaps[0].turn(2)
    swaps[1].turn(2)
    swaps[2].start()
    swaps[3].start()
    far_inputs = jnp.concatenate([held[0, 3], held[1, 3]], axis=0).astype(F32)
    normed[ROWS:] = (normalize(far_inputs)[0] * gain[...]).astype(BF16)
    sections[KEYS].arrived()
    project(KEYS, ROWS + MOST)
    sections[GATES].finish()
    sections[VALUES].arrived()
    project(VALUES, ROWS + MOST)
    sections[GATES].collect()

    far_slopes = []
    for h in range(HEADS):
        q, k, v = active[QUERIES, :, head(h)], active[KEYS, :, head(h)], active[VALUES, :, head(h)]
        value, slope = silu_parts(dot_nt(q, k) * SCALE)
        weight = (jnp.where(visible, value, 0.0) / MOST).astype(BF16)
        weights[h] = weight
        score_slopes[h] = jnp.where(visible, slope, 0.0) * BACK
        value, slope = silu_parts(dot_nt(q[LAST:], far_active[KEYS, :MOST, head(h)]) * SCALE)
        far_slopes.append(slope * BACK)
        far_part = dot((value / MOST).astype(BF16), far_active[VALUES, :MOST, head(h)])
        local_part = dot(weight, v)
        attended[:LAST, head(h)] = local_part[:LAST]
        attended[LAST:, head(h)] = local_part[LAST:] + far_part

    cring.forward()
    sections[GATES].arrived()
    project(GATES)
    for r in range(0, ROWS, CHUNK):
        n, inverse = normalize(attended[r : r + CHUNK])
        normed_out[r : r + CHUNK] = n
        inverse_out[r : r + CHUNK] = inverse
        mix = (n * active[GATES, r : r + CHUNK].astype(F32)).astype(BF16)
        for h in range(HEADS):
            mixed[h, r : r + CHUNK] = mix[:, head(h)]
    own_rows = pl.ds(pl.multiple_of(me * ROWS, ROWS), ROWS)
    msend, mrecv, xsend, xrecv, zsend, zrecv, asend, arecv = [new() for _ in range(8)]
    spread = [remote(mixed.at[group[d]], all_mixed.at[own_rows], msend, mrecv, in_group[d]) for d in range(7)]
    start_all(spread)
    all_mixed[own_rows] = mixed[me]
    swaps[3].turn(0)
    swaps[2].turn(0)
    sections[OUT].spread()
    sections[OUT].start()
    cring.finish()
    swaps[3].turn(1)
    swaps[2].turn(1)

    await_received(all_mixed.at[: 7 * ROWS], mrecv, other)
    cown.wait()
    cring.arrived()
    for d in (2, 1, 3, 0):
        quarter = pl.ds(pl.multiple_of((x + d) % 4 * 256, 256), 256)
        product = dot(cots[quarter], all_mixed[...])
        if d:
            sums[quarter] = product.astype(BF16)
            copy = remote(sums.at[quarter], xbuf.at[d - 1], xsend, xrecv, in_x[d - 1])
            copy.start()
        else:
            total[...] = product

    sections[OUT].across()
    swaps[2].turn(2)
    swaps[3].turn(2)
    spill_inputs = held[2, 3].astype(F32)
    far_normed[...] = (normalize(spill_inputs)[0] * gain[...]).astype(BF16)
    for t in (GATES, VALUES, QUERIES, KEYS):
        small(t, far_normed[...], MOST, SPILL)
    rows16 = lax.broadcasted_iota(jnp.int32, (SPILL, SPILL), 0)
    cols16 = lax.broadcasted_iota(jnp.int32, (SPILL, SPILL), 1)
    causal = cols16 <= rows16
    near_weights, near_slopes, near_attended = [], [], []
    for h in range(HEADS):
        q = far_active[QUERIES, MOST:, head(h)]
        value, slope = silu_parts(dot_nt(q, active[KEYS, FIRST:LAST, head(h)]) * SCALE)
        weight = (value / MOST).astype(BF16)
        near_weights.append(weight)
        near_slopes.append(slope * BACK)
        value, _ = silu_parts(dot_nt(q, far_active[KEYS, MOST:, head(h)]) * SCALE)
        weight2 = (jnp.where(causal, value, 0.0) / MOST).astype(BF16)
        near_attended.append(
            dot(weight, active[VALUES, FIRST:LAST, head(h)]) + dot(weight2, far_active[VALUES, MOST:, head(h)])
        )
    await_received(xbuf, xrecv, other)
    part[...] = (
        total[...] + xbuf[0].astype(F32) + xbuf[1].astype(F32) + xbuf[2].astype(F32)
    ).astype(BF16)
    zcopies = [
        remote(part.at[pl.ds(pl.multiple_of((z + d + 1) % NZ * 16, 16), 16)], zbuf.at[d], zsend, zrecv, in_z[d])
        for d in range(NZ - 1)
    ]
    for d in (7, 6, 8, 5, 9, 4, 10, 3, 11, 2, 12, 1, 13, 0, 14):
        zcopies[d].start()

    sections[OUT].collect()
    sections[OUT].arrived()
    for l in range(0, WIDTH, LANES):
        grad_mix[:, l : l + LANES] = dot_nt(cot[...], wall[OUT, l : l + LANES])

    for r in range(0, ROWS, CHUNK):
        span = slice(r, r + CHUNK)
        grad = grad_mix[span]
        n = normed_out[span]
        grad_hidden[GATES, span] = (grad * n * slopes[GATES, span]).astype(BF16)
        grad_att[span] = norm_backward(
            grad * active[GATES, span].astype(F32), n, inverse_out[span]
        ).astype(BF16)

    mixed_rows = jnp.concatenate([mixed[h] for h in range(HEADS)], axis=1)
    for l in range(0, WIDTH, LANES):
        output[0, :, l : l + LANES] = (
            dot(mixed_rows, wall[OUT, :, l : l + LANES]) + actions[:, l : l + LANES].astype(F32)
        ).astype(BF16)
    near_grad = dot_nt(held[3, 3], wall[OUT])
    near_normed, near_inverse = normalize(jnp.concatenate(near_attended, axis=1))
    near_att = norm_backward(
        near_grad * far_active[GATES, MOST:].astype(F32), near_normed, near_inverse
    ).astype(BF16)

    for h in range(HEADS):
        q, k, v = active[QUERIES, :, head(h)], active[KEYS, :, head(h)], active[VALUES, :, head(h)]
        g = grad_att[:, head(h)]
        grad_s = (dot_nt(g, v) * score_slopes[h]).astype(BF16)
        far_s = (dot_nt(g[LAST:], far_active[VALUES, :MOST, head(h)]) * far_slopes[h]).astype(BF16)
        near_g = near_att[:, head(h)]
        near_s = (dot_nt(near_g, v[FIRST:LAST]) * near_slopes[h]).astype(BF16)
        grad_q = dot(grad_s, k)
        far_q = dot(far_s, far_active[KEYS, :MOST, head(h)])
        grad_k = dot_tn(grad_s, q)
        near_k = dot_tn(near_s, far_active[QUERIES, MOST:, head(h)])
        grad_v = dot_tn(weights[h], g)
        near_v = dot_tn(near_weights[h], near_g)
        slope = slopes[QUERIES, :, head(h)]
        grad_hidden[QUERIES, :LAST, head(h)] = (grad_q[:LAST] * slope[:LAST]).astype(BF16)
        grad_hidden[QUERIES, LAST:, head(h)] = ((grad_q[LAST:] + far_q) * slope[LAST:]).astype(BF16)
        for t, grad, extra in ((KEYS, grad_k, near_k), (VALUES, grad_v, near_v)):
            slope = slopes[t, :, head(h)]
            grad_hidden[t, :FIRST, head(h)] = (grad[:FIRST] * slope[:FIRST]).astype(BF16)
            grad_hidden[t, FIRST:LAST, head(h)] = ((grad[FIRST:LAST] + extra) * slope[FIRST:LAST]).astype(BF16)
            grad_hidden[t, LAST:, head(h)] = (grad[LAST:] * slope[LAST:]).astype(BF16)

    await_received(zbuf, zrecv, other)
    summed = part[pl.ds(pl.multiple_of(z * 16, 16), 16)].astype(F32)
    for d in range(NZ - 1):
        summed = summed + zbuf[d].astype(F32)
    final[...] = summed * (1.0 / 256.0)
    acopies = [remote(final, wide.at[me], asend, arecv, in_group[d]) for d in range(7)]
    start_all(acopies)
    wide[me] = final[...]

    for l in range(0, WIDTH, LANES):
        grad_mix[:, l : l + LANES] = (
            dot_nt(grad_hidden[0], wall[0, l : l + LANES])
            + dot_nt(grad_hidden[1], wall[1, l : l + LANES])
            + dot_nt(grad_hidden[2], wall[2, l : l + LANES])
            + dot_nt(grad_hidden[3], wall[3, l : l + LANES])
        ) * gain[:, l : l + LANES]
    for r in range(0, ROWS, CHUNK):
        span = slice(r, r + CHUNK)
        grad_input[0, span] = (
            cot[span].astype(F32) + norm_backward(grad_mix[span], normed_in[span], inverse_in[span])
        ).astype(BF16)

    for section in sections.values():
        section.sent()
    cring.sent()
    await_sent(wall.at[OUT, : 12 * SPILL], swap_send, other)
    await_sent(all_mixed.at[: 7 * ROWS], msend, other)
    await_sent(xbuf, xsend, other)
    await_sent(zbuf, zsend, other)
    await_received(wide.at[:7], arecv, other)
    for i in range(8):
        weight_grad[:, i * 128 : (i + 1) * 128] = wide[i]
    await_sent(wide.at[:7], asend, other)


def publish_kernel(*refs):
    copies = [pltpu.make_async_copy(refs[i], refs[3 + i], refs[6].at[i]) for i in range(3)]
    start_all(copies)
    for copy in copies:
        copy.wait()


def per_device(actions, lengths, partner_mask, norm_gain, w_in, w_out, cotangent):
    hbm = pl.BlockSpec(memory_space=pltpu.HBM)
    vmem = pl.BlockSpec(memory_space=pltpu.VMEM)
    dma = pltpu.SemaphoreType.DMA
    block = (ROWS, WIDTH)
    shapes = (
        jax.ShapeDtypeStruct((1, ROWS, WIDTH), BF16),
        jax.ShapeDtypeStruct((1, ROWS, WIDTH), BF16),
        jax.ShapeDtypeStruct((16, WIDTH), F32),
    )
    results = pl.pallas_call(
        layer_kernel,
        out_shape=tuple(pltpu.VMEM(shape.shape, shape.dtype) for shape in shapes),
        in_specs=[hbm] * 7,
        out_specs=(vmem, vmem, vmem),
        scratch_shapes=[
            pltpu.SMEM((1, 1), jnp.int32),
            pltpu.SMEM((1, 1, 7), jnp.int32),

            pltpu.VMEM(block, BF16),
            pltpu.VMEM((1, WIDTH), F32),
            pltpu.VMEM(block, BF16),
            pltpu.VMEM((5, WIDTH, WIDTH), BF16),
            pltpu.VMEM((WIDTH, WIDTH), BF16),
            pltpu.VMEM((WIDTH, ROWS), BF16),
            pltpu.VMEM((ROWS + MOST, WIDTH), BF16),
            pltpu.VMEM(block, F32),
            pltpu.VMEM((ROWS, 1), F32),
            pltpu.VMEM((4, ROWS, WIDTH), BF16),
            pltpu.VMEM((4, ROWS, WIDTH), F32),
            pltpu.VMEM((HEADS, ROWS, ROWS), BF16),
            pltpu.VMEM((HEADS, ROWS, ROWS), F32),
            pltpu.VMEM(block, F32),
            pltpu.VMEM(block, F32),
            pltpu.VMEM((ROWS, 1), F32),
            pltpu.VMEM((HEADS, ROWS, HEAD_DIM), BF16),
            pltpu.VMEM((SPILL, WIDTH), BF16),
            pltpu.VMEM((4, MOST + SPILL, WIDTH), BF16),
            pltpu.VMEM(block, BF16),
            pltpu.VMEM(block, F32),
            pltpu.VMEM((4, ROWS, WIDTH), BF16),
            pltpu.VMEM((4, 4, SPILL, WIDTH), BF16),
            pltpu.VMEM((4, 3, SPILL, WIDTH), BF16),
            pltpu.VMEM((WIDTH, 128), BF16),
            pltpu.VMEM((256, 128), F32),
            pltpu.VMEM((WIDTH, 128), BF16),
            pltpu.VMEM((3, 256, 128), BF16),
            pltpu.VMEM((256, 128), BF16),
            pltpu.VMEM((NZ - 1, 16, 128), BF16),
            pltpu.VMEM((16, 128), F32),
            pltpu.VMEM((8, 16, 128), F32),
            dma((SEMAPHORES,)),
        ],
        compiler_params=pltpu.CompilerParams(
            collective_id=0, has_side_effects=True, vmem_limit_bytes=56 * 1024 * 1024
        ),
        name="layer",
    )(partner_mask, lengths, actions, norm_gain.reshape(1, WIDTH), w_in, w_out, cotangent)
    return pl.pallas_call(
        publish_kernel,
        out_shape=shapes,
        in_specs=[vmem, vmem, vmem],
        out_specs=(hbm, hbm, hbm),
        scratch_shapes=[dma((3,))],
        compiler_params=pltpu.CompilerParams(vmem_limit_bytes=16 * 1024 * 1024),
        name="publish",
    )(*results)


def solution(mesh):
    placed = (
        P("fsdp", "dp", None),
        P("fsdp", "dp", None),
        P("fsdp", "dp"),
        P(),
        P("fsdp", None),
        P("fsdp", None),
        P("fsdp", "dp", None),
    )
    return jax.shard_map(
        per_device,
        mesh=mesh,
        in_specs=placed,
        out_specs=(P("fsdp", "dp", None), P("fsdp", "dp", None), P("dp", None)),
        check_vma=False,
    )
```

```python
import jax
import jax.numpy as jnp
from jax import lax
from jax.experimental import pallas as pl
from jax.experimental.pallas import tpu as pltpu
from jax.sharding import PartitionSpec as P

HEADS = 8
HEAD_DIM = 128
SPILL = 16
MOST = 32
ROWS = 128
WIDTH = 1024
LAST = ROWS - SPILL
FIRST = LAST - MOST
NZ = 16
EPSILON = 1e-05
SCALE = HEAD_DIM ** (-0.5)
BACK = SCALE / MOST
MESH = pl.DeviceIdType.MESH
F32 = jnp.float32
BF16 = jnp.bfloat16
GATES, VALUES, QUERIES, KEYS, OUT = range(5)
HALF = WIDTH // 2
PLAN = {
    QUERIES: (128, []),
    KEYS: (0, [("x", 0, 16, 0, WIDTH), ("z", 64, 16, 0, WIDTH)]),
    VALUES: (0, [("x", 0, 16, 0, WIDTH), ("z", 64, 16, 0, WIDTH)]),
    GATES: (64, [("x", 64, 16, 0, HALF), ("z", 64, 16, HALF, HALF)]),
    OUT: (128, []),
}
SEMAPHORES = 78
CHUNK = 32
LANES = 256


def device(x, y, z, c):
    return (x * NZ + z, y * 2 + c)


def remote(src, dst, send, recv, target):
    return pltpu.make_async_remote_copy(
        src_ref=src, dst_ref=dst, send_sem=send, recv_sem=recv, device_id=target, device_id_type=MESH
    )


def start_all(copies):
    for copy in copies:
        copy.start()


def dot(a, b):
    return jnp.dot(a, b, preferred_element_type=F32)


def dot_nt(a, b):
    return lax.dot_general(a, b, (((1,), (1,)), ((), ())), preferred_element_type=F32)


def dot_tn(a, b):
    return lax.dot_general(a, b, (((0,), (0,)), ((), ())), preferred_element_type=F32)


def normalize(values):
    centred = values - jnp.mean(values, axis=-1, keepdims=True)
    inverse = lax.rsqrt(jnp.mean(centred * centred, axis=-1, keepdims=True) + EPSILON)
    return (centred * inverse, inverse)


def norm_backward(grad, normed, inverse):
    return inverse * (
        grad
        - jnp.mean(grad, axis=-1, keepdims=True)
        - normed * jnp.mean(grad * normed, axis=-1, keepdims=True)
    )


def silu_parts(values):
    sigma = jax.nn.sigmoid(values)
    return values * sigma, sigma * (1.0 + values * (1.0 - sigma))


def await_received(ref, sem, target):
    remote(ref, ref, sem, sem, target).wait_recv()


def await_sent(ref, sem, target):
    remote(ref, ref, sem, sem, target).wait_send()


class Section:
    def __init__(self, src, wall, t, at, new):
        x, y, z, c = at
        direct, blocks = PLAN[t]
        other = device(x, y, z, 1 - c)
        sent = new()
        self.send, self.other, self.wall = sent, other, wall.at[t]
        self.rows_sent = 0

        def move(piece, target, recv, source=None):
            self.rows_sent += piece.shape[0] * piece.shape[1] // WIDTH
            return remote(piece if source is None else source, piece, sent, recv, target)

        def block(owner, first, count, column=0, columns=WIDTH):
            base = pl.multiple_of((2 * owner + c) * ROWS + first, 16)
            return wall.at[t, pl.ds(base, count), column : column + columns]

        ahead, behind, across = (y + 1) % 4, (y + 3) % 4, (y + 2) % 4
        to_ahead, to_behind = device(x, ahead, z, c), device(x, behind, z, c)
        self.own = pltpu.make_async_copy(src, block(y, 0, ROWS), new())
        self.core = new()
        self.to_core = move(block(y, 0, ROWS), other, self.core, src)
        self.first, self.forwards, self.cores, self.halves = [], [], [], []
        if direct:
            half = direct // 2
            piece = src.at[:direct]
            self.first = [
                move(block(y, 0, direct), to_ahead, new(), piece), move(block(y, 0, direct), to_behind, new(), piece)
            ]
            self.forwards = [
                move(block(behind, 0, half), to_ahead, new()), move(block(ahead, half, half), to_behind, new())
            ]
            self.cores = [
                move(block(behind, 0, direct), other, self.core), move(block(ahead, 0, direct), other, self.core)
            ]
            self.halves = [move(block(across, h * half, half), other, self.core) for h in range(2)]
        self.fetched, self.passed, self.spreads, self.late = {}, {}, {}, {}
        if not blocks:
            return
        self.near, self.far, self.spread_sem = {1: new(), 3: new()}, new(), {d: new() for d in (1, 3, 2)}
        self.block_rows = sum(count * columns // WIDTH for _, _, count, _, columns in blocks)
        for d, source, to in ((1, behind, to_ahead), (3, ahead, to_behind)):
            self.fetched[d], self.passed[d] = [], []
            for axis, first, count, column, columns in blocks:
                first = first + (x if axis == "x" else z % 4) * count
                self.fetched[d].append(
                    move(
                        block(y, first, count, column, columns), to, self.near[d],
                        src.at[pl.ds(pl.multiple_of(first, 16), count), column : column + columns],
                    )
                )
                part = columns // 2
                start = column + (part if d == 3 else 0)
                self.passed[d].append(move(block(source, first, count, start, part), to, self.far))
        for d, source in ((1, behind), (3, ahead), (2, across)):
            self.spreads[d] = []
            sem = self.spread_sem[d]
            for axis, first, count, column, columns in blocks:
                first = first + (x if axis == "x" else z % 4) * count
                whole = block(source, first, count, column, columns)
                if axis == "x":
                    self.spreads[d] += [move(whole, device((x + e) % 4, y, z, c), sem) for e in (2, 1, 3)]
                else:
                    part = columns // 2
                    self.spreads[d] += [
                        move(block(source, first, count, column, part), device(x, y, (z + 2) % NZ, c), sem),
                        move(block(source, first, count, column + part, part), device(x, y, (z + NZ - 2) % NZ, c), sem),
                        move(whole, device(x, y, (z + 1) % NZ, c), sem),
                        move(whole, device(x, y, (z + NZ - 1) % NZ, c), sem),
                    ]
            self.late[d] = move(block(source, direct, ROWS - direct), other, self.core)

    def received(self, rows, sem):
        await_received(self.wall.at[:rows], sem, self.other)

    def fetch(self):
        start_all(self.fetched[1] + self.fetched[3])

    def start(self):
        start_all(self.first)
        self.to_core.start()
        self.own.start()

    def pass_on(self):
        for d in (1, 3):
            self.received(self.block_rows, self.near[d])
            start_all(self.passed[d])

    def spread(self):
        start_all(self.spreads[1] + self.spreads[3])

    def across(self):
        self.received(self.block_rows, self.far)
        start_all(self.spreads[2])

    def collect(self):
        for d, late in self.late.items():
            self.received(3 * self.block_rows, self.spread_sem[d])
            late.start()

    def forward(self):
        for i, copy in enumerate(self.first):
            copy.wait_recv()
            self.forwards[i].start()
            self.cores[i].start()

    def finish(self):
        for forward, half in zip(self.forwards, self.halves):
            forward.wait_recv()
            half.start()

    def arrived(self):
        self.own.wait()
        self.received(4 * ROWS, self.core)

    def sent(self):
        await_sent(self.wall.at[: self.rows_sent], self.send, self.other)


class Ring:
    def __init__(self, own, cots, view, half, me, towards, other, new):
        ahead, behind, across = (me + 1) % 4, (me + 3) % 4, (me + 2) % 4
        self.cots, self.other = cots, other
        self.send = send = new()
        self.core = core = new()
        self.first = [
            remote(own, view(me), send, new(), towards(ahead)),
            remote(own, view(me), send, new(), towards(behind)),
            remote(own, view(me), send, core, other),
        ]
        self.behind = [
            remote(half(behind, 0), half(behind, 0), send, new(), towards(ahead)),
            remote(view(behind), view(behind), send, core, other),
        ]
        self.ahead = [
            remote(half(ahead, 1), half(ahead, 1), send, new(), towards(behind)),
            remote(view(ahead), view(ahead), send, core, other),
        ]
        self.across = [remote(half(across, h), half(across, h), send, core, other) for h in range(2)]

    def start(self):
        start_all(self.first)

    def forward(self):
        self.first[0].wait_recv()
        start_all(self.behind)
        self.first[1].wait_recv()
        start_all(self.ahead)

    def finish(self):
        self.behind[0].wait_recv()
        self.across[0].start()
        self.ahead[0].wait_recv()
        self.across[1].start()

    def arrived(self):
        await_received(self.cots.at[: 4 * ROWS], self.core, self.other)

    def sent(self):
        await_sent(self.cots.at[: 7 * ROWS], self.send, self.other)


class Swap:
    def __init__(self, held, landed, at, order, mask, send, new):
        x, y, z, c = at
        self.held, self.landed, self.order, self.mask = held, landed, order, mask
        self.copies = []
        for step, bit in enumerate(order):
            size = 1 << bit
            to = z + size - 2 * size * (z // size % 2)
            self.copies.append(
                remote(held.at[step], landed.at[step], send, new(), device(x, y, to, c))
            )

    def start(self):
        self.copies[0].start()

    def turn(self, step):
        self.copies[step].wait_recv()
        bit = jnp.full((SPILL, WIDTH), lax.shift_right_logical(self.mask[0, 0], self.order[step]) & 1, jnp.int32)
        chosen = jnp.where(bit == 1, self.landed[step].astype(F32), self.held[step].astype(F32))
        self.held[step + 1] = chosen.astype(BF16)
        if step < 2:
            self.copies[step + 1].start()


def layer_kernel(
    mask_hbm, lengths_hbm, actions_hbm, gain_hbm, w_in_ref, w_out_ref, cot_hbm,
    output, grad_input, weight_grad,
    mask_ref, lengths_ref,
    actions, gain, cot, wall, cots, cot_t, normed, normed_in, inverse_in,
    active, slopes, weights, score_slopes, attended, normed_out, inverse_out, mixed,
    far_normed, far_active, grad_att, grad_mix, grad_hidden,
    held, landed, all_mixed, total, sums, ybuf, part, zbuf, final, wide,
    sems,
):
    dp = lax.axis_index("dp")
    fsdp = lax.axis_index("fsdp")
    x, y, z, c = dp // NZ, fsdp // 2, dp % NZ, fsdp % 2
    me = 2 * x + c
    at = (x, y, z, c)
    other = device(x, y, z, 1 - c)
    group = [(2 * x + c + d) % 8 for d in range(1, 8)]
    in_group = [device(i // 2, y, z, i % 2) for i in group]
    in_y = [device(x, (y + d) % 4, z, c) for d in range(1, 4)]
    in_z = [device(x, y, (z + d) % NZ, c) for d in range(1, NZ)]
    ends = [device(y, i // 2, z, i % 2) for i in range(8)]
    begins = [device(i // 2, x, z, i % 2) for i in range(8)]
    apart = [jnp.logical_or(x != y, i != me) for i in range(8)]

    used = [0]

    def new():
        used[0] += 1
        return sems.at[used[0] - 1]

    loads = [
        pltpu.make_async_copy(actions_hbm.at[0], actions, new()),
        pltpu.make_async_copy(cot_hbm.at[0], cot, new()),
        pltpu.make_async_copy(gain_hbm, gain, new()),
        pltpu.make_async_copy(mask_hbm, mask_ref, new()),
        pltpu.make_async_copy(lengths_hbm, lengths_ref, new()),
    ]
    barrier = pltpu.get_barrier_semaphore()
    for target in [in_z[d] for d in (7, 6, 8, 5, 9, 4, 10, 3, 11, 2, 12, 1, 13, 0, 14)] + in_group + in_y:
        pl.semaphore_signal(barrier, inc=1, device_id=target, device_id_type=MESH)
    for i in range(8):
        @pl.when(apart[i])
        def _():
            pl.semaphore_signal(barrier, inc=1, device_id=ends[i], device_id_type=MESH)
            pl.semaphore_signal(barrier, inc=1, device_id=begins[i], device_id_type=MESH)
    start_all(loads)

    sections = {
        t: Section(
            w_out_ref if t == OUT else w_in_ref.at[:, t * WIDTH : (t + 1) * WIDTH],
            wall, t, at, new,
        )
        for t in range(5)
    }
    column = lambda i: pl.ds(pl.multiple_of((2 * i + c) * ROWS, ROWS), ROWS)
    cring = Ring(
        cot_t, cots,
        lambda i: cots.at[:, column(i)],
        lambda i, h: cots.at[h * 512 : h * 512 + 512, column(i)],
        x, lambda i: device(i, y, z, c), other, new,
    )
    cown = pltpu.make_async_copy(cot_t, cots.at[:, column(x)], new())
    orders = [(2, 1, 0), (0, 1, 2), (2, 1, 0), (1, 2, 0)]
    swap_send = new()
    swaps = [Swap(held.at[i], landed.at[i], at, orders[i], mask_ref, swap_send, new) for i in range(4)]

    pl.semaphore_wait(barrier, 41 - 2 * (x == y).astype(jnp.int32))
    sections[KEYS].fetch()
    for copy in loads:
        copy.wait()
    held[0, 0] = actions[FIRST : FIRST + 16]
    held[1, 0] = actions[FIRST + 16 : LAST]
    held[2, 0] = actions[LAST:]
    held[3, 0] = cot[LAST:]
    swaps[0].start()
    swaps[1].start()
    sections[VALUES].fetch()
    sections[GATES].fetch()
    cot_t[...] = cot[...].astype(F32).T.astype(BF16)
    cring.start()
    cown.start()
    sections[KEYS].start()
    sections[VALUES].start()

    for r in range(0, ROWS, CHUNK):
        n, inverse = normalize(actions[r : r + CHUNK].astype(F32))
        normed_in[r : r + CHUNK] = n
        inverse_in[r : r + CHUNK] = inverse
        normed[r : r + CHUNK] = (n * gain[...]).astype(BF16)

    row = lax.broadcasted_iota(jnp.int32, (ROWS, ROWS), 0)
    col = lax.broadcasted_iota(jnp.int32, (ROWS, ROWS), 1)
    begin = jnp.zeros((ROWS, ROWS), jnp.int32)
    end = jnp.zeros((), jnp.int32)
    for k in range(7):
        end = end + lengths_ref[0, 0, k]
        begin = begin + jnp.where(row >= end, lengths_ref[0, 0, k], 0)
    begin = jnp.where(row >= FIRST, FIRST, begin)
    begin = jnp.where(row >= LAST, LAST, begin)
    visible = (col >= begin) & (col <= row)

    def project(t, count=ROWS):
        for l in range(0, WIDTH, LANES):
            hidden = dot(normed[:count], wall[t, :, l : l + LANES])
            value, slope = silu_parts(hidden)
            active[t, :, l : l + LANES] = value[:ROWS].astype(BF16)
            slopes[t, :, l : l + LANES] = slope[:ROWS]
            if count > ROWS:
                far_active[t, :MOST, l : l + LANES] = value[ROWS:].astype(BF16)

    def small(t, rows, first, count):
        for l in range(0, WIDTH, LANES):
            hidden = dot(rows, wall[t, :, l : l + LANES])
            far_active[t, first : first + count, l : l + LANES] = silu_parts(hidden)[0].astype(BF16)

    def head(h):
        return slice(h * HEAD_DIM, (h + 1) * HEAD_DIM)

    swaps[1].turn(0)
    sections[KEYS].pass_on()
    sections[QUERIES].start()
    sections[KEYS].spread()
    sections[VALUES].pass_on()
    sections[VALUES].spread()
    sections[GATES].pass_on()
    sections[GATES].start()
    swaps[0].turn(0)
    swaps[1].turn(1)
    sections[KEYS].across()
    sections[GATES].spread()
    sections[VALUES].across()
    sections[GATES].across()
    cring.forward()
    sections[QUERIES].forward()
    swaps[0].turn(1)
    sections[KEYS].collect()
    sections[GATES].forward()
    sections[OUT].start()
    sections[VALUES].collect()
    swaps[2].start()
    swaps[3].start()
    swaps[0].turn(2)
    swaps[1].turn(2)
    far_inputs = jnp.concatenate([held[0, 3], held[1, 3]], axis=0).astype(F32)
    normed[ROWS:] = (normalize(far_inputs)[0] * gain[...]).astype(BF16)
    sections[KEYS].arrived()
    project(KEYS, ROWS + MOST)
    sections[QUERIES].finish()
    sections[VALUES].arrived()
    project(VALUES, ROWS + MOST)
    sections[GATES].collect()
    sections[GATES].finish()
    sections[QUERIES].arrived()
    project(QUERIES)

    far_slopes = []
    for h in range(HEADS):
        q, k, v = active[QUERIES, :, head(h)], active[KEYS, :, head(h)], active[VALUES, :, head(h)]
        value, slope = silu_parts(dot_nt(q, k) * SCALE)
        weight = (jnp.where(visible, value, 0.0) / MOST).astype(BF16)
        weights[h] = weight
        score_slopes[h] = jnp.where(visible, slope, 0.0) * BACK
        value, slope = silu_parts(dot_nt(q[LAST:], far_active[KEYS, :MOST, head(h)]) * SCALE)
        far_slopes.append(slope * BACK)
        far_part = dot((value / MOST).astype(BF16), far_active[VALUES, :MOST, head(h)])
        local_part = dot(weight, v)
        attended[:LAST, head(h)] = local_part[:LAST]
        attended[LAST:, head(h)] = local_part[LAST:] + far_part

    sections[GATES].arrived()
    project(GATES)
    for r in range(0, ROWS, CHUNK):
        n, inverse = normalize(attended[r : r + CHUNK])
        normed_out[r : r + CHUNK] = n
        inverse_out[r : r + CHUNK] = inverse
        mix = (n * active[GATES, r : r + CHUNK].astype(F32)).astype(BF16)
        for h in range(HEADS):
            mixed[h, r : r + CHUNK] = mix[:, head(h)]
    own_rows = pl.ds(pl.multiple_of(me * ROWS, ROWS), ROWS)
    msend, mrecv, ysend, yrecv, zsend, zrecv, asend, arecv = [new() for _ in range(8)]
    spread = [remote(mixed.at[group[d]], all_mixed.at[own_rows], msend, mrecv, in_group[d]) for d in range(7)]
    start_all(spread)
    all_mixed[own_rows] = mixed[me]
    cring.finish()
    sections[OUT].forward()
    swaps[2].turn(0)
    swaps[3].turn(0)

    await_received(all_mixed.at[: 7 * ROWS], mrecv, other)
    cown.wait()
    cring.arrived()
    for d in (2, 1, 3, 0):
        quarter = pl.ds(pl.multiple_of((y + d) % 4 * 256, 256), 256)
        product = dot(cots[quarter], all_mixed[...])
        if d:
            sums[quarter] = product.astype(BF16)
            copy = remote(sums.at[quarter], ybuf.at[d - 1], ysend, yrecv, in_y[d - 1])
            copy.start()
        else:
            total[...] = product

    swaps[2].turn(1)
    swaps[3].turn(1)
    sections[OUT].finish()
    sections[OUT].arrived()
    for l in range(0, WIDTH, LANES):
        grad_mix[:, l : l + LANES] = dot_nt(cot[...], wall[OUT, l : l + LANES])

    for r in range(0, ROWS, CHUNK):
        span = slice(r, r + CHUNK)
        grad = grad_mix[span]
        n = normed_out[span]
        grad_hidden[GATES, span] = (grad * n * slopes[GATES, span]).astype(BF16)
        grad_att[span] = norm_backward(
            grad * active[GATES, span].astype(F32), n, inverse_out[span]
        ).astype(BF16)

    mixed_rows = jnp.concatenate([mixed[h] for h in range(HEADS)], axis=1)
    for l in range(0, WIDTH, LANES):
        output[0, :, l : l + LANES] = (
            dot(mixed_rows, wall[OUT, :, l : l + LANES]) + actions[:, l : l + LANES].astype(F32)
        ).astype(BF16)
    await_received(ybuf, yrecv, other)
    part[...] = (
        total[...] + ybuf[0].astype(F32) + ybuf[1].astype(F32) + ybuf[2].astype(F32)
    ).astype(BF16)
    zcopies = [
        remote(part.at[pl.ds(pl.multiple_of((z + d + 1) % NZ * 16, 16), 16)], zbuf.at[d], zsend, zrecv, in_z[d])
        for d in range(NZ - 1)
    ]
    for d in (7, 6, 8, 5, 9, 4, 10, 3, 11, 2, 12, 1, 13, 0, 14):
        zcopies[d].start()

    swaps[2].turn(2)
    swaps[3].turn(2)
    spill_inputs = held[2, 3].astype(F32)
    far_normed[...] = (normalize(spill_inputs)[0] * gain[...]).astype(BF16)
    for t in (GATES, VALUES, QUERIES, KEYS):
        small(t, far_normed[...], MOST, SPILL)
    rows16 = lax.broadcasted_iota(jnp.int32, (SPILL, SPILL), 0)
    cols16 = lax.broadcasted_iota(jnp.int32, (SPILL, SPILL), 1)
    causal = cols16 <= rows16
    near_weights, near_slopes, near_attended = [], [], []
    for h in range(HEADS):
        q = far_active[QUERIES, MOST:, head(h)]
        value, slope = silu_parts(dot_nt(q, active[KEYS, FIRST:LAST, head(h)]) * SCALE)
        weight = (value / MOST).astype(BF16)
        near_weights.append(weight)
        near_slopes.append(slope * BACK)
        value, _ = silu_parts(dot_nt(q, far_active[KEYS, MOST:, head(h)]) * SCALE)
        weight2 = (jnp.where(causal, value, 0.0) / MOST).astype(BF16)
        near_attended.append(
            dot(weight, active[VALUES, FIRST:LAST, head(h)]) + dot(weight2, far_active[VALUES, MOST:, head(h)])
        )
    near_grad = dot_nt(held[3, 3], wall[OUT])
    near_normed, near_inverse = normalize(jnp.concatenate(near_attended, axis=1))
    near_att = norm_backward(
        near_grad * far_active[GATES, MOST:].astype(F32), near_normed, near_inverse
    ).astype(BF16)

    for h in range(HEADS):
        q, k, v = active[QUERIES, :, head(h)], active[KEYS, :, head(h)], active[VALUES, :, head(h)]
        g = grad_att[:, head(h)]
        grad_s = (dot_nt(g, v) * score_slopes[h]).astype(BF16)
        far_s = (dot_nt(g[LAST:], far_active[VALUES, :MOST, head(h)]) * far_slopes[h]).astype(BF16)
        near_g = near_att[:, head(h)]
        near_s = (dot_nt(near_g, v[FIRST:LAST]) * near_slopes[h]).astype(BF16)
        grad_q = dot(grad_s, k)
        far_q = dot(far_s, far_active[KEYS, :MOST, head(h)])
        grad_k = dot_tn(grad_s, q)
        near_k = dot_tn(near_s, far_active[QUERIES, MOST:, head(h)])
        grad_v = dot_tn(weights[h], g)
        near_v = dot_tn(near_weights[h], near_g)
        slope = slopes[QUERIES, :, head(h)]
        grad_hidden[QUERIES, :LAST, head(h)] = (grad_q[:LAST] * slope[:LAST]).astype(BF16)
        grad_hidden[QUERIES, LAST:, head(h)] = ((grad_q[LAST:] + far_q) * slope[LAST:]).astype(BF16)
        for t, grad, extra in ((KEYS, grad_k, near_k), (VALUES, grad_v, near_v)):
            slope = slopes[t, :, head(h)]
            grad_hidden[t, :FIRST, head(h)] = (grad[:FIRST] * slope[:FIRST]).astype(BF16)
            grad_hidden[t, FIRST:LAST, head(h)] = ((grad[FIRST:LAST] + extra) * slope[FIRST:LAST]).astype(BF16)
            grad_hidden[t, LAST:, head(h)] = (grad[LAST:] * slope[LAST:]).astype(BF16)

    await_received(zbuf, zrecv, other)
    summed = part[pl.ds(pl.multiple_of(z * 16, 16), 16)].astype(F32)
    for d in range(NZ - 1):
        summed = summed + zbuf[d].astype(F32)
    final[...] = summed * (1.0 / 256.0)
    for i in range(8):
        copy = remote(final, wide.at[me], asend, arecv, ends[i])

        @pl.when(apart[i])
        def _():
            copy.start()

    @pl.when(x == y)
    def _():
        wide[me] = final[...]


    for l in range(0, WIDTH, LANES):
        grad_mix[:, l : l + LANES] = (
            dot_nt(grad_hidden[0], wall[0, l : l + LANES])
            + dot_nt(grad_hidden[1], wall[1, l : l + LANES])
            + dot_nt(grad_hidden[2], wall[2, l : l + LANES])
            + dot_nt(grad_hidden[3], wall[3, l : l + LANES])
        ) * gain[:, l : l + LANES]
    for r in range(0, ROWS, CHUNK):
        span = slice(r, r + CHUNK)
        grad_input[0, span] = (
            cot[span].astype(F32) + norm_backward(grad_mix[span], normed_in[span], inverse_in[span])
        ).astype(BF16)

    for section in sections.values():
        section.sent()
    cring.sent()
    await_sent(wall.at[OUT, : 12 * SPILL], swap_send, other)
    await_sent(all_mixed.at[: 7 * ROWS], msend, other)
    await_sent(ybuf, ysend, other)
    await_sent(zbuf, zsend, other)
    @pl.when(x == y)
    def _():
        await_received(wide.at[:7], arecv, other)

    @pl.when(x != y)
    def _():
        await_received(wide, arecv, other)

    for i in range(8):
        weight_grad[:, i * 128 : (i + 1) * 128] = wide[i]

    @pl.when(x == y)
    def _():
        await_sent(wide.at[:7], asend, other)

    @pl.when(x != y)
    def _():
        await_sent(wide, asend, other)


def publish_kernel(*refs):
    copies = [pltpu.make_async_copy(refs[i], refs[3 + i], refs[6].at[i]) for i in range(3)]
    start_all(copies)
    for copy in copies:
        copy.wait()


def per_device(actions, lengths, partner_mask, norm_gain, w_in, w_out, cotangent):
    hbm = pl.BlockSpec(memory_space=pltpu.HBM)
    vmem = pl.BlockSpec(memory_space=pltpu.VMEM)
    dma = pltpu.SemaphoreType.DMA
    block = (ROWS, WIDTH)
    shapes = (
        jax.ShapeDtypeStruct((1, ROWS, WIDTH), BF16),
        jax.ShapeDtypeStruct((1, ROWS, WIDTH), BF16),
        jax.ShapeDtypeStruct((16, WIDTH), F32),
    )
    results = pl.pallas_call(
        layer_kernel,
        out_shape=tuple(pltpu.VMEM(shape.shape, shape.dtype) for shape in shapes),
        in_specs=[hbm] * 7,
        out_specs=(vmem, vmem, vmem),
        scratch_shapes=[
            pltpu.SMEM((1, 1), jnp.int32),
            pltpu.SMEM((1, 1, 7), jnp.int32),

            pltpu.VMEM(block, BF16),
            pltpu.VMEM((1, WIDTH), F32),
            pltpu.VMEM(block, BF16),
            pltpu.VMEM((5, WIDTH, WIDTH), BF16),
            pltpu.VMEM((WIDTH, WIDTH), BF16),
            pltpu.VMEM((WIDTH, ROWS), BF16),
            pltpu.VMEM((ROWS + MOST, WIDTH), BF16),
            pltpu.VMEM(block, F32),
            pltpu.VMEM((ROWS, 1), F32),
            pltpu.VMEM((4, ROWS, WIDTH), BF16),
            pltpu.VMEM((4, ROWS, WIDTH), F32),
            pltpu.VMEM((HEADS, ROWS, ROWS), BF16),
            pltpu.VMEM((HEADS, ROWS, ROWS), F32),
            pltpu.VMEM(block, F32),
            pltpu.VMEM(block, F32),
            pltpu.VMEM((ROWS, 1), F32),
            pltpu.VMEM((HEADS, ROWS, HEAD_DIM), BF16),
            pltpu.VMEM((SPILL, WIDTH), BF16),
            pltpu.VMEM((4, MOST + SPILL, WIDTH), BF16),
            pltpu.VMEM(block, BF16),
            pltpu.VMEM(block, F32),
            pltpu.VMEM((4, ROWS, WIDTH), BF16),
            pltpu.VMEM((4, 4, SPILL, WIDTH), BF16),
            pltpu.VMEM((4, 3, SPILL, WIDTH), BF16),
            pltpu.VMEM((WIDTH, 128), BF16),
            pltpu.VMEM((256, 128), F32),
            pltpu.VMEM((WIDTH, 128), BF16),
            pltpu.VMEM((3, 256, 128), BF16),
            pltpu.VMEM((256, 128), BF16),
            pltpu.VMEM((NZ - 1, 16, 128), BF16),
            pltpu.VMEM((16, 128), F32),
            pltpu.VMEM((8, 16, 128), F32),
            dma((SEMAPHORES,)),
        ],
        compiler_params=pltpu.CompilerParams(
            collective_id=0, has_side_effects=True, vmem_limit_bytes=56 * 1024 * 1024
        ),
        name="layer",
    )(partner_mask, lengths, actions, norm_gain.reshape(1, WIDTH), w_in, w_out, cotangent)
    return pl.pallas_call(
        publish_kernel,
        out_shape=shapes,
        in_specs=[vmem, vmem, vmem],
        out_specs=(hbm, hbm, hbm),
        scratch_shapes=[dma((3,))],
        compiler_params=pltpu.CompilerParams(vmem_limit_bytes=16 * 1024 * 1024),
        name="publish",
    )(*results)


def solution(mesh):
    placed = (
        P("fsdp", "dp", None),
        P("fsdp", "dp", None),
        P("fsdp", "dp"),
        P(),
        P("fsdp", None),
        P("fsdp", None),
        P("fsdp", "dp", None),
    )
    return jax.shard_map(
        per_device,
        mesh=mesh,
        in_specs=placed,
        out_specs=(P("fsdp", "dp", None), P("fsdp", "dp", None), P("dp", None)),
        check_vma=False,
    )
```

```python
import jax
import jax.numpy as jnp
from jax import lax
from jax.experimental import pallas as pl
from jax.experimental.pallas import tpu as pltpu
from jax.sharding import PartitionSpec as P

HEADS = 8
HEAD_DIM = 128
SPILL = 16
MOST = 32
ROWS = 128
WIDTH = 1024
LAST = ROWS - SPILL
FIRST = LAST - MOST
NZ = 16
EPSILON = 1e-05
SCALE = HEAD_DIM ** (-0.5)
BACK = SCALE / MOST
MESH = pl.DeviceIdType.MESH
F32 = jnp.float32
BF16 = jnp.bfloat16
GATES, VALUES, QUERIES, KEYS, OUT = range(5)
HALF = WIDTH // 2
PLAN = {
    VALUES: (128, []),
    KEYS: (0, [("x", 0, 16, 0, WIDTH), ("z", 64, 16, 0, WIDTH)]),
    QUERIES: (0, [("x", 0, 16, 0, WIDTH), ("z", 64, 16, 0, WIDTH)]),
    GATES: (64, [("x", 64, 16, 0, HALF), ("z", 64, 16, HALF, HALF)]),
    OUT: (128, []),
}
SEMAPHORES = 78
CHUNK = 32
LANES = 256


def device(x, y, z, c):
    return (x * NZ + z, y * 2 + c)


def remote(src, dst, send, recv, target):
    return pltpu.make_async_remote_copy(
        src_ref=src, dst_ref=dst, send_sem=send, recv_sem=recv, device_id=target, device_id_type=MESH
    )


def start_all(copies):
    for copy in copies:
        copy.start()


def dot(a, b):
    return jnp.dot(a, b, preferred_element_type=F32)


def dot_nt(a, b):
    return lax.dot_general(a, b, (((1,), (1,)), ((), ())), preferred_element_type=F32)


def dot_tn(a, b):
    return lax.dot_general(a, b, (((0,), (0,)), ((), ())), preferred_element_type=F32)


def normalize(values):
    centred = values - jnp.mean(values, axis=-1, keepdims=True)
    inverse = lax.rsqrt(jnp.mean(centred * centred, axis=-1, keepdims=True) + EPSILON)
    return (centred * inverse, inverse)


def norm_backward(grad, normed, inverse):
    return inverse * (
        grad
        - jnp.mean(grad, axis=-1, keepdims=True)
        - normed * jnp.mean(grad * normed, axis=-1, keepdims=True)
    )


def silu_parts(values):
    sigma = jax.nn.sigmoid(values)
    return values * sigma, sigma * (1.0 + values * (1.0 - sigma))


def await_received(ref, sem, target):
    remote(ref, ref, sem, sem, target).wait_recv()


def await_sent(ref, sem, target):
    remote(ref, ref, sem, sem, target).wait_send()


class Section:
    def __init__(self, src, wall, t, at, new):
        x, y, z, c = at
        direct, blocks = PLAN[t]
        other = device(x, y, z, 1 - c)
        sent = new()
        self.send, self.other, self.wall = sent, other, wall.at[t]
        self.rows_sent = 0

        def move(piece, target, recv, source=None):
            self.rows_sent += piece.shape[0] * piece.shape[1] // WIDTH
            return remote(piece if source is None else source, piece, sent, recv, target)

        def block(owner, first, count, column=0, columns=WIDTH):
            base = pl.multiple_of((2 * owner + c) * ROWS + first, 16)
            return wall.at[t, pl.ds(base, count), column : column + columns]

        ahead, behind, across = (y + 1) % 4, (y + 3) % 4, (y + 2) % 4
        to_ahead, to_behind = device(x, ahead, z, c), device(x, behind, z, c)
        self.own = pltpu.make_async_copy(src, block(y, 0, ROWS), new())
        self.core = new()
        self.to_core = move(block(y, 0, ROWS), other, self.core, src)
        self.first, self.forwards, self.cores, self.halves = [], [], [], []
        if direct:
            half = direct // 2
            piece = src.at[:direct]
            self.first = [
                move(block(y, 0, direct), to_ahead, new(), piece), move(block(y, 0, direct), to_behind, new(), piece)
            ]
            self.forwards = [
                move(block(behind, 0, half), to_ahead, new()), move(block(ahead, half, half), to_behind, new())
            ]
            self.cores = [
                move(block(behind, 0, direct), other, self.core), move(block(ahead, 0, direct), other, self.core)
            ]
            self.halves = [move(block(across, h * half, half), other, self.core) for h in range(2)]
        self.fetched, self.passed, self.spreads, self.late = {}, {}, {}, {}
        if not blocks:
            return
        self.near, self.far, self.spread_sem = {1: new(), 3: new()}, new(), {d: new() for d in (1, 3, 2)}
        self.block_rows = sum(count * columns // WIDTH for _, _, count, _, columns in blocks)
        for d, source, to in ((1, behind, to_ahead), (3, ahead, to_behind)):
            self.fetched[d], self.passed[d] = [], []
            for axis, first, count, column, columns in blocks:
                first = first + (x if axis == "x" else z % 4) * count
                self.fetched[d].append(
                    move(
                        block(y, first, count, column, columns), to, self.near[d],
                        src.at[pl.ds(pl.multiple_of(first, 16), count), column : column + columns],
                    )
                )
                part = columns // 2
                start = column + (part if d == 3 else 0)
                self.passed[d].append(move(block(source, first, count, start, part), to, self.far))
        for d, source in ((1, behind), (3, ahead), (2, across)):
            self.spreads[d] = []
            sem = self.spread_sem[d]
            for axis, first, count, column, columns in blocks:
                first = first + (x if axis == "x" else z % 4) * count
                whole = block(source, first, count, column, columns)
                if axis == "x":
                    self.spreads[d] += [move(whole, device((x + e) % 4, y, z, c), sem) for e in (2, 1, 3)]
                else:
                    part = columns // 2
                    self.spreads[d] += [
                        move(block(source, first, count, column, part), device(x, y, (z + 2) % NZ, c), sem),
                        move(block(source, first, count, column + part, part), device(x, y, (z + NZ - 2) % NZ, c), sem),
                        move(whole, device(x, y, (z + 1) % NZ, c), sem),
                        move(whole, device(x, y, (z + NZ - 1) % NZ, c), sem),
                    ]
            self.late[d] = move(block(source, direct, ROWS - direct), other, self.core)

    def received(self, rows, sem):
        await_received(self.wall.at[:rows], sem, self.other)

    def fetch(self):
        start_all(self.fetched[1] + self.fetched[3])

    def start(self):
        start_all(self.first)
        self.to_core.start()
        self.own.start()

    def pass_on(self):
        for d in (1, 3):
            self.received(self.block_rows, self.near[d])
            start_all(self.passed[d])

    def spread(self):
        start_all(self.spreads[1] + self.spreads[3])

    def across(self):
        self.received(self.block_rows, self.far)
        start_all(self.spreads[2])

    def collect(self):
        for d, late in self.late.items():
            self.received(3 * self.block_rows, self.spread_sem[d])
            late.start()

    def forward(self):
        for i, copy in enumerate(self.first):
            copy.wait_recv()
            self.forwards[i].start()
            self.cores[i].start()

    def finish(self):
        for forward, half in zip(self.forwards, self.halves):
            forward.wait_recv()
            half.start()

    def arrived(self):
        self.own.wait()
        self.received(4 * ROWS, self.core)

    def sent(self):
        await_sent(self.wall.at[: self.rows_sent], self.send, self.other)


class Ring:
    def __init__(self, own, cots, view, half, me, towards, other, new):
        ahead, behind, across = (me + 1) % 4, (me + 3) % 4, (me + 2) % 4
        self.cots, self.other = cots, other
        self.send = send = new()
        self.core = core = new()
        self.first = [
            remote(own, view(me), send, new(), towards(ahead)),
            remote(own, view(me), send, new(), towards(behind)),
            remote(own, view(me), send, core, other),
        ]
        self.behind = [
            remote(half(behind, 0), half(behind, 0), send, new(), towards(ahead)),
            remote(view(behind), view(behind), send, core, other),
        ]
        self.ahead = [
            remote(half(ahead, 1), half(ahead, 1), send, new(), towards(behind)),
            remote(view(ahead), view(ahead), send, core, other),
        ]
        self.across = [remote(half(across, h), half(across, h), send, core, other) for h in range(2)]

    def start(self):
        start_all(self.first)

    def forward(self):
        self.first[0].wait_recv()
        start_all(self.behind)
        self.first[1].wait_recv()
        start_all(self.ahead)

    def finish(self):
        self.behind[0].wait_recv()
        self.across[0].start()
        self.ahead[0].wait_recv()
        self.across[1].start()

    def arrived(self):
        await_received(self.cots.at[: 4 * ROWS], self.core, self.other)

    def sent(self):
        await_sent(self.cots.at[: 7 * ROWS], self.send, self.other)


class Swap:
    def __init__(self, held, landed, at, order, mask, send, new):
        x, y, z, c = at
        self.held, self.landed, self.order, self.mask = held, landed, order, mask
        self.copies = []
        for step, bit in enumerate(order):
            size = 1 << bit
            to = z + size - 2 * size * (z // size % 2)
            self.copies.append(
                remote(held.at[step], landed.at[step], send, new(), device(x, y, to, c))
            )

    def start(self):
        self.copies[0].start()

    def turn(self, step):
        self.copies[step].wait_recv()
        bit = jnp.full((SPILL, WIDTH), lax.shift_right_logical(self.mask[0, 0], self.order[step]) & 1, jnp.int32)
        chosen = jnp.where(bit == 1, self.landed[step].astype(F32), self.held[step].astype(F32))
        self.held[step + 1] = chosen.astype(BF16)
        if step < 2:
            self.copies[step + 1].start()


def layer_kernel(
    mask_hbm, lengths_hbm, actions_hbm, gain_hbm, w_in_ref, w_out_ref, cot_hbm,
    output, grad_input, weight_grad,
    mask_ref, lengths_ref,
    actions, gain, cot, wall, cots, cot_t, normed, normed_in, inverse_in,
    active, slopes, weights, score_slopes, attended, normed_out, inverse_out, mixed,
    far_normed, far_active, grad_att, grad_mix, grad_hidden,
    held, landed, all_mixed, total, sums, ybuf, part, zbuf, final, wide,
    sems,
):
    dp = lax.axis_index("dp")
    fsdp = lax.axis_index("fsdp")
    x, y, z, c = dp // NZ, fsdp // 2, dp % NZ, fsdp % 2
    me = 2 * x + c
    at = (x, y, z, c)
    other = device(x, y, z, 1 - c)
    group = [(2 * x + c + d) % 8 for d in range(1, 8)]
    in_group = [device(i // 2, y, z, i % 2) for i in group]
    in_y = [device(x, (y + d) % 4, z, c) for d in range(1, 4)]
    in_z = [device(x, y, (z + d) % NZ, c) for d in range(1, NZ)]
    ends = [device(y, i // 2, z, i % 2) for i in range(8)]
    begins = [device(i // 2, x, z, i % 2) for i in range(8)]
    apart = [jnp.logical_or(x != y, i != me) for i in range(8)]

    used = [0]

    def new():
        used[0] += 1
        return sems.at[used[0] - 1]

    loads = [
        pltpu.make_async_copy(actions_hbm.at[0], actions, new()),
        pltpu.make_async_copy(cot_hbm.at[0], cot, new()),
        pltpu.make_async_copy(gain_hbm, gain, new()),
        pltpu.make_async_copy(mask_hbm, mask_ref, new()),
        pltpu.make_async_copy(lengths_hbm, lengths_ref, new()),
    ]
    barrier = pltpu.get_barrier_semaphore()
    for target in [in_z[d] for d in (7, 6, 8, 5, 9, 4, 10, 3, 11, 2, 12, 1, 13, 0, 14)] + in_group + in_y:
        pl.semaphore_signal(barrier, inc=1, device_id=target, device_id_type=MESH)
    for i in range(8):
        @pl.when(apart[i])
        def _():
            pl.semaphore_signal(barrier, inc=1, device_id=ends[i], device_id_type=MESH)
            pl.semaphore_signal(barrier, inc=1, device_id=begins[i], device_id_type=MESH)
    start_all(loads)

    sections = {
        t: Section(
            w_out_ref if t == OUT else w_in_ref.at[:, t * WIDTH : (t + 1) * WIDTH],
            wall, t, at, new,
        )
        for t in range(5)
    }
    column = lambda i: pl.ds(pl.multiple_of((2 * i + c) * ROWS, ROWS), ROWS)
    cring = Ring(
        cot_t, cots,
        lambda i: cots.at[:, column(i)],
        lambda i, h: cots.at[h * 512 : h * 512 + 512, column(i)],
        x, lambda i: device(i, y, z, c), other, new,
    )
    cown = pltpu.make_async_copy(cot_t, cots.at[:, column(x)], new())
    orders = [(2, 1, 0), (0, 1, 2), (2, 1, 0), (1, 2, 0)]
    swap_send = new()
    swaps = [Swap(held.at[i], landed.at[i], at, orders[i], mask_ref, swap_send, new) for i in range(4)]

    pl.semaphore_wait(barrier, 41 - 2 * (x == y).astype(jnp.int32))
    sections[KEYS].fetch()
    for copy in loads:
        copy.wait()
    held[0, 0] = actions[FIRST : FIRST + 16]
    held[1, 0] = actions[FIRST + 16 : LAST]
    held[2, 0] = actions[LAST:]
    held[3, 0] = cot[LAST:]
    swaps[0].start()
    swaps[1].start()
    sections[QUERIES].fetch()
    sections[GATES].fetch()
    cot_t[...] = cot[...].astype(F32).T.astype(BF16)
    cring.start()
    cown.start()
    sections[KEYS].start()
    sections[QUERIES].start()

    for r in range(0, ROWS, CHUNK):
        n, inverse = normalize(actions[r : r + CHUNK].astype(F32))
        normed_in[r : r + CHUNK] = n
        inverse_in[r : r + CHUNK] = inverse
        normed[r : r + CHUNK] = (n * gain[...]).astype(BF16)

    row = lax.broadcasted_iota(jnp.int32, (ROWS, ROWS), 0)
    col = lax.broadcasted_iota(jnp.int32, (ROWS, ROWS), 1)
    begin = jnp.zeros((ROWS, ROWS), jnp.int32)
    end = jnp.zeros((), jnp.int32)
    for k in range(7):
        end = end + lengths_ref[0, 0, k]
        begin = begin + jnp.where(row >= end, lengths_ref[0, 0, k], 0)
    begin = jnp.where(row >= FIRST, FIRST, begin)
    begin = jnp.where(row >= LAST, LAST, begin)
    visible = (col >= begin) & (col <= row)

    def project(t, count=ROWS):
        for l in range(0, WIDTH, LANES):
            hidden = dot(normed[:count], wall[t, :, l : l + LANES])
            value, slope = silu_parts(hidden)
            active[t, :, l : l + LANES] = value[:ROWS].astype(BF16)
            slopes[t, :, l : l + LANES] = slope[:ROWS]
            if count > ROWS:
                far_active[t, :MOST, l : l + LANES] = value[ROWS:].astype(BF16)

    def small(t, rows, first, count):
        for l in range(0, WIDTH, LANES):
            hidden = dot(rows, wall[t, :, l : l + LANES])
            far_active[t, first : first + count, l : l + LANES] = silu_parts(hidden)[0].astype(BF16)

    def head(h):
        return slice(h * HEAD_DIM, (h + 1) * HEAD_DIM)

    swaps[1].turn(0)
    sections[KEYS].pass_on()
    sections[VALUES].start()
    sections[KEYS].spread()
    sections[QUERIES].pass_on()
    sections[QUERIES].spread()
    sections[GATES].pass_on()
    sections[GATES].start()
    swaps[0].turn(0)
    swaps[1].turn(1)
    sections[KEYS].across()
    sections[GATES].spread()
    sections[QUERIES].across()
    sections[GATES].across()
    cring.forward()
    sections[VALUES].forward()
    swaps[0].turn(1)
    sections[KEYS].collect()
    sections[GATES].forward()
    sections[OUT].start()
    sections[QUERIES].collect()
    swaps[2].start()
    swaps[3].start()
    swaps[0].turn(2)
    swaps[1].turn(2)
    far_inputs = jnp.concatenate([held[0, 3], held[1, 3]], axis=0).astype(F32)
    normed[ROWS:] = (normalize(far_inputs)[0] * gain[...]).astype(BF16)
    sections[VALUES].finish()
    sections[KEYS].arrived()
    project(KEYS, ROWS + MOST)
    sections[QUERIES].arrived()
    project(QUERIES)
    sections[GATES].collect()
    sections[GATES].finish()

    far_slopes, far_weights = [], []
    for h in range(HEADS):
        q, k = active[QUERIES, :, head(h)], active[KEYS, :, head(h)]
        value, slope = silu_parts(dot_nt(q, k) * SCALE)
        weights[h] = (jnp.where(visible, value, 0.0) / MOST).astype(BF16)
        score_slopes[h] = jnp.where(visible, slope, 0.0) * BACK
        value, slope = silu_parts(dot_nt(q[LAST:], far_active[KEYS, :MOST, head(h)]) * SCALE)
        far_slopes.append(slope * BACK)
        far_weights.append((value / MOST).astype(BF16))
    sections[VALUES].arrived()
    project(VALUES, ROWS + MOST)
    for h in range(HEADS):
        local_part = dot(weights[h], active[VALUES, :, head(h)])
        far_part = dot(far_weights[h], far_active[VALUES, :MOST, head(h)])
        attended[:LAST, head(h)] = local_part[:LAST]
        attended[LAST:, head(h)] = local_part[LAST:] + far_part

    sections[GATES].arrived()
    project(GATES)
    for r in range(0, ROWS, CHUNK):
        n, inverse = normalize(attended[r : r + CHUNK])
        normed_out[r : r + CHUNK] = n
        inverse_out[r : r + CHUNK] = inverse
        mix = (n * active[GATES, r : r + CHUNK].astype(F32)).astype(BF16)
        for h in range(HEADS):
            mixed[h, r : r + CHUNK] = mix[:, head(h)]
    own_rows = pl.ds(pl.multiple_of(me * ROWS, ROWS), ROWS)
    msend, mrecv, ysend, yrecv, zsend, zrecv, asend, arecv = [new() for _ in range(8)]
    spread = [remote(mixed.at[group[d]], all_mixed.at[own_rows], msend, mrecv, in_group[d]) for d in range(7)]
    start_all(spread)
    all_mixed[own_rows] = mixed[me]
    cring.finish()
    sections[OUT].forward()
    swaps[2].turn(0)
    swaps[3].turn(0)

    await_received(all_mixed.at[: 7 * ROWS], mrecv, other)
    cown.wait()
    cring.arrived()
    for d in (2, 1, 3, 0):
        quarter = pl.ds(pl.multiple_of((y + d) % 4 * 256, 256), 256)
        product = dot(cots[quarter], all_mixed[...])
        if d:
            sums[quarter] = product.astype(BF16)
            copy = remote(sums.at[quarter], ybuf.at[d - 1], ysend, yrecv, in_y[d - 1])
            copy.start()
        else:
            total[...] = product

    swaps[2].turn(1)
    swaps[3].turn(1)
    sections[OUT].finish()
    sections[OUT].arrived()
    for l in range(0, WIDTH, LANES):
        grad_mix[:, l : l + LANES] = dot_nt(cot[...], wall[OUT, l : l + LANES])

    for r in range(0, ROWS, CHUNK):
        span = slice(r, r + CHUNK)
        grad = grad_mix[span]
        n = normed_out[span]
        grad_hidden[GATES, span] = (grad * n * slopes[GATES, span]).astype(BF16)
        grad_att[span] = norm_backward(
            grad * active[GATES, span].astype(F32), n, inverse_out[span]
        ).astype(BF16)

    mixed_rows = jnp.concatenate([mixed[h] for h in range(HEADS)], axis=1)
    for l in range(0, WIDTH, LANES):
        output[0, :, l : l + LANES] = (
            dot(mixed_rows, wall[OUT, :, l : l + LANES]) + actions[:, l : l + LANES].astype(F32)
        ).astype(BF16)
    await_received(ybuf, yrecv, other)
    part[...] = (
        total[...] + ybuf[0].astype(F32) + ybuf[1].astype(F32) + ybuf[2].astype(F32)
    ).astype(BF16)
    zcopies = [
        remote(part.at[pl.ds(pl.multiple_of((z + d + 1) % NZ * 16, 16), 16)], zbuf.at[d], zsend, zrecv, in_z[d])
        for d in range(NZ - 1)
    ]
    for d in (7, 6, 8, 5, 9, 4, 10, 3, 11, 2, 12, 1, 13, 0, 14):
        zcopies[d].start()

    swaps[2].turn(2)
    swaps[3].turn(2)
    spill_inputs = held[2, 3].astype(F32)
    far_normed[...] = (normalize(spill_inputs)[0] * gain[...]).astype(BF16)
    for t in (GATES, VALUES, QUERIES, KEYS):
        small(t, far_normed[...], MOST, SPILL)
    rows16 = lax.broadcasted_iota(jnp.int32, (SPILL, SPILL), 0)
    cols16 = lax.broadcasted_iota(jnp.int32, (SPILL, SPILL), 1)
    causal = cols16 <= rows16
    near_weights, near_slopes, near_attended = [], [], []
    for h in range(HEADS):
        q = far_active[QUERIES, MOST:, head(h)]
        value, slope = silu_parts(dot_nt(q, active[KEYS, FIRST:LAST, head(h)]) * SCALE)
        weight = (value / MOST).astype(BF16)
        near_weights.append(weight)
        near_slopes.append(slope * BACK)
        value, _ = silu_parts(dot_nt(q, far_active[KEYS, MOST:, head(h)]) * SCALE)
        weight2 = (jnp.where(causal, value, 0.0) / MOST).astype(BF16)
        near_attended.append(
            dot(weight, active[VALUES, FIRST:LAST, head(h)]) + dot(weight2, far_active[VALUES, MOST:, head(h)])
        )
    near_grad = dot_nt(held[3, 3], wall[OUT])
    near_normed, near_inverse = normalize(jnp.concatenate(near_attended, axis=1))
    near_att = norm_backward(
        near_grad * far_active[GATES, MOST:].astype(F32), near_normed, near_inverse
    ).astype(BF16)

    for h in range(HEADS):
        q, k, v = active[QUERIES, :, head(h)], active[KEYS, :, head(h)], active[VALUES, :, head(h)]
        g = grad_att[:, head(h)]
        grad_s = (dot_nt(g, v) * score_slopes[h]).astype(BF16)
        far_s = (dot_nt(g[LAST:], far_active[VALUES, :MOST, head(h)]) * far_slopes[h]).astype(BF16)
        near_g = near_att[:, head(h)]
        near_s = (dot_nt(near_g, v[FIRST:LAST]) * near_slopes[h]).astype(BF16)
        grad_q = dot(grad_s, k)
        far_q = dot(far_s, far_active[KEYS, :MOST, head(h)])
        grad_k = dot_tn(grad_s, q)
        near_k = dot_tn(near_s, far_active[QUERIES, MOST:, head(h)])
        grad_v = dot_tn(weights[h], g)
        near_v = dot_tn(near_weights[h], near_g)
        slope = slopes[QUERIES, :, head(h)]
        grad_hidden[QUERIES, :LAST, head(h)] = (grad_q[:LAST] * slope[:LAST]).astype(BF16)
        grad_hidden[QUERIES, LAST:, head(h)] = ((grad_q[LAST:] + far_q) * slope[LAST:]).astype(BF16)
        for t, grad, extra in ((KEYS, grad_k, near_k), (VALUES, grad_v, near_v)):
            slope = slopes[t, :, head(h)]
            grad_hidden[t, :FIRST, head(h)] = (grad[:FIRST] * slope[:FIRST]).astype(BF16)
            grad_hidden[t, FIRST:LAST, head(h)] = ((grad[FIRST:LAST] + extra) * slope[FIRST:LAST]).astype(BF16)
            grad_hidden[t, LAST:, head(h)] = (grad[LAST:] * slope[LAST:]).astype(BF16)

    await_received(zbuf, zrecv, other)
    summed = part[pl.ds(pl.multiple_of(z * 16, 16), 16)].astype(F32)
    for d in range(NZ - 1):
        summed = summed + zbuf[d].astype(F32)
    final[...] = summed * (1.0 / 256.0)
    for i in range(8):
        copy = remote(final, wide.at[me], asend, arecv, ends[i])

        @pl.when(apart[i])
        def _():
            copy.start()

    @pl.when(x == y)
    def _():
        wide[me] = final[...]


    for l in range(0, WIDTH, LANES):
        grad_mix[:, l : l + LANES] = (
            dot_nt(grad_hidden[0], wall[0, l : l + LANES])
            + dot_nt(grad_hidden[1], wall[1, l : l + LANES])
            + dot_nt(grad_hidden[2], wall[2, l : l + LANES])
            + dot_nt(grad_hidden[3], wall[3, l : l + LANES])
        ) * gain[:, l : l + LANES]
    for r in range(0, ROWS, CHUNK):
        span = slice(r, r + CHUNK)
        grad_input[0, span] = (
            cot[span].astype(F32) + norm_backward(grad_mix[span], normed_in[span], inverse_in[span])
        ).astype(BF16)

    for section in sections.values():
        section.sent()
    cring.sent()
    await_sent(wall.at[OUT, : 12 * SPILL], swap_send, other)
    await_sent(all_mixed.at[: 7 * ROWS], msend, other)
    await_sent(ybuf, ysend, other)
    await_sent(zbuf, zsend, other)
    @pl.when(x == y)
    def _():
        await_received(wide.at[:7], arecv, other)

    @pl.when(x != y)
    def _():
        await_received(wide, arecv, other)

    for i in range(8):
        weight_grad[:, i * 128 : (i + 1) * 128] = wide[i]

    @pl.when(x == y)
    def _():
        await_sent(wide.at[:7], asend, other)

    @pl.when(x != y)
    def _():
        await_sent(wide, asend, other)


def publish_kernel(*refs):
    copies = [pltpu.make_async_copy(refs[i], refs[3 + i], refs[6].at[i]) for i in range(3)]
    start_all(copies)
    for copy in copies:
        copy.wait()


def per_device(actions, lengths, partner_mask, norm_gain, w_in, w_out, cotangent):
    hbm = pl.BlockSpec(memory_space=pltpu.HBM)
    vmem = pl.BlockSpec(memory_space=pltpu.VMEM)
    dma = pltpu.SemaphoreType.DMA
    block = (ROWS, WIDTH)
    shapes = (
        jax.ShapeDtypeStruct((1, ROWS, WIDTH), BF16),
        jax.ShapeDtypeStruct((1, ROWS, WIDTH), BF16),
        jax.ShapeDtypeStruct((16, WIDTH), F32),
    )
    results = pl.pallas_call(
        layer_kernel,
        out_shape=tuple(pltpu.VMEM(shape.shape, shape.dtype) for shape in shapes),
        in_specs=[hbm] * 7,
        out_specs=(vmem, vmem, vmem),
        scratch_shapes=[
            pltpu.SMEM((1, 1), jnp.int32),
            pltpu.SMEM((1, 1, 7), jnp.int32),

            pltpu.VMEM(block, BF16),
            pltpu.VMEM((1, WIDTH), F32),
            pltpu.VMEM(block, BF16),
            pltpu.VMEM((5, WIDTH, WIDTH), BF16),
            pltpu.VMEM((WIDTH, WIDTH), BF16),
            pltpu.VMEM((WIDTH, ROWS), BF16),
            pltpu.VMEM((ROWS + MOST, WIDTH), BF16),
            pltpu.VMEM(block, F32),
            pltpu.VMEM((ROWS, 1), F32),
            pltpu.VMEM((4, ROWS, WIDTH), BF16),
            pltpu.VMEM((4, ROWS, WIDTH), F32),
            pltpu.VMEM((HEADS, ROWS, ROWS), BF16),
            pltpu.VMEM((HEADS, ROWS, ROWS), F32),
            pltpu.VMEM(block, F32),
            pltpu.VMEM(block, F32),
            pltpu.VMEM((ROWS, 1), F32),
            pltpu.VMEM((HEADS, ROWS, HEAD_DIM), BF16),
            pltpu.VMEM((SPILL, WIDTH), BF16),
            pltpu.VMEM((4, MOST + SPILL, WIDTH), BF16),
            pltpu.VMEM(block, BF16),
            pltpu.VMEM(block, F32),
            pltpu.VMEM((4, ROWS, WIDTH), BF16),
            pltpu.VMEM((4, 4, SPILL, WIDTH), BF16),
            pltpu.VMEM((4, 3, SPILL, WIDTH), BF16),
            pltpu.VMEM((WIDTH, 128), BF16),
            pltpu.VMEM((256, 128), F32),
            pltpu.VMEM((WIDTH, 128), BF16),
            pltpu.VMEM((3, 256, 128), BF16),
            pltpu.VMEM((256, 128), BF16),
            pltpu.VMEM((NZ - 1, 16, 128), BF16),
            pltpu.VMEM((16, 128), F32),
            pltpu.VMEM((8, 16, 128), F32),
            dma((SEMAPHORES,)),
        ],
        compiler_params=pltpu.CompilerParams(
            collective_id=0, has_side_effects=True, vmem_limit_bytes=56 * 1024 * 1024
        ),
        name="layer",
    )(partner_mask, lengths, actions, norm_gain.reshape(1, WIDTH), w_in, w_out, cotangent)
    return pl.pallas_call(
        publish_kernel,
        out_shape=shapes,
        in_specs=[vmem, vmem, vmem],
        out_specs=(hbm, hbm, hbm),
        scratch_shapes=[dma((3,))],
        compiler_params=pltpu.CompilerParams(vmem_limit_bytes=16 * 1024 * 1024),
        name="publish",
    )(*results)


def solution(mesh):
    placed = (
        P("fsdp", "dp", None),
        P("fsdp", "dp", None),
        P("fsdp", "dp"),
        P(),
        P("fsdp", None),
        P("fsdp", None),
        P("fsdp", "dp", None),
    )
    return jax.shard_map(
        per_device,
        mesh=mesh,
        in_specs=placed,
        out_specs=(P("fsdp", "dp", None), P("fsdp", "dp", None), P("dp", None)),
        check_vma=False,
    )
```

```python
import jax
import jax.numpy as jnp
from jax import lax
from jax.experimental import pallas as pl
from jax.experimental.pallas import tpu as pltpu
from jax.sharding import PartitionSpec as P

HEADS = 8
HEAD_DIM = 128
SPILL = 16
MOST = 32
ROWS = 128
WIDTH = 1024
LAST = ROWS - SPILL
FIRST = LAST - MOST
NZ = 16
EPSILON = 1e-05
SCALE = HEAD_DIM ** (-0.5)
BACK = SCALE / MOST
MESH = pl.DeviceIdType.MESH
F32 = jnp.float32
BF16 = jnp.bfloat16
GATES, VALUES, QUERIES, KEYS, OUT = range(5)
HALF = WIDTH // 2
PLAN = {
    VALUES: (128, []),
    KEYS: (0, [("x", 0, 16, 0, WIDTH), ("z", 64, 16, 0, WIDTH)]),
    QUERIES: (0, [("x", 0, 16, 0, WIDTH), ("z", 64, 16, 0, WIDTH)]),
    GATES: (64, [("x", 64, 16, 0, HALF), ("z", 64, 16, HALF, HALF)]),
    OUT: (128, []),
}
SEMAPHORES = 78
CHUNK = 32
LANES = 256


def device(x, y, z, c):
    return (x * NZ + z, y * 2 + c)


def remote(src, dst, send, recv, target):
    return pltpu.make_async_remote_copy(
        src_ref=src, dst_ref=dst, send_sem=send, recv_sem=recv, device_id=target, device_id_type=MESH
    )


def start_all(copies):
    for copy in copies:
        copy.start()


def dot(a, b):
    return jnp.dot(a, b, preferred_element_type=F32)


def dot_nt(a, b):
    return lax.dot_general(a, b, (((1,), (1,)), ((), ())), preferred_element_type=F32)


def dot_tn(a, b):
    return lax.dot_general(a, b, (((0,), (0,)), ((), ())), preferred_element_type=F32)


def normalize(values):
    centred = values - jnp.mean(values, axis=-1, keepdims=True)
    inverse = lax.rsqrt(jnp.mean(centred * centred, axis=-1, keepdims=True) + EPSILON)
    return (centred * inverse, inverse)


def norm_backward(grad, normed, inverse):
    return inverse * (
        grad
        - jnp.mean(grad, axis=-1, keepdims=True)
        - normed * jnp.mean(grad * normed, axis=-1, keepdims=True)
    )


def silu_parts(values):
    sigma = jax.nn.sigmoid(values)
    return values * sigma, sigma * (1.0 + values * (1.0 - sigma))


def await_received(ref, sem, target):
    remote(ref, ref, sem, sem, target).wait_recv()


def await_sent(ref, sem, target):
    remote(ref, ref, sem, sem, target).wait_send()


class Section:
    def __init__(self, src, wall, t, at, new):
        x, y, z, c = at
        direct, blocks = PLAN[t]
        other = device(x, y, z, 1 - c)
        sent = new()
        self.send, self.other, self.wall = sent, other, wall.at[t]
        self.rows_sent = 0

        def move(piece, target, recv, source=None):
            self.rows_sent += piece.shape[0] * piece.shape[1] // WIDTH
            return remote(piece if source is None else source, piece, sent, recv, target)

        def block(owner, first, count, column=0, columns=WIDTH):
            base = pl.multiple_of((2 * owner + c) * ROWS + first, 16)
            return wall.at[t, pl.ds(base, count), column : column + columns]

        ahead, behind, across = (y + 1) % 4, (y + 3) % 4, (y + 2) % 4
        to_ahead, to_behind = device(x, ahead, z, c), device(x, behind, z, c)
        self.own = pltpu.make_async_copy(src, block(y, 0, ROWS), new())
        self.core = new()
        self.to_core = move(block(y, 0, ROWS), other, self.core, src)
        self.first, self.forwards, self.cores, self.halves = [], [], [], []
        if direct:
            half = direct // 2
            piece = src.at[:direct]
            self.first = [
                move(block(y, 0, direct), to_ahead, new(), piece), move(block(y, 0, direct), to_behind, new(), piece)
            ]
            self.forwards = [
                move(block(behind, 0, half), to_ahead, new()), move(block(ahead, half, half), to_behind, new())
            ]
            self.cores = [
                move(block(behind, 0, direct), other, self.core), move(block(ahead, 0, direct), other, self.core)
            ]
            self.halves = [move(block(across, h * half, half), other, self.core) for h in range(2)]
        self.fetched, self.passed, self.spreads, self.late = {}, {}, {}, {}
        if not blocks:
            return
        self.near, self.far, self.spread_sem = {1: new(), 3: new()}, new(), {d: new() for d in (1, 3, 2)}
        self.block_rows = sum(count * columns // WIDTH for _, _, count, _, columns in blocks)
        for d, source, to in ((1, behind, to_ahead), (3, ahead, to_behind)):
            self.fetched[d], self.passed[d] = [], []
            for axis, first, count, column, columns in blocks:
                first = first + (x if axis == "x" else z % 4) * count
                self.fetched[d].append(
                    move(
                        block(y, first, count, column, columns), to, self.near[d],
                        src.at[pl.ds(pl.multiple_of(first, 16), count), column : column + columns],
                    )
                )
                part = columns // 2
                start = column + (part if d == 3 else 0)
                self.passed[d].append(move(block(source, first, count, start, part), to, self.far))
        for d, source in ((1, behind), (3, ahead), (2, across)):
            self.spreads[d] = []
            sem = self.spread_sem[d]
            for axis, first, count, column, columns in blocks:
                first = first + (x if axis == "x" else z % 4) * count
                whole = block(source, first, count, column, columns)
                if axis == "x":
                    self.spreads[d] += [move(whole, device((x + e) % 4, y, z, c), sem) for e in (2, 1, 3)]
                else:
                    part = columns // 2
                    self.spreads[d] += [
                        move(block(source, first, count, column, part), device(x, y, (z + 2) % NZ, c), sem),
                        move(block(source, first, count, column + part, part), device(x, y, (z + NZ - 2) % NZ, c), sem),
                        move(whole, device(x, y, (z + 1) % NZ, c), sem),
                        move(whole, device(x, y, (z + NZ - 1) % NZ, c), sem),
                    ]
            self.late[d] = move(block(source, direct, ROWS - direct), other, self.core)

    def received(self, rows, sem):
        await_received(self.wall.at[:rows], sem, self.other)

    def fetch(self):
        start_all(self.fetched[1] + self.fetched[3])

    def start(self):
        start_all(self.first)
        self.to_core.start()
        self.own.start()

    def pass_on(self):
        for d in (1, 3):
            self.received(self.block_rows, self.near[d])
            start_all(self.passed[d])

    def spread(self):
        start_all(self.spreads[1] + self.spreads[3])

    def across(self):
        self.received(self.block_rows, self.far)
        start_all(self.spreads[2])

    def collect(self):
        for d, late in self.late.items():
            self.received(3 * self.block_rows, self.spread_sem[d])
            late.start()

    def forward(self):
        for i, copy in enumerate(self.first):
            copy.wait_recv()
            self.forwards[i].start()
            self.cores[i].start()

    def finish(self):
        for forward, half in zip(self.forwards, self.halves):
            forward.wait_recv()
            half.start()

    def arrived(self):
        self.own.wait()
        self.received(4 * ROWS, self.core)

    def sent(self):
        await_sent(self.wall.at[: self.rows_sent], self.send, self.other)


class Ring:
    def __init__(self, own, cots, view, half, me, towards, other, new):
        ahead, behind, across = (me + 1) % 4, (me + 3) % 4, (me + 2) % 4
        self.cots, self.other = cots, other
        self.send = send = new()
        self.core = core = new()
        self.first = [
            remote(own, view(me), send, new(), towards(ahead)),
            remote(own, view(me), send, new(), towards(behind)),
            remote(own, view(me), send, core, other),
        ]
        self.behind = [
            remote(half(behind, 0), half(behind, 0), send, new(), towards(ahead)),
            remote(view(behind), view(behind), send, core, other),
        ]
        self.ahead = [
            remote(half(ahead, 1), half(ahead, 1), send, new(), towards(behind)),
            remote(view(ahead), view(ahead), send, core, other),
        ]
        self.across = [remote(half(across, h), half(across, h), send, core, other) for h in range(2)]

    def start(self):
        start_all(self.first)

    def forward(self):
        self.first[0].wait_recv()
        start_all(self.behind)
        self.first[1].wait_recv()
        start_all(self.ahead)

    def finish(self):
        self.behind[0].wait_recv()
        self.across[0].start()
        self.ahead[0].wait_recv()
        self.across[1].start()

    def arrived(self):
        await_received(self.cots.at[: 4 * ROWS], self.core, self.other)

    def sent(self):
        await_sent(self.cots.at[: 7 * ROWS], self.send, self.other)


class Swap:
    def __init__(self, held, landed, at, order, mask, send, new):
        x, y, z, c = at
        self.held, self.landed, self.order, self.mask = held, landed, order, mask
        self.copies = []
        for step, bit in enumerate(order):
            size = 1 << bit
            to = z + size - 2 * size * (z // size % 2)
            self.copies.append(
                remote(held.at[step], landed.at[step], send, new(), device(x, y, to, c))
            )

    def start(self):
        self.copies[0].start()

    def turn(self, step):
        self.copies[step].wait_recv()
        bit = jnp.full((SPILL, WIDTH), lax.shift_right_logical(self.mask[0, 0], self.order[step]) & 1, jnp.int32)
        chosen = jnp.where(bit == 1, self.landed[step].astype(F32), self.held[step].astype(F32))
        self.held[step + 1] = chosen.astype(BF16)
        if step < 2:
            self.copies[step + 1].start()


def layer_kernel(
    mask_hbm, lengths_hbm, actions_hbm, gain_hbm, w_in_ref, w_out_ref, cot_hbm,
    output, grad_input, weight_grad,
    mask_ref, lengths_ref,
    actions, gain, cot, wall, cots, cot_t, normed, normed_in, inverse_in,
    active, slopes, weights, score_slopes, attended, normed_out, inverse_out, mixed,
    far_normed, far_active, grad_att, grad_mix, grad_hidden,
    held, landed, all_mixed, total, sums, ybuf, part, zbuf, final, wide,
    sems, vouch,
):
    dp = lax.axis_index("dp")
    fsdp = lax.axis_index("fsdp")
    x, y, z, c = dp // NZ, fsdp // 2, dp % NZ, fsdp % 2
    me = 2 * x + c
    at = (x, y, z, c)
    other = device(x, y, z, 1 - c)
    group = [(2 * x + c + d) % 8 for d in range(1, 8)]
    in_group = [device(i // 2, y, z, i % 2) for i in group]
    in_y = [device(x, (y + d) % 4, z, c) for d in range(1, 4)]
    in_z = [device(x, y, (z + d) % NZ, c) for d in range(1, NZ)]
    ends = [device(y, i // 2, z, i % 2) for i in range(8)]
    near_z = [device(x, y, (z + d) % NZ, c) for d in (1, 2, NZ - 1, NZ - 2)]
    across_z = device(x, y, z + 4 - 8 * (z // 4 % 2), c)
    apart = [jnp.logical_or(x != y, i != me) for i in range(8)]

    used = [0]

    def new():
        used[0] += 1
        return sems.at[used[0] - 1]

    loads = [
        pltpu.make_async_copy(actions_hbm.at[0], actions, new()),
        pltpu.make_async_copy(cot_hbm.at[0], cot, new()),
        pltpu.make_async_copy(gain_hbm, gain, new()),
        pltpu.make_async_copy(mask_hbm, mask_ref, new()),
        pltpu.make_async_copy(lengths_hbm, lengths_ref, new()),
    ]
    barrier = pltpu.get_barrier_semaphore()
    for target in near_z + [across_z] + in_group + in_y:
        pl.semaphore_signal(barrier, inc=1, device_id=target, device_id_type=MESH)
    start_all(loads)

    sections = {
        t: Section(
            w_out_ref if t == OUT else w_in_ref.at[:, t * WIDTH : (t + 1) * WIDTH],
            wall, t, at, new,
        )
        for t in range(5)
    }
    column = lambda i: pl.ds(pl.multiple_of((2 * i + c) * ROWS, ROWS), ROWS)
    cring = Ring(
        cot_t, cots,
        lambda i: cots.at[:, column(i)],
        lambda i, h: cots.at[h * 512 : h * 512 + 512, column(i)],
        x, lambda i: device(i, y, z, c), other, new,
    )
    cown = pltpu.make_async_copy(cot_t, cots.at[:, column(x)], new())
    orders = [(2, 1, 0), (0, 1, 2), (2, 1, 0), (1, 2, 0)]
    swap_send = new()
    swaps = [Swap(held.at[i], landed.at[i], at, orders[i], mask_ref, swap_send, new) for i in range(4)]

    pl.semaphore_wait(barrier, 15)
    sections[KEYS].fetch()
    for copy in loads:
        copy.wait()
    held[0, 0] = actions[FIRST : FIRST + 16]
    held[1, 0] = actions[FIRST + 16 : LAST]
    held[2, 0] = actions[LAST:]
    held[3, 0] = cot[LAST:]
    swaps[0].start()
    swaps[1].start()
    sections[QUERIES].fetch()
    sections[GATES].fetch()
    cot_t[...] = cot[...].astype(F32).T.astype(BF16)
    cring.start()
    cown.start()
    sections[KEYS].start()
    sections[QUERIES].start()
    for target in in_y:
        pl.semaphore_signal(vouch.at[0], inc=1, device_id=target, device_id_type=MESH)
    for d in (2, NZ - 2):
        pl.semaphore_signal(vouch.at[1], inc=1, device_id=device(x, y, (z + d) % NZ, c), device_id_type=MESH)

    for r in range(0, ROWS, CHUNK):
        n, inverse = normalize(actions[r : r + CHUNK].astype(F32))
        normed_in[r : r + CHUNK] = n
        inverse_in[r : r + CHUNK] = inverse
        normed[r : r + CHUNK] = (n * gain[...]).astype(BF16)

    row = lax.broadcasted_iota(jnp.int32, (ROWS, ROWS), 0)
    col = lax.broadcasted_iota(jnp.int32, (ROWS, ROWS), 1)
    begin = jnp.zeros((ROWS, ROWS), jnp.int32)
    end = jnp.zeros((), jnp.int32)
    for k in range(7):
        end = end + lengths_ref[0, 0, k]
        begin = begin + jnp.where(row >= end, lengths_ref[0, 0, k], 0)
    begin = jnp.where(row >= FIRST, FIRST, begin)
    begin = jnp.where(row >= LAST, LAST, begin)
    visible = (col >= begin) & (col <= row)

    def project(t, count=ROWS):
        for l in range(0, WIDTH, LANES):
            hidden = dot(normed[:count], wall[t, :, l : l + LANES])
            value, slope = silu_parts(hidden)
            active[t, :, l : l + LANES] = value[:ROWS].astype(BF16)
            slopes[t, :, l : l + LANES] = slope[:ROWS]
            if count > ROWS:
                far_active[t, :MOST, l : l + LANES] = value[ROWS:].astype(BF16)

    def small(t, rows, first, count):
        for l in range(0, WIDTH, LANES):
            hidden = dot(rows, wall[t, :, l : l + LANES])
            far_active[t, first : first + count, l : l + LANES] = silu_parts(hidden)[0].astype(BF16)

    def head(h):
        return slice(h * HEAD_DIM, (h + 1) * HEAD_DIM)

    swaps[1].turn(0)
    sections[KEYS].pass_on()
    sections[VALUES].start()
    sections[KEYS].spread()
    sections[QUERIES].pass_on()
    sections[QUERIES].spread()
    sections[GATES].pass_on()
    sections[GATES].start()
    swaps[0].turn(0)
    swaps[1].turn(1)
    pl.semaphore_wait(vouch.at[0], 3)
    pl.semaphore_wait(vouch.at[1], 2)
    for d in (4, NZ - 4):
        pl.semaphore_signal(vouch.at[2], inc=1, device_id=device(x, y, (z + d) % NZ, c), device_id_type=MESH)
    sections[KEYS].across()
    sections[GATES].spread()
    sections[QUERIES].across()
    sections[GATES].across()
    cring.forward()
    sections[VALUES].forward()
    swaps[0].turn(1)
    sections[KEYS].collect()
    sections[GATES].forward()
    sections[OUT].start()
    sections[QUERIES].collect()
    swaps[2].start()
    swaps[3].start()
    swaps[0].turn(2)
    swaps[1].turn(2)
    far_inputs = jnp.concatenate([held[0, 3], held[1, 3]], axis=0).astype(F32)
    normed[ROWS:] = (normalize(far_inputs)[0] * gain[...]).astype(BF16)
    sections[VALUES].finish()
    sections[KEYS].arrived()
    project(KEYS, ROWS + MOST)
    sections[QUERIES].arrived()
    project(QUERIES)
    sections[GATES].collect()
    sections[GATES].finish()

    far_slopes, far_weights = [], []
    for h in range(HEADS):
        q, k = active[QUERIES, :, head(h)], active[KEYS, :, head(h)]
        value, slope = silu_parts(dot_nt(q, k) * SCALE)
        weights[h] = (jnp.where(visible, value, 0.0) / MOST).astype(BF16)
        score_slopes[h] = jnp.where(visible, slope, 0.0) * BACK
        value, slope = silu_parts(dot_nt(q[LAST:], far_active[KEYS, :MOST, head(h)]) * SCALE)
        far_slopes.append(slope * BACK)
        far_weights.append((value / MOST).astype(BF16))
    sections[VALUES].arrived()
    project(VALUES, ROWS + MOST)
    for h in range(HEADS):
        local_part = dot(weights[h], active[VALUES, :, head(h)])
        far_part = dot(far_weights[h], far_active[VALUES, :MOST, head(h)])
        attended[:LAST, head(h)] = local_part[:LAST]
        attended[LAST:, head(h)] = local_part[LAST:] + far_part

    sections[GATES].arrived()
    project(GATES)
    for r in range(0, ROWS, CHUNK):
        n, inverse = normalize(attended[r : r + CHUNK])
        normed_out[r : r + CHUNK] = n
        inverse_out[r : r + CHUNK] = inverse
        mix = (n * active[GATES, r : r + CHUNK].astype(F32)).astype(BF16)
        for h in range(HEADS):
            mixed[h, r : r + CHUNK] = mix[:, head(h)]
    pl.semaphore_wait(vouch.at[2], 2)
    own_rows = pl.ds(pl.multiple_of(me * ROWS, ROWS), ROWS)
    msend, mrecv, ysend, yrecv, zsend, zrecv, asend, arecv = [new() for _ in range(8)]
    spread = [remote(mixed.at[group[d]], all_mixed.at[own_rows], msend, mrecv, in_group[d]) for d in range(7)]
    start_all(spread)
    all_mixed[own_rows] = mixed[me]
    cring.finish()
    sections[OUT].forward()
    swaps[2].turn(0)
    swaps[3].turn(0)

    await_received(all_mixed.at[: 7 * ROWS], mrecv, other)
    cown.wait()
    cring.arrived()
    for d in (2, 1, 3, 0):
        quarter = pl.ds(pl.multiple_of((y + d) % 4 * 256, 256), 256)
        product = dot(cots[quarter], all_mixed[...])
        if d:
            sums[quarter] = product.astype(BF16)
            copy = remote(sums.at[quarter], ybuf.at[d - 1], ysend, yrecv, in_y[d - 1])
            copy.start()
        else:
            total[...] = product

    swaps[2].turn(1)
    swaps[3].turn(1)
    sections[OUT].finish()
    sections[OUT].arrived()
    for l in range(0, WIDTH, LANES):
        grad_mix[:, l : l + LANES] = dot_nt(cot[...], wall[OUT, l : l + LANES])

    for r in range(0, ROWS, CHUNK):
        span = slice(r, r + CHUNK)
        grad = grad_mix[span]
        n = normed_out[span]
        grad_hidden[GATES, span] = (grad * n * slopes[GATES, span]).astype(BF16)
        grad_att[span] = norm_backward(
            grad * active[GATES, span].astype(F32), n, inverse_out[span]
        ).astype(BF16)

    mixed_rows = jnp.concatenate([mixed[h] for h in range(HEADS)], axis=1)
    for l in range(0, WIDTH, LANES):
        output[0, :, l : l + LANES] = (
            dot(mixed_rows, wall[OUT, :, l : l + LANES]) + actions[:, l : l + LANES].astype(F32)
        ).astype(BF16)
    await_received(ybuf, yrecv, other)
    part[...] = (
        total[...] + ybuf[0].astype(F32) + ybuf[1].astype(F32) + ybuf[2].astype(F32)
    ).astype(BF16)
    zcopies = [
        remote(part.at[pl.ds(pl.multiple_of((z + d + 1) % NZ * 16, 16), 16)], zbuf.at[d], zsend, zrecv, in_z[d])
        for d in range(NZ - 1)
    ]
    for d in (7, 6, 8, 5, 9, 4, 10, 3, 11, 2, 12, 1, 13, 0, 14):
        zcopies[d].start()

    swaps[2].turn(2)
    swaps[3].turn(2)
    spill_inputs = held[2, 3].astype(F32)
    far_normed[...] = (normalize(spill_inputs)[0] * gain[...]).astype(BF16)
    for t in (GATES, VALUES, QUERIES, KEYS):
        small(t, far_normed[...], MOST, SPILL)
    rows16 = lax.broadcasted_iota(jnp.int32, (SPILL, SPILL), 0)
    cols16 = lax.broadcasted_iota(jnp.int32, (SPILL, SPILL), 1)
    causal = cols16 <= rows16
    near_weights, near_slopes, near_attended = [], [], []
    for h in range(HEADS):
        q = far_active[QUERIES, MOST:, head(h)]
        value, slope = silu_parts(dot_nt(q, active[KEYS, FIRST:LAST, head(h)]) * SCALE)
        weight = (value / MOST).astype(BF16)
        near_weights.append(weight)
        near_slopes.append(slope * BACK)
        value, _ = silu_parts(dot_nt(q, far_active[KEYS, MOST:, head(h)]) * SCALE)
        weight2 = (jnp.where(causal, value, 0.0) / MOST).astype(BF16)
        near_attended.append(
            dot(weight, active[VALUES, FIRST:LAST, head(h)]) + dot(weight2, far_active[VALUES, MOST:, head(h)])
        )
    near_grad = dot_nt(held[3, 3], wall[OUT])
    near_normed, near_inverse = normalize(jnp.concatenate(near_attended, axis=1))
    near_att = norm_backward(
        near_grad * far_active[GATES, MOST:].astype(F32), near_normed, near_inverse
    ).astype(BF16)

    for h in range(HEADS):
        q, k, v = active[QUERIES, :, head(h)], active[KEYS, :, head(h)], active[VALUES, :, head(h)]
        g = grad_att[:, head(h)]
        grad_s = (dot_nt(g, v) * score_slopes[h]).astype(BF16)
        far_s = (dot_nt(g[LAST:], far_active[VALUES, :MOST, head(h)]) * far_slopes[h]).astype(BF16)
        near_g = near_att[:, head(h)]
        near_s = (dot_nt(near_g, v[FIRST:LAST]) * near_slopes[h]).astype(BF16)
        grad_q = dot(grad_s, k)
        far_q = dot(far_s, far_active[KEYS, :MOST, head(h)])
        grad_k = dot_tn(grad_s, q)
        near_k = dot_tn(near_s, far_active[QUERIES, MOST:, head(h)])
        grad_v = dot_tn(weights[h], g)
        near_v = dot_tn(near_weights[h], near_g)
        slope = slopes[QUERIES, :, head(h)]
        grad_hidden[QUERIES, :LAST, head(h)] = (grad_q[:LAST] * slope[:LAST]).astype(BF16)
        grad_hidden[QUERIES, LAST:, head(h)] = ((grad_q[LAST:] + far_q) * slope[LAST:]).astype(BF16)
        for t, grad, extra in ((KEYS, grad_k, near_k), (VALUES, grad_v, near_v)):
            slope = slopes[t, :, head(h)]
            grad_hidden[t, :FIRST, head(h)] = (grad[:FIRST] * slope[:FIRST]).astype(BF16)
            grad_hidden[t, FIRST:LAST, head(h)] = ((grad[FIRST:LAST] + extra) * slope[FIRST:LAST]).astype(BF16)
            grad_hidden[t, LAST:, head(h)] = (grad[LAST:] * slope[LAST:]).astype(BF16)

    await_received(zbuf, zrecv, other)
    summed = part[pl.ds(pl.multiple_of(z * 16, 16), 16)].astype(F32)
    for d in range(NZ - 1):
        summed = summed + zbuf[d].astype(F32)
    final[...] = summed * (1.0 / 256.0)
    for i in range(8):
        copy = remote(final, wide.at[me], asend, arecv, ends[i])

        @pl.when(apart[i])
        def _():
            copy.start()

    @pl.when(x == y)
    def _():
        wide[me] = final[...]


    for l in range(0, WIDTH, LANES):
        grad_mix[:, l : l + LANES] = (
            dot_nt(grad_hidden[0], wall[0, l : l + LANES])
            + dot_nt(grad_hidden[1], wall[1, l : l + LANES])
            + dot_nt(grad_hidden[2], wall[2, l : l + LANES])
            + dot_nt(grad_hidden[3], wall[3, l : l + LANES])
        ) * gain[:, l : l + LANES]
    for r in range(0, ROWS, CHUNK):
        span = slice(r, r + CHUNK)
        grad_input[0, span] = (
            cot[span].astype(F32) + norm_backward(grad_mix[span], normed_in[span], inverse_in[span])
        ).astype(BF16)

    for section in sections.values():
        section.sent()
    cring.sent()
    await_sent(wall.at[OUT, : 12 * SPILL], swap_send, other)
    await_sent(all_mixed.at[: 7 * ROWS], msend, other)
    await_sent(ybuf, ysend, other)
    await_sent(zbuf, zsend, other)
    @pl.when(x == y)
    def _():
        await_received(wide.at[:7], arecv, other)

    @pl.when(x != y)
    def _():
        await_received(wide, arecv, other)

    for i in range(8):
        weight_grad[:, i * 128 : (i + 1) * 128] = wide[i]

    @pl.when(x == y)
    def _():
        await_sent(wide.at[:7], asend, other)

    @pl.when(x != y)
    def _():
        await_sent(wide, asend, other)


def publish_kernel(*refs):
    copies = [pltpu.make_async_copy(refs[i], refs[3 + i], refs[6].at[i]) for i in range(3)]
    start_all(copies)
    for copy in copies:
        copy.wait()


def per_device(actions, lengths, partner_mask, norm_gain, w_in, w_out, cotangent):
    hbm = pl.BlockSpec(memory_space=pltpu.HBM)
    vmem = pl.BlockSpec(memory_space=pltpu.VMEM)
    dma = pltpu.SemaphoreType.DMA
    block = (ROWS, WIDTH)
    shapes = (
        jax.ShapeDtypeStruct((1, ROWS, WIDTH), BF16),
        jax.ShapeDtypeStruct((1, ROWS, WIDTH), BF16),
        jax.ShapeDtypeStruct((16, WIDTH), F32),
    )
    results = pl.pallas_call(
        layer_kernel,
        out_shape=tuple(pltpu.VMEM(shape.shape, shape.dtype) for shape in shapes),
        in_specs=[hbm] * 7,
        out_specs=(vmem, vmem, vmem),
        scratch_shapes=[
            pltpu.SMEM((1, 1), jnp.int32),
            pltpu.SMEM((1, 1, 7), jnp.int32),

            pltpu.VMEM(block, BF16),
            pltpu.VMEM((1, WIDTH), F32),
            pltpu.VMEM(block, BF16),
            pltpu.VMEM((5, WIDTH, WIDTH), BF16),
            pltpu.VMEM((WIDTH, WIDTH), BF16),
            pltpu.VMEM((WIDTH, ROWS), BF16),
            pltpu.VMEM((ROWS + MOST, WIDTH), BF16),
            pltpu.VMEM(block, F32),
            pltpu.VMEM((ROWS, 1), F32),
            pltpu.VMEM((4, ROWS, WIDTH), BF16),
            pltpu.VMEM((4, ROWS, WIDTH), F32),
            pltpu.VMEM((HEADS, ROWS, ROWS), BF16),
            pltpu.VMEM((HEADS, ROWS, ROWS), F32),
            pltpu.VMEM(block, F32),
            pltpu.VMEM(block, F32),
            pltpu.VMEM((ROWS, 1), F32),
            pltpu.VMEM((HEADS, ROWS, HEAD_DIM), BF16),
            pltpu.VMEM((SPILL, WIDTH), BF16),
            pltpu.VMEM((4, MOST + SPILL, WIDTH), BF16),
            pltpu.VMEM(block, BF16),
            pltpu.VMEM(block, F32),
            pltpu.VMEM((4, ROWS, WIDTH), BF16),
            pltpu.VMEM((4, 4, SPILL, WIDTH), BF16),
            pltpu.VMEM((4, 3, SPILL, WIDTH), BF16),
            pltpu.VMEM((WIDTH, 128), BF16),
            pltpu.VMEM((256, 128), F32),
            pltpu.VMEM((WIDTH, 128), BF16),
            pltpu.VMEM((3, 256, 128), BF16),
            pltpu.VMEM((256, 128), BF16),
            pltpu.VMEM((NZ - 1, 16, 128), BF16),
            pltpu.VMEM((16, 128), F32),
            pltpu.VMEM((8, 16, 128), F32),
            dma((SEMAPHORES,)),
            pltpu.SemaphoreType.REGULAR((3,)),
        ],
        compiler_params=pltpu.CompilerParams(
            collective_id=0, has_side_effects=True, vmem_limit_bytes=56 * 1024 * 1024
        ),
        name="layer",
    )(partner_mask, lengths, actions, norm_gain.reshape(1, WIDTH), w_in, w_out, cotangent)
    return pl.pallas_call(
        publish_kernel,
        out_shape=shapes,
        in_specs=[vmem, vmem, vmem],
        out_specs=(hbm, hbm, hbm),
        scratch_shapes=[dma((3,))],
        compiler_params=pltpu.CompilerParams(vmem_limit_bytes=16 * 1024 * 1024),
        name="publish",
    )(*results)


def solution(mesh):
    placed = (
        P("fsdp", "dp", None),
        P("fsdp", "dp", None),
        P("fsdp", "dp"),
        P(),
        P("fsdp", None),
        P("fsdp", None),
        P("fsdp", "dp", None),
    )
    return jax.shard_map(
        per_device,
        mesh=mesh,
        in_specs=placed,
        out_specs=(P("fsdp", "dp", None), P("fsdp", "dp", None), P("dp", None)),
        check_vma=False,
    )
```

```python
import jax
import jax.numpy as jnp
from jax import lax
from jax.experimental import pallas as pl
from jax.experimental.pallas import tpu as pltpu
from jax.sharding import PartitionSpec as P

HEADS = 8
HEAD_DIM = 128
SPILL = 16
MOST = 32
ROWS = 128
WIDTH = 1024
LAST = ROWS - SPILL
FIRST = LAST - MOST
NZ = 16
EPSILON = 1e-05
SCALE = HEAD_DIM ** (-0.5)
BACK = SCALE / MOST
MESH = pl.DeviceIdType.MESH
F32 = jnp.float32
BF16 = jnp.bfloat16
GATES, VALUES, QUERIES, KEYS, OUT = range(5)
HALF = WIDTH // 2
PLAN = {
    VALUES: (128, []),
    KEYS: (0, [("x", 0, 16, 0, WIDTH), ("z", 64, 16, 0, WIDTH)]),
    QUERIES: (0, [("x", 0, 16, 0, WIDTH), ("z", 64, 16, 0, WIDTH)]),
    GATES: (64, [("x", 64, 16, 0, WIDTH)]),
    OUT: (128, []),
}
SEMAPHORES = 78
CHUNK = 32
LANES = 256


def device(x, y, z, c):
    return (x * NZ + z, y * 2 + c)


def remote(src, dst, send, recv, target):
    return pltpu.make_async_remote_copy(
        src_ref=src, dst_ref=dst, send_sem=send, recv_sem=recv, device_id=target, device_id_type=MESH
    )


def start_all(copies):
    for copy in copies:
        copy.start()


def dot(a, b):
    return jnp.dot(a, b, preferred_element_type=F32)


def dot_nt(a, b):
    return lax.dot_general(a, b, (((1,), (1,)), ((), ())), preferred_element_type=F32)


def dot_tn(a, b):
    return lax.dot_general(a, b, (((0,), (0,)), ((), ())), preferred_element_type=F32)


def normalize(values):
    centred = values - jnp.mean(values, axis=-1, keepdims=True)
    inverse = lax.rsqrt(jnp.mean(centred * centred, axis=-1, keepdims=True) + EPSILON)
    return (centred * inverse, inverse)


def norm_backward(grad, normed, inverse):
    return inverse * (
        grad
        - jnp.mean(grad, axis=-1, keepdims=True)
        - normed * jnp.mean(grad * normed, axis=-1, keepdims=True)
    )


def silu_parts(values):
    sigma = jax.nn.sigmoid(values)
    return values * sigma, sigma * (1.0 + values * (1.0 - sigma))


def await_received(ref, sem, target):
    remote(ref, ref, sem, sem, target).wait_recv()


def await_sent(ref, sem, target):
    remote(ref, ref, sem, sem, target).wait_send()


class Section:
    def __init__(self, src, wall, t, at, new):
        x, y, z, c = at
        direct, blocks = PLAN[t]
        other = device(x, y, z, 1 - c)
        sent = new()
        self.send, self.other, self.wall = sent, other, wall.at[t]
        self.rows_sent = 0

        def move(piece, target, recv, source=None):
            self.rows_sent += piece.shape[0] * piece.shape[1] // WIDTH
            return remote(piece if source is None else source, piece, sent, recv, target)

        def block(owner, first, count, column=0, columns=WIDTH):
            base = pl.multiple_of((2 * owner + c) * ROWS + first, 16)
            return wall.at[t, pl.ds(base, count), column : column + columns]

        ahead, behind, across = (y + 1) % 4, (y + 3) % 4, (y + 2) % 4
        to_ahead, to_behind = device(x, ahead, z, c), device(x, behind, z, c)
        self.own = pltpu.make_async_copy(src, block(y, 0, ROWS), new())
        self.core = new()
        self.to_core = move(block(y, 0, ROWS), other, self.core, src)
        self.first, self.forwards, self.cores, self.halves = [], [], [], []
        if direct:
            half = direct // 2
            piece = src.at[:direct]
            self.first = [
                move(block(y, 0, direct), to_ahead, new(), piece), move(block(y, 0, direct), to_behind, new(), piece)
            ]
            self.forwards = [
                move(block(behind, 0, half), to_ahead, new()), move(block(ahead, half, half), to_behind, new())
            ]
            self.cores = [
                move(block(behind, 0, direct), other, self.core), move(block(ahead, 0, direct), other, self.core)
            ]
            self.halves = [move(block(across, h * half, half), other, self.core) for h in range(2)]
        self.fetched, self.passed, self.spreads, self.late = {}, {}, {}, {}
        if not blocks:
            return
        self.near, self.far, self.spread_sem = {1: new(), 3: new()}, new(), {d: new() for d in (1, 3, 2)}
        self.block_rows = sum(count * columns // WIDTH for _, _, count, _, columns in blocks)
        for d, source, to in ((1, behind, to_ahead), (3, ahead, to_behind)):
            self.fetched[d], self.passed[d] = [], []
            for axis, first, count, column, columns in blocks:
                first = first + (x if axis == "x" else z % 4) * count
                self.fetched[d].append(
                    move(
                        block(y, first, count, column, columns), to, self.near[d],
                        src.at[pl.ds(pl.multiple_of(first, 16), count), column : column + columns],
                    )
                )
                part = columns // 2
                start = column + (part if d == 3 else 0)
                self.passed[d].append(move(block(source, first, count, start, part), to, self.far))
        for d, source in ((1, behind), (3, ahead), (2, across)):
            self.spreads[d] = []
            sem = self.spread_sem[d]
            for axis, first, count, column, columns in blocks:
                first = first + (x if axis == "x" else z % 4) * count
                whole = block(source, first, count, column, columns)
                if axis == "x":
                    self.spreads[d] += [move(whole, device((x + e) % 4, y, z, c), sem) for e in (2, 1, 3)]
                else:
                    part = columns // 2
                    self.spreads[d] += [
                        move(block(source, first, count, column, part), device(x, y, (z + 2) % NZ, c), sem),
                        move(block(source, first, count, column + part, part), device(x, y, (z + NZ - 2) % NZ, c), sem),
                        move(whole, device(x, y, (z + 1) % NZ, c), sem),
                        move(whole, device(x, y, (z + NZ - 1) % NZ, c), sem),
                    ]
            self.late[d] = move(block(source, direct, ROWS - direct), other, self.core)

    def received(self, rows, sem):
        await_received(self.wall.at[:rows], sem, self.other)

    def fetch(self):
        start_all(self.fetched[1] + self.fetched[3])

    def start(self):
        start_all(self.first)
        self.to_core.start()
        self.own.start()

    def pass_on(self):
        for d in (1, 3):
            self.received(self.block_rows, self.near[d])
            start_all(self.passed[d])

    def spread(self):
        start_all(self.spreads[1] + self.spreads[3])

    def across(self):
        self.received(self.block_rows, self.far)
        start_all(self.spreads[2])

    def collect(self):
        for d, late in self.late.items():
            self.received(3 * self.block_rows, self.spread_sem[d])
            late.start()

    def forward(self):
        for i, copy in enumerate(self.first):
            copy.wait_recv()
            self.forwards[i].start()
            self.cores[i].start()

    def finish(self):
        for forward, half in zip(self.forwards, self.halves):
            forward.wait_recv()
            half.start()

    def arrived(self):
        self.own.wait()
        self.received(4 * ROWS, self.core)

    def sent(self):
        await_sent(self.wall.at[: self.rows_sent], self.send, self.other)


class Ring:
    def __init__(self, own, cots, view, half, me, towards, other, new):
        ahead, behind, across = (me + 1) % 4, (me + 3) % 4, (me + 2) % 4
        self.cots, self.other = cots, other
        self.send = send = new()
        self.core = core = new()
        self.first = [
            remote(own, view(me), send, new(), towards(ahead)),
            remote(own, view(me), send, new(), towards(behind)),
            remote(own, view(me), send, core, other),
        ]
        self.behind = [
            remote(half(behind, 0), half(behind, 0), send, new(), towards(ahead)),
            remote(view(behind), view(behind), send, core, other),
        ]
        self.ahead = [
            remote(half(ahead, 1), half(ahead, 1), send, new(), towards(behind)),
            remote(view(ahead), view(ahead), send, core, other),
        ]
        self.across = [remote(half(across, h), half(across, h), send, core, other) for h in range(2)]

    def start(self):
        start_all(self.first)

    def forward(self):
        self.first[0].wait_recv()
        start_all(self.behind)
        self.first[1].wait_recv()
        start_all(self.ahead)

    def finish(self):
        self.behind[0].wait_recv()
        self.across[0].start()
        self.ahead[0].wait_recv()
        self.across[1].start()

    def arrived(self):
        await_received(self.cots.at[: 4 * ROWS], self.core, self.other)

    def sent(self):
        await_sent(self.cots.at[: 7 * ROWS], self.send, self.other)


class Swap:
    def __init__(self, held, landed, at, order, mask, send, new):
        x, y, z, c = at
        self.held, self.landed, self.order, self.mask = held, landed, order, mask
        self.copies = []
        for step, bit in enumerate(order):
            size = 1 << bit
            to = z + size - 2 * size * (z // size % 2)
            self.copies.append(
                remote(held.at[step], landed.at[step], send, new(), device(x, y, to, c))
            )

    def start(self):
        self.copies[0].start()

    def turn(self, step):
        self.copies[step].wait_recv()
        bit = jnp.full((SPILL, WIDTH), lax.shift_right_logical(self.mask[0, 0], self.order[step]) & 1, jnp.int32)
        chosen = jnp.where(bit == 1, self.landed[step].astype(F32), self.held[step].astype(F32))
        self.held[step + 1] = chosen.astype(BF16)
        if step < 2:
            self.copies[step + 1].start()


def layer_kernel(
    mask_hbm, lengths_hbm, actions_hbm, gain_hbm, w_in_ref, w_out_ref, cot_hbm,
    output, grad_input, weight_grad,
    mask_ref, lengths_ref,
    actions, gain, cot, wall, cots, cot_t, normed, normed_in, inverse_in,
    active, slopes, weights, score_slopes, attended, normed_out, inverse_out, mixed,
    far_normed, far_active, grad_att, grad_mix, grad_hidden,
    held, landed, all_mixed, total, sums, ybuf, part, zbuf, final, wide,
    sems, vouch,
):
    dp = lax.axis_index("dp")
    fsdp = lax.axis_index("fsdp")
    x, y, z, c = dp // NZ, fsdp // 2, dp % NZ, fsdp % 2
    me = 2 * x + c
    at = (x, y, z, c)
    other = device(x, y, z, 1 - c)
    group = [(2 * x + c + d) % 8 for d in range(1, 8)]
    in_group = [device(i // 2, y, z, i % 2) for i in group]
    in_y = [device(x, (y + d) % 4, z, c) for d in range(1, 4)]
    in_z = [device(x, y, (z + d) % NZ, c) for d in range(1, NZ)]
    ends = [device(y, i // 2, z, i % 2) for i in range(8)]
    near = [device((x + d) % 4, y, z, c) for d in (1, 3)] + [device(x, (y + d) % 4, z, c) for d in (1, 3)]
    near += [device(x, y, (z + d) % NZ, c) for d in (1, NZ - 1)] + [other]

    def vouch_for(step, targets):
        for target in targets:
            pl.semaphore_signal(vouch.at[step], inc=1, device_id=target, device_id_type=MESH)

    apart = [jnp.logical_or(x != y, i != me) for i in range(8)]

    used = [0]

    def new():
        used[0] += 1
        return sems.at[used[0] - 1]

    loads = [
        pltpu.make_async_copy(actions_hbm.at[0], actions, new()),
        pltpu.make_async_copy(cot_hbm.at[0], cot, new()),
        pltpu.make_async_copy(gain_hbm, gain, new()),
        pltpu.make_async_copy(mask_hbm, mask_ref, new()),
        pltpu.make_async_copy(lengths_hbm, lengths_ref, new()),
    ]
    barrier = pltpu.get_barrier_semaphore()
    for target in near:
        pl.semaphore_signal(barrier, inc=1, device_id=target, device_id_type=MESH)
    start_all(loads)

    sections = {
        t: Section(
            w_out_ref if t == OUT else w_in_ref.at[:, t * WIDTH : (t + 1) * WIDTH],
            wall, t, at, new,
        )
        for t in range(5)
    }
    column = lambda i: pl.ds(pl.multiple_of((2 * i + c) * ROWS, ROWS), ROWS)
    cring = Ring(
        cot_t, cots,
        lambda i: cots.at[:, column(i)],
        lambda i, h: cots.at[h * 512 : h * 512 + 512, column(i)],
        x, lambda i: device(i, y, z, c), other, new,
    )
    cown = pltpu.make_async_copy(cot_t, cots.at[:, column(x)], new())
    orders = [(2, 1, 0), (0, 1, 2), (2, 1, 0), (1, 2, 0)]
    swap_send = new()
    swaps = [Swap(held.at[i], landed.at[i], at, orders[i], mask_ref, swap_send, new) for i in range(4)]

    pl.semaphore_wait(barrier, len(near))
    sections[KEYS].fetch()
    for copy in loads:
        copy.wait()
    held[0, 0] = actions[FIRST : FIRST + 16]
    held[1, 0] = actions[FIRST + 16 : LAST]
    held[2, 0] = actions[LAST:]
    held[3, 0] = cot[LAST:]
    swaps[1].start()
    sections[QUERIES].fetch()
    sections[GATES].fetch()
    cot_t[...] = cot[...].astype(F32).T.astype(BF16)
    cring.start()
    cown.start()
    sections[KEYS].start()
    sections[QUERIES].start()
    vouch_for(0, near)

    for r in range(0, ROWS, CHUNK):
        n, inverse = normalize(actions[r : r + CHUNK].astype(F32))
        normed_in[r : r + CHUNK] = n
        inverse_in[r : r + CHUNK] = inverse
        normed[r : r + CHUNK] = (n * gain[...]).astype(BF16)

    row = lax.broadcasted_iota(jnp.int32, (ROWS, ROWS), 0)
    col = lax.broadcasted_iota(jnp.int32, (ROWS, ROWS), 1)
    begin = jnp.zeros((ROWS, ROWS), jnp.int32)
    end = jnp.zeros((), jnp.int32)
    for k in range(7):
        end = end + lengths_ref[0, 0, k]
        begin = begin + jnp.where(row >= end, lengths_ref[0, 0, k], 0)
    begin = jnp.where(row >= FIRST, FIRST, begin)
    begin = jnp.where(row >= LAST, LAST, begin)
    visible = (col >= begin) & (col <= row)

    def project(t, count=ROWS):
        for l in range(0, WIDTH, LANES):
            hidden = dot(normed[:count], wall[t, :, l : l + LANES])
            value, slope = silu_parts(hidden)
            active[t, :, l : l + LANES] = value[:ROWS].astype(BF16)
            slopes[t, :, l : l + LANES] = slope[:ROWS]
            if count > ROWS:
                far_active[t, :MOST, l : l + LANES] = value[ROWS:].astype(BF16)

    def small(t, rows, first, count):
        for l in range(0, WIDTH, LANES):
            hidden = dot(rows, wall[t, :, l : l + LANES])
            far_active[t, first : first + count, l : l + LANES] = silu_parts(hidden)[0].astype(BF16)

    def head(h):
        return slice(h * HEAD_DIM, (h + 1) * HEAD_DIM)

    pl.semaphore_wait(vouch.at[0], len(near))
    vouch_for(1, [device(x, y, (z + d) % NZ, c) for d in (2, NZ - 2)] + [other])
    pl.semaphore_wait(vouch.at[1], 3)
    swaps[0].start()
    vouch_for(2, [device(x, y, (z + d) % NZ, c) for d in (4, NZ - 4)] + in_y)
    swaps[1].turn(0)
    sections[KEYS].pass_on()
    sections[VALUES].start()
    sections[KEYS].spread()
    sections[QUERIES].pass_on()
    sections[QUERIES].spread()
    sections[GATES].pass_on()
    sections[GATES].start()
    swaps[0].turn(0)
    swaps[1].turn(1)
    sections[KEYS].across()
    sections[GATES].spread()
    sections[QUERIES].across()
    sections[GATES].across()
    cring.forward()
    sections[VALUES].forward()
    swaps[0].turn(1)
    sections[KEYS].collect()
    sections[GATES].forward()
    sections[OUT].start()
    sections[QUERIES].collect()
    swaps[2].start()
    swaps[3].start()
    swaps[0].turn(2)
    swaps[1].turn(2)
    far_inputs = jnp.concatenate([held[0, 3], held[1, 3]], axis=0).astype(F32)
    normed[ROWS:] = (normalize(far_inputs)[0] * gain[...]).astype(BF16)
    sections[VALUES].finish()
    sections[KEYS].arrived()
    project(KEYS, ROWS + MOST)
    sections[QUERIES].arrived()
    project(QUERIES)
    sections[GATES].collect()
    sections[GATES].finish()

    far_slopes, far_weights = [], []
    for h in range(HEADS):
        q, k = active[QUERIES, :, head(h)], active[KEYS, :, head(h)]
        value, slope = silu_parts(dot_nt(q, k) * SCALE)
        weights[h] = (jnp.where(visible, value, 0.0) / MOST).astype(BF16)
        score_slopes[h] = jnp.where(visible, slope, 0.0) * BACK
        value, slope = silu_parts(dot_nt(q[LAST:], far_active[KEYS, :MOST, head(h)]) * SCALE)
        far_slopes.append(slope * BACK)
        far_weights.append((value / MOST).astype(BF16))
    sections[VALUES].arrived()
    project(VALUES, ROWS + MOST)
    for h in range(HEADS):
        local_part = dot(weights[h], active[VALUES, :, head(h)])
        far_part = dot(far_weights[h], far_active[VALUES, :MOST, head(h)])
        attended[:LAST, head(h)] = local_part[:LAST]
        attended[LAST:, head(h)] = local_part[LAST:] + far_part

    sections[GATES].arrived()
    project(GATES)
    for r in range(0, ROWS, CHUNK):
        n, inverse = normalize(attended[r : r + CHUNK])
        normed_out[r : r + CHUNK] = n
        inverse_out[r : r + CHUNK] = inverse
        mix = (n * active[GATES, r : r + CHUNK].astype(F32)).astype(BF16)
        for h in range(HEADS):
            mixed[h, r : r + CHUNK] = mix[:, head(h)]
    pl.semaphore_wait(vouch.at[2], 5)
    own_rows = pl.ds(pl.multiple_of(me * ROWS, ROWS), ROWS)
    msend, mrecv, ysend, yrecv, zsend, zrecv, asend, arecv = [new() for _ in range(8)]
    spread = [remote(mixed.at[group[d]], all_mixed.at[own_rows], msend, mrecv, in_group[d]) for d in range(7)]
    start_all(spread)
    all_mixed[own_rows] = mixed[me]
    cring.finish()
    sections[OUT].forward()
    swaps[2].turn(0)
    swaps[3].turn(0)

    await_received(all_mixed.at[: 7 * ROWS], mrecv, other)
    cown.wait()
    cring.arrived()
    for d in (2, 1, 3, 0):
        quarter = pl.ds(pl.multiple_of((y + d) % 4 * 256, 256), 256)
        product = dot(cots[quarter], all_mixed[...])
        if d:
            sums[quarter] = product.astype(BF16)
            copy = remote(sums.at[quarter], ybuf.at[d - 1], ysend, yrecv, in_y[d - 1])
            copy.start()
        else:
            total[...] = product

    swaps[2].turn(1)
    swaps[3].turn(1)
    sections[OUT].finish()
    sections[OUT].arrived()
    for l in range(0, WIDTH, LANES):
        grad_mix[:, l : l + LANES] = dot_nt(cot[...], wall[OUT, l : l + LANES])

    for r in range(0, ROWS, CHUNK):
        span = slice(r, r + CHUNK)
        grad = grad_mix[span]
        n = normed_out[span]
        grad_hidden[GATES, span] = (grad * n * slopes[GATES, span]).astype(BF16)
        grad_att[span] = norm_backward(
            grad * active[GATES, span].astype(F32), n, inverse_out[span]
        ).astype(BF16)

    mixed_rows = jnp.concatenate([mixed[h] for h in range(HEADS)], axis=1)
    for l in range(0, WIDTH, LANES):
        output[0, :, l : l + LANES] = (
            dot(mixed_rows, wall[OUT, :, l : l + LANES]) + actions[:, l : l + LANES].astype(F32)
        ).astype(BF16)
    await_received(ybuf, yrecv, other)
    part[...] = (
        total[...] + ybuf[0].astype(F32) + ybuf[1].astype(F32) + ybuf[2].astype(F32)
    ).astype(BF16)
    zcopies = [
        remote(part.at[pl.ds(pl.multiple_of((z + d + 1) % NZ * 16, 16), 16)], zbuf.at[d], zsend, zrecv, in_z[d])
        for d in range(NZ - 1)
    ]
    for d in (7, 6, 8, 5, 9, 4, 10, 3, 11, 2, 12, 1, 13, 0, 14):
        zcopies[d].start()

    swaps[2].turn(2)
    swaps[3].turn(2)
    spill_inputs = held[2, 3].astype(F32)
    far_normed[...] = (normalize(spill_inputs)[0] * gain[...]).astype(BF16)
    for t in (GATES, VALUES, QUERIES, KEYS):
        small(t, far_normed[...], MOST, SPILL)
    rows16 = lax.broadcasted_iota(jnp.int32, (SPILL, SPILL), 0)
    cols16 = lax.broadcasted_iota(jnp.int32, (SPILL, SPILL), 1)
    causal = cols16 <= rows16
    near_weights, near_slopes, near_attended = [], [], []
    for h in range(HEADS):
        q = far_active[QUERIES, MOST:, head(h)]
        value, slope = silu_parts(dot_nt(q, active[KEYS, FIRST:LAST, head(h)]) * SCALE)
        weight = (value / MOST).astype(BF16)
        near_weights.append(weight)
        near_slopes.append(slope * BACK)
        value, _ = silu_parts(dot_nt(q, far_active[KEYS, MOST:, head(h)]) * SCALE)
        weight2 = (jnp.where(causal, value, 0.0) / MOST).astype(BF16)
        near_attended.append(
            dot(weight, active[VALUES, FIRST:LAST, head(h)]) + dot(weight2, far_active[VALUES, MOST:, head(h)])
        )
    near_grad = dot_nt(held[3, 3], wall[OUT])
    near_normed, near_inverse = normalize(jnp.concatenate(near_attended, axis=1))
    near_att = norm_backward(
        near_grad * far_active[GATES, MOST:].astype(F32), near_normed, near_inverse
    ).astype(BF16)

    for h in range(HEADS):
        q, k, v = active[QUERIES, :, head(h)], active[KEYS, :, head(h)], active[VALUES, :, head(h)]
        g = grad_att[:, head(h)]
        grad_s = (dot_nt(g, v) * score_slopes[h]).astype(BF16)
        far_s = (dot_nt(g[LAST:], far_active[VALUES, :MOST, head(h)]) * far_slopes[h]).astype(BF16)
        near_g = near_att[:, head(h)]
        near_s = (dot_nt(near_g, v[FIRST:LAST]) * near_slopes[h]).astype(BF16)
        grad_q = dot(grad_s, k)
        far_q = dot(far_s, far_active[KEYS, :MOST, head(h)])
        grad_k = dot_tn(grad_s, q)
        near_k = dot_tn(near_s, far_active[QUERIES, MOST:, head(h)])
        grad_v = dot_tn(weights[h], g)
        near_v = dot_tn(near_weights[h], near_g)
        slope = slopes[QUERIES, :, head(h)]
        grad_hidden[QUERIES, :LAST, head(h)] = (grad_q[:LAST] * slope[:LAST]).astype(BF16)
        grad_hidden[QUERIES, LAST:, head(h)] = ((grad_q[LAST:] + far_q) * slope[LAST:]).astype(BF16)
        for t, grad, extra in ((KEYS, grad_k, near_k), (VALUES, grad_v, near_v)):
            slope = slopes[t, :, head(h)]
            grad_hidden[t, :FIRST, head(h)] = (grad[:FIRST] * slope[:FIRST]).astype(BF16)
            grad_hidden[t, FIRST:LAST, head(h)] = ((grad[FIRST:LAST] + extra) * slope[FIRST:LAST]).astype(BF16)
            grad_hidden[t, LAST:, head(h)] = (grad[LAST:] * slope[LAST:]).astype(BF16)

    await_received(zbuf, zrecv, other)
    summed = part[pl.ds(pl.multiple_of(z * 16, 16), 16)].astype(F32)
    for d in range(NZ - 1):
        summed = summed + zbuf[d].astype(F32)
    final[...] = summed * (1.0 / 256.0)
    for i in range(8):
        copy = remote(final, wide.at[me], asend, arecv, ends[i])

        @pl.when(apart[i])
        def _():
            copy.start()

    @pl.when(x == y)
    def _():
        wide[me] = final[...]


    for l in range(0, WIDTH, LANES):
        grad_mix[:, l : l + LANES] = (
            dot_nt(grad_hidden[0], wall[0, l : l + LANES])
            + dot_nt(grad_hidden[1], wall[1, l : l + LANES])
            + dot_nt(grad_hidden[2], wall[2, l : l + LANES])
            + dot_nt(grad_hidden[3], wall[3, l : l + LANES])
        ) * gain[:, l : l + LANES]
    for r in range(0, ROWS, CHUNK):
        span = slice(r, r + CHUNK)
        grad_input[0, span] = (
            cot[span].astype(F32) + norm_backward(grad_mix[span], normed_in[span], inverse_in[span])
        ).astype(BF16)

    for section in sections.values():
        section.sent()
    cring.sent()
    await_sent(wall.at[OUT, : 12 * SPILL], swap_send, other)
    await_sent(all_mixed.at[: 7 * ROWS], msend, other)
    await_sent(ybuf, ysend, other)
    await_sent(zbuf, zsend, other)
    @pl.when(x == y)
    def _():
        await_received(wide.at[:7], arecv, other)

    @pl.when(x != y)
    def _():
        await_received(wide, arecv, other)

    for i in range(8):
        weight_grad[:, i * 128 : (i + 1) * 128] = wide[i]

    @pl.when(x == y)
    def _():
        await_sent(wide.at[:7], asend, other)

    @pl.when(x != y)
    def _():
        await_sent(wide, asend, other)


def publish_kernel(*refs):
    copies = [pltpu.make_async_copy(refs[i], refs[3 + i], refs[6].at[i]) for i in range(3)]
    start_all(copies)
    for copy in copies:
        copy.wait()


def per_device(actions, lengths, partner_mask, norm_gain, w_in, w_out, cotangent):
    hbm = pl.BlockSpec(memory_space=pltpu.HBM)
    vmem = pl.BlockSpec(memory_space=pltpu.VMEM)
    dma = pltpu.SemaphoreType.DMA
    block = (ROWS, WIDTH)
    shapes = (
        jax.ShapeDtypeStruct((1, ROWS, WIDTH), BF16),
        jax.ShapeDtypeStruct((1, ROWS, WIDTH), BF16),
        jax.ShapeDtypeStruct((16, WIDTH), F32),
    )
    results = pl.pallas_call(
        layer_kernel,
        out_shape=tuple(pltpu.VMEM(shape.shape, shape.dtype) for shape in shapes),
        in_specs=[hbm] * 7,
        out_specs=(vmem, vmem, vmem),
        scratch_shapes=[
            pltpu.SMEM((1, 1), jnp.int32),
            pltpu.SMEM((1, 1, 7), jnp.int32),

            pltpu.VMEM(block, BF16),
            pltpu.VMEM((1, WIDTH), F32),
            pltpu.VMEM(block, BF16),
            pltpu.VMEM((5, WIDTH, WIDTH), BF16),
            pltpu.VMEM((WIDTH, WIDTH), BF16),
            pltpu.VMEM((WIDTH, ROWS), BF16),
            pltpu.VMEM((ROWS + MOST, WIDTH), BF16),
            pltpu.VMEM(block, F32),
            pltpu.VMEM((ROWS, 1), F32),
            pltpu.VMEM((4, ROWS, WIDTH), BF16),
            pltpu.VMEM((4, ROWS, WIDTH), F32),
            pltpu.VMEM((HEADS, ROWS, ROWS), BF16),
            pltpu.VMEM((HEADS, ROWS, ROWS), F32),
            pltpu.VMEM(block, F32),
            pltpu.VMEM(block, F32),
            pltpu.VMEM((ROWS, 1), F32),
            pltpu.VMEM((HEADS, ROWS, HEAD_DIM), BF16),
            pltpu.VMEM((SPILL, WIDTH), BF16),
            pltpu.VMEM((4, MOST + SPILL, WIDTH), BF16),
            pltpu.VMEM(block, BF16),
            pltpu.VMEM(block, F32),
            pltpu.VMEM((4, ROWS, WIDTH), BF16),
            pltpu.VMEM((4, 4, SPILL, WIDTH), BF16),
            pltpu.VMEM((4, 3, SPILL, WIDTH), BF16),
            pltpu.VMEM((WIDTH, 128), BF16),
            pltpu.VMEM((256, 128), F32),
            pltpu.VMEM((WIDTH, 128), BF16),
            pltpu.VMEM((3, 256, 128), BF16),
            pltpu.VMEM((256, 128), BF16),
            pltpu.VMEM((NZ - 1, 16, 128), BF16),
            pltpu.VMEM((16, 128), F32),
            pltpu.VMEM((8, 16, 128), F32),
            dma((SEMAPHORES,)),
            pltpu.SemaphoreType.REGULAR((3,)),
        ],
        compiler_params=pltpu.CompilerParams(
            collective_id=0, has_side_effects=True, vmem_limit_bytes=56 * 1024 * 1024
        ),
        name="layer",
    )(partner_mask, lengths, actions, norm_gain.reshape(1, WIDTH), w_in, w_out, cotangent)
    return pl.pallas_call(
        publish_kernel,
        out_shape=shapes,
        in_specs=[vmem, vmem, vmem],
        out_specs=(hbm, hbm, hbm),
        scratch_shapes=[dma((3,))],
        compiler_params=pltpu.CompilerParams(vmem_limit_bytes=16 * 1024 * 1024),
        name="publish",
    )(*results)


def solution(mesh):
    placed = (
        P("fsdp", "dp", None),
        P("fsdp", "dp", None),
        P("fsdp", "dp"),
        P(),
        P("fsdp", None),
        P("fsdp", None),
        P("fsdp", "dp", None),
    )
    return jax.shard_map(
        per_device,
        mesh=mesh,
        in_specs=placed,
        out_specs=(P("fsdp", "dp", None), P("fsdp", "dp", None), P("dp", None)),
        check_vma=False,
    )
```

```python
import jax
import jax.numpy as jnp
from jax import lax
from jax.experimental import pallas as pl
from jax.experimental.pallas import tpu as pltpu
from jax.sharding import PartitionSpec as P

HEADS = 8
HEAD_DIM = 128
SPILL = 16
MOST = 32
ROWS = 128
WIDTH = 1024
LAST = ROWS - SPILL
FIRST = LAST - MOST
NZ = 16
EPSILON = 1e-05
SCALE = HEAD_DIM ** (-0.5)
BACK = SCALE / MOST
MESH = pl.DeviceIdType.MESH
F32 = jnp.float32
BF16 = jnp.bfloat16
GATES, VALUES, QUERIES, KEYS, OUT = range(5)
HALF = WIDTH // 2
PLAN = {
    VALUES: (128, []),
    KEYS: (0, [("x", 0, 16, 0, WIDTH), ("z", 64, 16, 0, WIDTH)]),
    QUERIES: (0, [("x", 0, 16, 0, WIDTH), ("z", 64, 16, 0, WIDTH)]),
    GATES: (64, [("x", 64, 16, 0, WIDTH)]),
    OUT: (128, []),
}
SEMAPHORES = 78
CHUNK = 32
LANES = 256


def device(x, y, z, c):
    return (x * NZ + z, y * 2 + c)


def remote(src, dst, send, recv, target):
    return pltpu.make_async_remote_copy(
        src_ref=src, dst_ref=dst, send_sem=send, recv_sem=recv, device_id=target, device_id_type=MESH
    )


def start_all(copies):
    for copy in copies:
        copy.start()


def dot(a, b):
    return jnp.dot(a, b, preferred_element_type=F32)


def dot_nt(a, b):
    return lax.dot_general(a, b, (((1,), (1,)), ((), ())), preferred_element_type=F32)


def dot_tn(a, b):
    return lax.dot_general(a, b, (((0,), (0,)), ((), ())), preferred_element_type=F32)


def normalize(values):
    centred = values - jnp.mean(values, axis=-1, keepdims=True)
    inverse = lax.rsqrt(jnp.mean(centred * centred, axis=-1, keepdims=True) + EPSILON)
    return (centred * inverse, inverse)


def norm_backward(grad, normed, inverse):
    return inverse * (
        grad
        - jnp.mean(grad, axis=-1, keepdims=True)
        - normed * jnp.mean(grad * normed, axis=-1, keepdims=True)
    )


def silu_parts(values):
    sigma = jax.nn.sigmoid(values)
    return values * sigma, sigma * (1.0 + values * (1.0 - sigma))


def await_received(ref, sem, target):
    remote(ref, ref, sem, sem, target).wait_recv()


def await_sent(ref, sem, target):
    remote(ref, ref, sem, sem, target).wait_send()


class Section:
    def __init__(self, src, wall, t, at, new):
        x, y, z, c = at
        direct, blocks = PLAN[t]
        other = device(x, y, z, 1 - c)
        sent = new()
        self.send, self.other, self.wall = sent, other, wall.at[t]
        self.rows_sent = 0

        def move(piece, target, recv, source=None):
            self.rows_sent += piece.shape[0] * piece.shape[1] // WIDTH
            return remote(piece if source is None else source, piece, sent, recv, target)

        def block(owner, first, count, column=0, columns=WIDTH):
            base = pl.multiple_of((2 * owner + c) * ROWS + first, 16)
            return wall.at[t, pl.ds(base, count), column : column + columns]

        ahead, behind, across = (y + 1) % 4, (y + 3) % 4, (y + 2) % 4
        to_ahead, to_behind = device(x, ahead, z, c), device(x, behind, z, c)
        self.own = pltpu.make_async_copy(src, block(y, 0, ROWS), new())
        self.core = new()
        self.to_core = move(block(y, 0, ROWS), other, self.core, src)
        self.first, self.forwards, self.cores, self.halves = [], [], [], []
        if direct:
            half = direct // 2
            piece = src.at[:direct]
            self.first = [
                move(block(y, 0, direct), to_ahead, new(), piece), move(block(y, 0, direct), to_behind, new(), piece)
            ]
            self.forwards = [
                move(block(behind, 0, half), to_ahead, new()), move(block(ahead, half, half), to_behind, new())
            ]
            self.cores = [
                move(block(behind, 0, direct), other, self.core), move(block(ahead, 0, direct), other, self.core)
            ]
            self.halves = [move(block(across, h * half, half), other, self.core) for h in range(2)]
        self.fetched, self.passed, self.spreads, self.late = {}, {}, {}, {}
        if not blocks:
            return
        self.near, self.far, self.spread_sem = {1: new(), 3: new()}, new(), {d: new() for d in (1, 3, 2)}
        self.block_rows = sum(count * columns // WIDTH for _, _, count, _, columns in blocks)
        for d, source, to in ((1, behind, to_ahead), (3, ahead, to_behind)):
            self.fetched[d], self.passed[d] = [], []
            for axis, first, count, column, columns in blocks:
                first = first + (x if axis == "x" else z % 4) * count
                self.fetched[d].append(
                    move(
                        block(y, first, count, column, columns), to, self.near[d],
                        src.at[pl.ds(pl.multiple_of(first, 16), count), column : column + columns],
                    )
                )
                part = columns // 2
                start = column + (part if d == 3 else 0)
                self.passed[d].append(move(block(source, first, count, start, part), to, self.far))
        for d, source in ((1, behind), (3, ahead), (2, across)):
            self.spreads[d] = []
            sem = self.spread_sem[d]
            for axis, first, count, column, columns in blocks:
                first = first + (x if axis == "x" else z % 4) * count
                whole = block(source, first, count, column, columns)
                if axis == "x":
                    self.spreads[d] += [move(whole, device((x + e) % 4, y, z, c), sem) for e in (2, 1, 3)]
                else:
                    part = columns // 2
                    self.spreads[d] += [
                        move(block(source, first, count, column, part), device(x, y, (z + 2) % NZ, c), sem),
                        move(block(source, first, count, column + part, part), device(x, y, (z + NZ - 2) % NZ, c), sem),
                        move(whole, device(x, y, (z + 1) % NZ, c), sem),
                        move(whole, device(x, y, (z + NZ - 1) % NZ, c), sem),
                    ]
            self.late[d] = move(block(source, direct, ROWS - direct), other, self.core)

    def received(self, rows, sem):
        await_received(self.wall.at[:rows], sem, self.other)

    def fetch(self):
        start_all(self.fetched[1] + self.fetched[3])

    def start(self):
        start_all(self.first)
        self.to_core.start()
        self.own.start()

    def pass_on(self):
        for d in (1, 3):
            self.received(self.block_rows, self.near[d])
            start_all(self.passed[d])

    def spread(self):
        start_all(self.spreads[1] + self.spreads[3])

    def across(self):
        self.received(self.block_rows, self.far)
        start_all(self.spreads[2])

    def collect(self):
        for d, late in self.late.items():
            self.received(3 * self.block_rows, self.spread_sem[d])
            late.start()

    def forward(self):
        for i, copy in enumerate(self.first):
            copy.wait_recv()
            self.forwards[i].start()
            self.cores[i].start()

    def finish(self):
        for forward, half in zip(self.forwards, self.halves):
            forward.wait_recv()
            half.start()

    def arrived(self):
        self.own.wait()
        self.received(4 * ROWS, self.core)

    def sent(self):
        await_sent(self.wall.at[: self.rows_sent], self.send, self.other)


class Ring:
    def __init__(self, own, cots, view, half, me, towards, other, new):
        ahead, behind, across = (me + 1) % 4, (me + 3) % 4, (me + 2) % 4
        self.cots, self.other = cots, other
        self.send = send = new()
        self.core = core = new()
        self.first = [
            remote(own, view(me), send, new(), towards(ahead)),
            remote(own, view(me), send, new(), towards(behind)),
            remote(own, view(me), send, core, other),
        ]
        self.behind = [
            remote(half(behind, 0), half(behind, 0), send, new(), towards(ahead)),
            remote(view(behind), view(behind), send, core, other),
        ]
        self.ahead = [
            remote(half(ahead, 1), half(ahead, 1), send, new(), towards(behind)),
            remote(view(ahead), view(ahead), send, core, other),
        ]
        self.across = [remote(half(across, h), half(across, h), send, core, other) for h in range(2)]

    def start(self):
        start_all(self.first)

    def forward(self):
        self.first[0].wait_recv()
        start_all(self.behind)
        self.first[1].wait_recv()
        start_all(self.ahead)

    def finish(self):
        self.behind[0].wait_recv()
        self.across[0].start()
        self.ahead[0].wait_recv()
        self.across[1].start()

    def arrived(self):
        await_received(self.cots.at[: 4 * ROWS], self.core, self.other)

    def sent(self):
        await_sent(self.cots.at[: 7 * ROWS], self.send, self.other)


class Swap:
    def __init__(self, held, landed, at, order, mask, send, new):
        x, y, z, c = at
        self.held, self.landed, self.order, self.mask = held, landed, order, mask
        self.copies = []
        for step, bit in enumerate(order):
            size = 1 << bit
            to = z + size - 2 * size * (z // size % 2)
            self.copies.append(
                remote(held.at[step], landed.at[step], send, new(), device(x, y, to, c))
            )

    def start(self):
        self.copies[0].start()

    def turn(self, step):
        self.copies[step].wait_recv()
        bit = jnp.full((SPILL, WIDTH), lax.shift_right_logical(self.mask[0, 0], self.order[step]) & 1, jnp.int32)
        chosen = jnp.where(bit == 1, self.landed[step].astype(F32), self.held[step].astype(F32))
        self.held[step + 1] = chosen.astype(BF16)
        if step < 2:
            self.copies[step + 1].start()


def layer_kernel(
    mask_hbm, lengths_hbm, actions_hbm, gain_hbm, w_in_ref, w_out_ref, cot_hbm,
    output, grad_input, weight_grad,
    mask_ref, lengths_ref,
    actions, gain, cot, wall, cots, cot_t, normed, normed_in, inverse_in,
    active, slopes, weights, score_slopes, attended, normed_out, inverse_out, mixed,
    far_normed, far_active, grad_att, grad_mix, grad_hidden,
    held, landed, all_mixed, total, sums, ybuf, part, zbuf, final, wide,
    sems, vouch,
):
    dp = lax.axis_index("dp")
    fsdp = lax.axis_index("fsdp")
    x, y, z, c = dp // NZ, fsdp // 2, dp % NZ, fsdp % 2
    me = 2 * x + c
    at = (x, y, z, c)
    other = device(x, y, z, 1 - c)
    group = [(2 * x + c + d) % 8 for d in range(1, 8)]
    in_group = [device(i // 2, y, z, i % 2) for i in group]
    in_y = [device(x, (y + d) % 4, z, c) for d in range(1, 4)]
    in_z = [device(x, y, (z + d) % NZ, c) for d in range(1, NZ)]
    ends = [device(y, i // 2, z, i % 2) for i in range(8)]
    near = [device((x + d) % 4, y, z, c) for d in (1, 3)] + [device(x, (y + d) % 4, z, c) for d in (1, 3)]
    near += [device(x, y, (z + d) % NZ, c) for d in (1, NZ - 1)] + [other]

    def vouch_for(step, targets):
        for target in targets:
            pl.semaphore_signal(vouch.at[step], inc=1, device_id=target, device_id_type=MESH)

    apart = [jnp.logical_or(x != y, i != me) for i in range(8)]

    used = [0]

    def new():
        used[0] += 1
        return sems.at[used[0] - 1]

    loads = [
        pltpu.make_async_copy(actions_hbm.at[0], actions, new()),
        pltpu.make_async_copy(cot_hbm.at[0], cot, new()),
        pltpu.make_async_copy(gain_hbm, gain, new()),
        pltpu.make_async_copy(mask_hbm, mask_ref, new()),
        pltpu.make_async_copy(lengths_hbm, lengths_ref, new()),
    ]
    barrier = pltpu.get_barrier_semaphore()
    for target in near:
        pl.semaphore_signal(barrier, inc=1, device_id=target, device_id_type=MESH)
    start_all(loads)

    sections = {
        t: Section(
            w_out_ref if t == OUT else w_in_ref.at[:, t * WIDTH : (t + 1) * WIDTH],
            wall, t, at, new,
        )
        for t in range(5)
    }
    column = lambda i: pl.ds(pl.multiple_of((2 * i + c) * ROWS, ROWS), ROWS)
    cring = Ring(
        cot_t, cots,
        lambda i: cots.at[:, column(i)],
        lambda i, h: cots.at[h * 512 : h * 512 + 512, column(i)],
        x, lambda i: device(i, y, z, c), other, new,
    )
    cown = pltpu.make_async_copy(cot_t, cots.at[:, column(x)], new())
    orders = [(2, 1, 0), (0, 1, 2), (2, 1, 0), (1, 2, 0)]
    swap_send = new()
    swaps = [Swap(held.at[i], landed.at[i], at, orders[i], mask_ref, swap_send, new) for i in range(4)]

    pl.semaphore_wait(barrier, len(near))
    sections[KEYS].fetch()
    for copy in loads:
        copy.wait()
    held[0, 0] = actions[FIRST : FIRST + 16]
    held[1, 0] = actions[FIRST + 16 : LAST]
    held[2, 0] = actions[LAST:]
    held[3, 0] = cot[LAST:]
    swaps[1].start()
    sections[QUERIES].fetch()
    sections[GATES].fetch()
    cot_t[...] = cot[...].astype(F32).T.astype(BF16)
    cring.start()
    cown.start()
    sections[KEYS].start()
    sections[QUERIES].start()
    vouch_for(0, near)

    for r in range(0, ROWS, CHUNK):
        n, inverse = normalize(actions[r : r + CHUNK].astype(F32))
        normed_in[r : r + CHUNK] = n
        inverse_in[r : r + CHUNK] = inverse
        normed[r : r + CHUNK] = (n * gain[...]).astype(BF16)

    row = lax.broadcasted_iota(jnp.int32, (ROWS, ROWS), 0)
    col = lax.broadcasted_iota(jnp.int32, (ROWS, ROWS), 1)
    begin = jnp.zeros((ROWS, ROWS), jnp.int32)
    end = jnp.zeros((), jnp.int32)
    for k in range(7):
        end = end + lengths_ref[0, 0, k]
        begin = begin + jnp.where(row >= end, lengths_ref[0, 0, k], 0)
    begin = jnp.where(row >= FIRST, FIRST, begin)
    begin = jnp.where(row >= LAST, LAST, begin)
    visible = (col >= begin) & (col <= row)

    def project(t, count=ROWS):
        for l in range(0, WIDTH, LANES):
            hidden = dot(normed[:count], wall[t, :, l : l + LANES])
            value, slope = silu_parts(hidden)
            active[t, :, l : l + LANES] = value[:ROWS].astype(BF16)
            slopes[t, :, l : l + LANES] = slope[:ROWS]
            if count > ROWS:
                far_active[t, :MOST, l : l + LANES] = value[ROWS:].astype(BF16)

    def small(t, rows, first, count):
        for l in range(0, WIDTH, LANES):
            hidden = dot(rows, wall[t, :, l : l + LANES])
            far_active[t, first : first + count, l : l + LANES] = silu_parts(hidden)[0].astype(BF16)

    def head(h):
        return slice(h * HEAD_DIM, (h + 1) * HEAD_DIM)

    pl.semaphore_wait(vouch.at[0], len(near))
    vouch_for(1, [device(x, y, (z + d) % NZ, c) for d in (2, NZ - 2)] + [other])
    pl.semaphore_wait(vouch.at[1], 3)
    swaps[0].start()
    vouch_for(2, [device(x, y, (z + d) % NZ, c) for d in (4, NZ - 4)] + in_y)
    swaps[1].turn(0)
    sections[KEYS].pass_on()
    sections[VALUES].start()
    sections[KEYS].spread()
    sections[QUERIES].pass_on()
    sections[QUERIES].spread()
    sections[GATES].pass_on()
    sections[GATES].start()
    swaps[0].turn(0)
    swaps[1].turn(1)
    sections[KEYS].across()
    sections[QUERIES].across()
    sections[GATES].spread()
    sections[GATES].across()
    cring.forward()
    sections[VALUES].forward()
    swaps[0].turn(1)
    sections[KEYS].collect()
    sections[GATES].forward()
    sections[OUT].start()
    sections[QUERIES].collect()
    swaps[2].start()
    swaps[3].start()
    swaps[0].turn(2)
    swaps[1].turn(2)
    far_inputs = jnp.concatenate([held[0, 3], held[1, 3]], axis=0).astype(F32)
    normed[ROWS:] = (normalize(far_inputs)[0] * gain[...]).astype(BF16)
    sections[KEYS].arrived()
    project(KEYS, ROWS + MOST)
    sections[VALUES].finish()
    sections[QUERIES].arrived()
    project(QUERIES)
    sections[GATES].collect()
    sections[GATES].finish()

    far_slopes, far_weights = [], []
    for h in range(HEADS):
        q, k = active[QUERIES, :, head(h)], active[KEYS, :, head(h)]
        value, slope = silu_parts(dot_nt(q, k) * SCALE)
        weights[h] = (jnp.where(visible, value, 0.0) / MOST).astype(BF16)
        score_slopes[h] = jnp.where(visible, slope, 0.0) * BACK
        value, slope = silu_parts(dot_nt(q[LAST:], far_active[KEYS, :MOST, head(h)]) * SCALE)
        far_slopes.append(slope * BACK)
        far_weights.append((value / MOST).astype(BF16))
    sections[VALUES].arrived()
    project(VALUES, ROWS + MOST)
    for h in range(HEADS):
        local_part = dot(weights[h], active[VALUES, :, head(h)])
        far_part = dot(far_weights[h], far_active[VALUES, :MOST, head(h)])
        attended[:LAST, head(h)] = local_part[:LAST]
        attended[LAST:, head(h)] = local_part[LAST:] + far_part

    sections[GATES].arrived()
    project(GATES)
    for r in range(0, ROWS, CHUNK):
        n, inverse = normalize(attended[r : r + CHUNK])
        normed_out[r : r + CHUNK] = n
        inverse_out[r : r + CHUNK] = inverse
        mix = (n * active[GATES, r : r + CHUNK].astype(F32)).astype(BF16)
        for h in range(HEADS):
            mixed[h, r : r + CHUNK] = mix[:, head(h)]
    pl.semaphore_wait(vouch.at[2], 5)
    own_rows = pl.ds(pl.multiple_of(me * ROWS, ROWS), ROWS)
    msend, mrecv, ysend, yrecv, zsend, zrecv, asend, arecv = [new() for _ in range(8)]
    spread = [remote(mixed.at[group[d]], all_mixed.at[own_rows], msend, mrecv, in_group[d]) for d in range(7)]
    start_all(spread)
    all_mixed[own_rows] = mixed[me]
    cring.finish()
    sections[OUT].forward()
    swaps[2].turn(0)
    swaps[3].turn(0)

    await_received(all_mixed.at[: 7 * ROWS], mrecv, other)
    cown.wait()
    cring.arrived()
    for d in (2, 1, 3, 0):
        quarter = pl.ds(pl.multiple_of((y + d) % 4 * 256, 256), 256)
        product = dot(cots[quarter], all_mixed[...])
        if d:
            sums[quarter] = product.astype(BF16)
            copy = remote(sums.at[quarter], ybuf.at[d - 1], ysend, yrecv, in_y[d - 1])
            copy.start()
        else:
            total[...] = product

    swaps[2].turn(1)
    swaps[3].turn(1)
    sections[OUT].finish()
    sections[OUT].arrived()
    for l in range(0, WIDTH, LANES):
        grad_mix[:, l : l + LANES] = dot_nt(cot[...], wall[OUT, l : l + LANES])

    for r in range(0, ROWS, CHUNK):
        span = slice(r, r + CHUNK)
        grad = grad_mix[span]
        n = normed_out[span]
        grad_hidden[GATES, span] = (grad * n * slopes[GATES, span]).astype(BF16)
        grad_att[span] = norm_backward(
            grad * active[GATES, span].astype(F32), n, inverse_out[span]
        ).astype(BF16)

    mixed_rows = jnp.concatenate([mixed[h] for h in range(HEADS)], axis=1)
    for l in range(0, WIDTH, LANES):
        output[0, :, l : l + LANES] = (
            dot(mixed_rows, wall[OUT, :, l : l + LANES]) + actions[:, l : l + LANES].astype(F32)
        ).astype(BF16)
    await_received(ybuf, yrecv, other)
    part[...] = (
        total[...] + ybuf[0].astype(F32) + ybuf[1].astype(F32) + ybuf[2].astype(F32)
    ).astype(BF16)
    zcopies = [
        remote(part.at[pl.ds(pl.multiple_of((z + d + 1) % NZ * 16, 16), 16)], zbuf.at[d], zsend, zrecv, in_z[d])
        for d in range(NZ - 1)
    ]
    for d in (7, 6, 8, 5, 9, 4, 10, 3, 11, 2, 12, 1, 13, 0, 14):
        zcopies[d].start()

    swaps[2].turn(2)
    swaps[3].turn(2)
    spill_inputs = held[2, 3].astype(F32)
    far_normed[...] = (normalize(spill_inputs)[0] * gain[...]).astype(BF16)
    for t in (GATES, VALUES, QUERIES, KEYS):
        small(t, far_normed[...], MOST, SPILL)
    rows16 = lax.broadcasted_iota(jnp.int32, (SPILL, SPILL), 0)
    cols16 = lax.broadcasted_iota(jnp.int32, (SPILL, SPILL), 1)
    causal = cols16 <= rows16
    near_weights, near_slopes, near_attended = [], [], []
    for h in range(HEADS):
        q = far_active[QUERIES, MOST:, head(h)]
        value, slope = silu_parts(dot_nt(q, active[KEYS, FIRST:LAST, head(h)]) * SCALE)
        weight = (value / MOST).astype(BF16)
        near_weights.append(weight)
        near_slopes.append(slope * BACK)
        value, _ = silu_parts(dot_nt(q, far_active[KEYS, MOST:, head(h)]) * SCALE)
        weight2 = (jnp.where(causal, value, 0.0) / MOST).astype(BF16)
        near_attended.append(
            dot(weight, active[VALUES, FIRST:LAST, head(h)]) + dot(weight2, far_active[VALUES, MOST:, head(h)])
        )
    near_grad = dot_nt(held[3, 3], wall[OUT])
    near_normed, near_inverse = normalize(jnp.concatenate(near_attended, axis=1))
    near_att = norm_backward(
        near_grad * far_active[GATES, MOST:].astype(F32), near_normed, near_inverse
    ).astype(BF16)

    for h in range(HEADS):
        q, k, v = active[QUERIES, :, head(h)], active[KEYS, :, head(h)], active[VALUES, :, head(h)]
        g = grad_att[:, head(h)]
        grad_s = (dot_nt(g, v) * score_slopes[h]).astype(BF16)
        far_s = (dot_nt(g[LAST:], far_active[VALUES, :MOST, head(h)]) * far_slopes[h]).astype(BF16)
        near_g = near_att[:, head(h)]
        near_s = (dot_nt(near_g, v[FIRST:LAST]) * near_slopes[h]).astype(BF16)
        grad_q = dot(grad_s, k)
        far_q = dot(far_s, far_active[KEYS, :MOST, head(h)])
        grad_k = dot_tn(grad_s, q)
        near_k = dot_tn(near_s, far_active[QUERIES, MOST:, head(h)])
        grad_v = dot_tn(weights[h], g)
        near_v = dot_tn(near_weights[h], near_g)
        slope = slopes[QUERIES, :, head(h)]
        grad_hidden[QUERIES, :LAST, head(h)] = (grad_q[:LAST] * slope[:LAST]).astype(BF16)
        grad_hidden[QUERIES, LAST:, head(h)] = ((grad_q[LAST:] + far_q) * slope[LAST:]).astype(BF16)
        for t, grad, extra in ((KEYS, grad_k, near_k), (VALUES, grad_v, near_v)):
            slope = slopes[t, :, head(h)]
            grad_hidden[t, :FIRST, head(h)] = (grad[:FIRST] * slope[:FIRST]).astype(BF16)
            grad_hidden[t, FIRST:LAST, head(h)] = ((grad[FIRST:LAST] + extra) * slope[FIRST:LAST]).astype(BF16)
            grad_hidden[t, LAST:, head(h)] = (grad[LAST:] * slope[LAST:]).astype(BF16)

    await_received(zbuf, zrecv, other)
    summed = part[pl.ds(pl.multiple_of(z * 16, 16), 16)].astype(F32)
    for d in range(NZ - 1):
        summed = summed + zbuf[d].astype(F32)
    final[...] = summed * (1.0 / 256.0)
    for i in range(8):
        copy = remote(final, wide.at[me], asend, arecv, ends[i])

        @pl.when(apart[i])
        def _():
            copy.start()

    @pl.when(x == y)
    def _():
        wide[me] = final[...]


    for l in range(0, WIDTH, LANES):
        grad_mix[:, l : l + LANES] = (
            dot_nt(grad_hidden[0], wall[0, l : l + LANES])
            + dot_nt(grad_hidden[1], wall[1, l : l + LANES])
            + dot_nt(grad_hidden[2], wall[2, l : l + LANES])
            + dot_nt(grad_hidden[3], wall[3, l : l + LANES])
        ) * gain[:, l : l + LANES]
    for r in range(0, ROWS, CHUNK):
        span = slice(r, r + CHUNK)
        grad_input[0, span] = (
            cot[span].astype(F32) + norm_backward(grad_mix[span], normed_in[span], inverse_in[span])
        ).astype(BF16)

    for section in sections.values():
        section.sent()
    cring.sent()
    await_sent(wall.at[OUT, : 12 * SPILL], swap_send, other)
    await_sent(all_mixed.at[: 7 * ROWS], msend, other)
    await_sent(ybuf, ysend, other)
    await_sent(zbuf, zsend, other)
    @pl.when(x == y)
    def _():
        await_received(wide.at[:7], arecv, other)

    @pl.when(x != y)
    def _():
        await_received(wide, arecv, other)

    for i in range(8):
        weight_grad[:, i * 128 : (i + 1) * 128] = wide[i]

    @pl.when(x == y)
    def _():
        await_sent(wide.at[:7], asend, other)

    @pl.when(x != y)
    def _():
        await_sent(wide, asend, other)


def publish_kernel(*refs):
    copies = [pltpu.make_async_copy(refs[i], refs[3 + i], refs[6].at[i]) for i in range(3)]
    start_all(copies)
    for copy in copies:
        copy.wait()


def per_device(actions, lengths, partner_mask, norm_gain, w_in, w_out, cotangent):
    hbm = pl.BlockSpec(memory_space=pltpu.HBM)
    vmem = pl.BlockSpec(memory_space=pltpu.VMEM)
    dma = pltpu.SemaphoreType.DMA
    block = (ROWS, WIDTH)
    shapes = (
        jax.ShapeDtypeStruct((1, ROWS, WIDTH), BF16),
        jax.ShapeDtypeStruct((1, ROWS, WIDTH), BF16),
        jax.ShapeDtypeStruct((16, WIDTH), F32),
    )
    results = pl.pallas_call(
        layer_kernel,
        out_shape=tuple(pltpu.VMEM(shape.shape, shape.dtype) for shape in shapes),
        in_specs=[hbm] * 7,
        out_specs=(vmem, vmem, vmem),
        scratch_shapes=[
            pltpu.SMEM((1, 1), jnp.int32),
            pltpu.SMEM((1, 1, 7), jnp.int32),

            pltpu.VMEM(block, BF16),
            pltpu.VMEM((1, WIDTH), F32),
            pltpu.VMEM(block, BF16),
            pltpu.VMEM((5, WIDTH, WIDTH), BF16),
            pltpu.VMEM((WIDTH, WIDTH), BF16),
            pltpu.VMEM((WIDTH, ROWS), BF16),
            pltpu.VMEM((ROWS + MOST, WIDTH), BF16),
            pltpu.VMEM(block, F32),
            pltpu.VMEM((ROWS, 1), F32),
            pltpu.VMEM((4, ROWS, WIDTH), BF16),
            pltpu.VMEM((4, ROWS, WIDTH), F32),
            pltpu.VMEM((HEADS, ROWS, ROWS), BF16),
            pltpu.VMEM((HEADS, ROWS, ROWS), F32),
            pltpu.VMEM(block, F32),
            pltpu.VMEM(block, F32),
            pltpu.VMEM((ROWS, 1), F32),
            pltpu.VMEM((HEADS, ROWS, HEAD_DIM), BF16),
            pltpu.VMEM((SPILL, WIDTH), BF16),
            pltpu.VMEM((4, MOST + SPILL, WIDTH), BF16),
            pltpu.VMEM(block, BF16),
            pltpu.VMEM(block, F32),
            pltpu.VMEM((4, ROWS, WIDTH), BF16),
            pltpu.VMEM((4, 4, SPILL, WIDTH), BF16),
            pltpu.VMEM((4, 3, SPILL, WIDTH), BF16),
            pltpu.VMEM((WIDTH, 128), BF16),
            pltpu.VMEM((256, 128), F32),
            pltpu.VMEM((WIDTH, 128), BF16),
            pltpu.VMEM((3, 256, 128), BF16),
            pltpu.VMEM((256, 128), BF16),
            pltpu.VMEM((NZ - 1, 16, 128), BF16),
            pltpu.VMEM((16, 128), F32),
            pltpu.VMEM((8, 16, 128), F32),
            dma((SEMAPHORES,)),
            pltpu.SemaphoreType.REGULAR((3,)),
        ],
        compiler_params=pltpu.CompilerParams(
            collective_id=0, has_side_effects=True, vmem_limit_bytes=56 * 1024 * 1024
        ),
        name="layer",
    )(partner_mask, lengths, actions, norm_gain.reshape(1, WIDTH), w_in, w_out, cotangent)
    return pl.pallas_call(
        publish_kernel,
        out_shape=shapes,
        in_specs=[vmem, vmem, vmem],
        out_specs=(hbm, hbm, hbm),
        scratch_shapes=[dma((3,))],
        compiler_params=pltpu.CompilerParams(vmem_limit_bytes=16 * 1024 * 1024),
        name="publish",
    )(*results)


def solution(mesh):
    placed = (
        P("fsdp", "dp", None),
        P("fsdp", "dp", None),
        P("fsdp", "dp"),
        P(),
        P("fsdp", None),
        P("fsdp", None),
        P("fsdp", "dp", None),
    )
    return jax.shard_map(
        per_device,
        mesh=mesh,
        in_specs=placed,
        out_specs=(P("fsdp", "dp", None), P("fsdp", "dp", None), P("dp", None)),
        check_vma=False,
    )
```
